128 devices in a mesh: tok: 16 (over y, z), exp: 8 (over x, core).
Axes of the slice: x: 4, y: 4, z: 4, core: 2. Of those that a mesh axis runs over, the one named last changes fastest.
Arguments:
- activations: bfloat16 [16384, 6144], P(('tok', 'exp')), may hold values from -6 to 6
- expert_ids: int32 [16384, 2], P(('tok', 'exp')), may hold values from 0 to 7, all different within a row; in each aligned block of 128 rows (0 to 127, 128 to 255, ...) at most 48 rows name the same one
- out_grads: bfloat16 [16384, 2, 16384], P(('tok', 'exp')), may hold values from -6 to 6
- sketch_matrix: bfloat16 [8, 16384, 128], P('exp'), may hold values from -0.046875 to 0.046875
Outputs:
- projector: float32 [8, 6144, 128], P('exp', 'tok')
The draws below stay inside these ranges and needn't reach their ends.
Inputs may be any that keep to these rules, and one draw needn't show every extreme that they name: `expert_ids`: each token names 2 different experts. In the tokens of one device (aligned blocks of 128 rows) no expert is named by more than 48 tokens, a bound that some block reaches.
All inputs are finite; a program needn't handle non-finite values.
Results may differ from the reference program's by a relative error of at most 0.034.
Values may be sent and summed in bfloat16 or wider, within the bound.
A program may use at most 128 MiB of HBM per device.

```python
import math
import jax
import jax.numpy as jnp
import numpy as np
from jax import lax

D = 6144
FF = 16384
TOP = 2
RANK = 128
TOK_DEV = 128
EXPERTS = 8
CAP = 48
TOKENS = 16384
DEVICES = 128


def steps_of(rng, shape, shards, smallest, top_value):
    def one(axis_at, blocks):
        draws = jax.random.uniform(jax.random.fold_in(jax.random.fold_in(rng, 6), axis_at), (blocks,), jnp.float32, smallest / len(shards), top_value / len(shards))
        return jnp.repeat(jnp.exp(draws), shape[axis_at] // blocks).reshape((-1,) + (1,) * (len(shape) - axis_at - 1))

    loudness = one(*shards[0])
    for cut in shards[1:]:
        loudness = loudness * one(*cut)
    return loudness


def shared_out(rng, own, number, rows, amount, top, bound, lean):
    ranking = jax.random.permutation(rng, amount)
    crowded, ordinary = load_shares(amount, rows * top, bound, lean, True), load_shares(amount, rows * top, bound, lean, False)
    places = jnp.arange(amount)

    def named(sizes, rotation):
        used = int((sizes > 0).sum())
        fixed = max(1, used // 4)
        shifted = fixed + (places - fixed + rotation * (used - fixed)) % max(1, amount - fixed)
        return jnp.zeros((amount,), jnp.int32).at[ranking[jnp.where(places < fixed, places, shifted)]].set(jnp.asarray(sizes, jnp.int32))

    sizes = jnp.where(number % 4 == 0, named(crowded, number // 4), named(ordinary, number - number // 4 - 1))
    mixed = jax.random.permutation(jax.random.fold_in(own, 3), amount)
    source_of, taker = mixed[0:amount // 2 * 2:2], mixed[1:amount // 2 * 2:2]
    margin = jnp.minimum(sizes[source_of] - 1, bound - sizes[taker]) // 2
    margin = jnp.where((source_of == ranking[0]) | (taker == ranking[0]) | (sizes[taker] == 0), 0, jnp.maximum(margin, 0))
    shifted = jax.random.randint(jax.random.fold_in(own, 4), (amount // 2,), 0, 1 << 20) % (margin + 1)
    sizes = sizes.at[source_of].add(-shifted).at[taker].add(shifted)
    members = jnp.searchsorted(jnp.cumsum(sizes), jnp.arange(rows * top), side="right").astype(jnp.int32)
    table = members.reshape(top, rows).T
    table = table[jax.random.permutation(jax.random.fold_in(own, 1), rows)]
    rotation = jax.random.randint(jax.random.fold_in(own, 2), (rows, 1), 0, top)
    return jnp.take_along_axis(table, (jnp.arange(top)[None, :] + rotation) % top, axis=1)


def load_shares(amount, total, most, lean, full):
    loads = [(1 << 20) // math.isqrt(grade ** lean) + 1 for grade in range(1, amount + 1)]
    largest = most if full else min(most, max(-(-total // amount), total * loads[0] // sum(loads)))
    least = 1 if total - largest >= amount - 1 else 0
    counts, surplus = [largest] + [least] * (amount - 1), total - largest - least * (amount - 1)
    while surplus > 0:
        free = [i for i in range(1, amount) if counts[i] < largest] or [i for i in range(1, amount) if counts[i] < most]
        whole, remaining = sum([loads[i] for i in free]), surplus
        for i in free:
            extra = min(most - counts[i], max(1, remaining * loads[i] // whole), surplus)
            counts[i] = counts[i] + extra
            surplus = surplus - extra
    return np.array(counts)


def centred(rng, shape, scale, most, cuts=(), kind=jnp.bfloat16):
    values = scale * jax.random.normal(rng, shape, jnp.float32)
    if cuts:
        values = values * steps_of(rng, shape, cuts, -0.22, 0.18)
    return jnp.clip(values, -most, most).astype(kind)


def setup_inputs(seed: int = 0) -> dict:
    arg_keys = jax.random.split(jax.random.key(seed), 5)
    activations = centred(arg_keys[0], (TOKENS, D), 1.0, 6.0, ((0, 128),))
    expert_ids_keys = jax.random.split(jax.random.fold_in(arg_keys[1], 1), TOKENS // TOK_DEV)
    expert_ids_turns = jax.random.permutation(jax.random.fold_in(arg_keys[1], 3), TOKENS // TOK_DEV)
    expert_ids = jax.vmap(lambda own, number: shared_out(jax.random.fold_in(arg_keys[1], 2), own, number, TOK_DEV, EXPERTS, TOP, CAP, 2))(expert_ids_keys, expert_ids_turns).reshape((TOKENS, TOP))
    out_grads = centred(arg_keys[2], (TOKENS, TOP, FF), 1.0, 6.0, ((0, 128),))
    sketch_matrix = centred(arg_keys[3], (EXPERTS, FF, RANK), FF ** -0.5, 0.046875, ((0, 8),))
    return {"activations": activations, "expert_ids": expert_ids, "out_grads": out_grads, "sketch_matrix": sketch_matrix}


HIGH = lax.Precision.HIGHEST

def orthonormal(block):
    gram = jnp.dot(block.T.astype(jnp.float32), block.astype(jnp.float32), precision=HIGH, preferred_element_type=jnp.float32)
    lower = jnp.linalg.cholesky(gram)
    return lax.linalg.triangular_solve(lower, block, left_side=False, lower=True, transpose_a=True)

def rounded(value):
    narrow = value.astype(jnp.bfloat16)
    narrow = lax.optimization_barrier(narrow)
    return narrow.astype(jnp.float32)

def reference(activations, expert_ids, out_grads, sketch_matrix):
    flat_ids = expert_ids.reshape(-1).astype(jnp.int32)
    flat_grads = out_grads.reshape(TOKENS * TOP, FF)

    def one_expert(expert):
        keyed = jnp.where(flat_ids == expert, 0, 1).astype(jnp.int32)
        order = jnp.argsort(keyed, stable=True)[:DEVICES * CAP].astype(jnp.int32)
        keep = (flat_ids[order] == expert)[:, None]
        rows_x = jnp.where(keep, activations[order // TOP], 0).astype(jnp.float32)
        rows_g = jnp.where(keep, flat_grads[order], 0).astype(jnp.float32)
        omega = sketch_matrix[expert].astype(jnp.float32)
        proj = rounded(jnp.dot(rows_g.astype(jnp.float32), omega.astype(jnp.float32), precision=HIGH, preferred_element_type=jnp.float32))
        sketch = jnp.dot(rows_x.T.astype(jnp.float32), proj.astype(jnp.float32), precision=HIGH, preferred_element_type=jnp.float32)
        basis = rounded(orthonormal(sketch))
        weights = rounded(jnp.dot(rows_x.astype(jnp.float32), basis.astype(jnp.float32), precision=HIGH, preferred_element_type=jnp.float32))
        power = jnp.dot(rows_g.T.astype(jnp.float32), weights.astype(jnp.float32), precision=HIGH, preferred_element_type=jnp.float32)
        right_basis = rounded(orthonormal(power))
        second = rounded(jnp.dot(rows_g.astype(jnp.float32), right_basis.astype(jnp.float32), precision=HIGH, preferred_element_type=jnp.float32))
        refined = jnp.dot(rows_x.T.astype(jnp.float32), second.astype(jnp.float32), precision=HIGH, preferred_element_type=jnp.float32)
        return orthonormal(refined) * jnp.float32(D ** 0.5)
    return lax.map(one_expert, jnp.arange(EXPERTS, dtype=jnp.int32))
```

```python
import functools

import jax
import jax.numpy as jnp
from jax import lax
from jax.experimental import pallas as pl
from jax.experimental.pallas import tpu as pltpu
from jax.sharding import PartitionSpec as P

MESH = pl.DeviceIdType.MESH
HIGH = lax.Precision.HIGHEST
F32 = jnp.float32
BF16 = jnp.bfloat16

N = 4
TOK = N * N
EXP = 2 * N
CAP = 48
ROWS = EXP * CAP
PIECE = 2 * CAP
RANK = 128
PANEL = 16


def dot(a, b):
    return jnp.dot(a, b, preferred_element_type=F32)


def dot_t(a, b, precision=None):
    return lax.dot_general(
        a, b, (((1,), (1,)), ((), ())), precision=precision, preferred_element_type=F32
    )


def sort_kernel(row_ids, col_ids, g_ref, x_ref, gs_ref, xs_ref, pick):
    pairs = row_ids.shape[1]
    toks = x_ref.shape[0]

    @pl.when(pl.program_id(0) == 0)
    def _():
        ids = row_ids[...]
        same = (col_ids[...] == ids) & (
            lax.broadcasted_iota(jnp.int32, (pairs, pairs), 0)
            < lax.broadcasted_iota(jnp.int32, (pairs, pairs), 1)
        )
        rank = jnp.sum(same.astype(F32), axis=0, keepdims=True).astype(jnp.int32)
        slot = ids * CAP + rank
        hot = lax.broadcasted_iota(jnp.int32, (ROWS, pairs), 0) == slot
        pick[...] = hot.astype(F32).astype(BF16)

    first = pick[:, :toks]
    second = pick[:, toks:]
    gs = dot(first, g_ref[:, 0, :]) + dot(second, g_ref[:, 1, :])
    gs_ref[...] = gs.astype(BF16)
    xs_ref[...] = dot(first + second, x_ref[...]).astype(BF16)


def sort_rows(expert_ids, out_grads, activations, steps=16):
    toks, top = expert_ids.shape
    hidden = out_grads.shape[2]
    width = activations.shape[1]
    ids = expert_ids.T.reshape(1, toks * top)
    hc, wc = hidden // steps, width // steps
    return pl.pallas_call(
        sort_kernel,
        grid=(steps,),
        out_shape=(
            jax.ShapeDtypeStruct((ROWS, hidden), BF16),
            jax.ShapeDtypeStruct((ROWS, width), BF16),
        ),
        in_specs=[
            pl.BlockSpec((1, toks * top), lambda i: (0, 0)),
            pl.BlockSpec((toks * top, 1), lambda i: (0, 0)),
            pl.BlockSpec((toks, top, hc), lambda i: (0, 0, i)),
            pl.BlockSpec((toks, wc), lambda i: (0, i)),
        ],
        out_specs=(
            pl.BlockSpec((ROWS, hc), lambda i: (0, i)),
            pl.BlockSpec((ROWS, wc), lambda i: (0, i)),
        ),
        scratch_shapes=[pltpu.VMEM((ROWS, toks * top), BF16)],
        compiler_params=pltpu.CompilerParams(vmem_limit_bytes=40 * 1024 * 1024),
        name="sort",
    )(ids, ids.reshape(toks * top, 1), out_grads, activations)


def bytes_wait(ref, sem):
    pltpu.make_async_copy(ref, ref, sem).wait()


def inverse_factor(c, cm, mm):
    cm[...] = c
    rows = lax.broadcasted_iota(jnp.int32, (RANK, RANK), 0)
    cols = lax.broadcasted_iota(jnp.int32, (RANK, RANK), 1)
    mm[...] = (rows == cols).astype(F32)
    prow = lax.broadcasted_iota(jnp.int32, (PANEL, RANK), 0)
    pcol = lax.broadcasted_iota(jnp.int32, (PANEL, RANK), 1)
    srow = lax.broadcasted_iota(jnp.int32, (PANEL, 1), 0)

    def panel(p, carry):
        base = pl.multiple_of(p * PANEL, PANEL)
        a = pltpu.roll(cm[pl.ds(base, PANEL), :], lax.rem(RANK - base, RANK), 1)
        m = mm[pl.ds(base, PANEL), :]
        for i in range(PANEL):
            ra = a[i : i + 1, :]
            rm = m[i : i + 1, :]
            r = lax.rsqrt(a[i : i + 1, i : i + 1])
            col = jnp.where(srow > i, a[:, i : i + 1] * (r * r), 0.0)
            a = jnp.where(prow == i, a * r, a - col * ra)
            m = jnp.where(prow == i, m * r, m - col * rm)
        mm[pl.ds(base, PANEL), :] = m
        a = pltpu.roll(a, base, 1)
        left = jnp.where(pcol >= base + PANEL, a, 0.0)
        both = jnp.concatenate([a, m], axis=1)
        change = lax.dot_general(
            left, both, (((0,), (0,)), ((), ())), precision=HIGH, preferred_element_type=F32
        )
        cm[...] -= change[:, :RANK]
        mm[...] -= change[:, RANK:]
        return carry

    lax.fori_loop(0, RANK // PANEL, panel, 0)
    return mm[...]


def body(
    scale,
    gs, xs, om,
    out,
    xr, gl, gr, wl, wr,
    nls, nrs, pxl, pxr, pxl2, pxr2,
    sp, rb, rb3, bt,
    ws, wgl, wgr,
    pwl, pwr, rl, rr, rbl, rbr,
    gm, gb, cm, mm,
    ssem, rsem, gsem, selfsem,
):
    tok = lax.axis_index("tok")
    ex = lax.axis_index("exp")
    y, z = lax.div(tok, N), lax.rem(tok, N)
    x, k = lax.div(ex, 2), lax.rem(ex, 2)
    half = gl.shape[1]
    width = xr.shape[1]
    wc = width // TOK
    hc = half // TOK

    def dev(a, b, c, core):
        return (b * N + c, a * 2 + core)

    def add(a, b, n):
        return lax.rem(a + b, n)

    def remote(src, dst, s, r, where):
        return pltpu.make_async_remote_copy(
            src_ref=src, dst_ref=dst, send_sem=s, recv_sem=r, device_id=where, device_id_type=MESH
        )

    def loop(lo, hi, fn):
        lax.fori_loop(lo, hi, lambda i, c: (fn(i), c)[1], 0)

    barrier = pltpu.get_barrier_semaphore()

    def greet(where):
        pl.semaphore_signal(barrier, inc=1, device_id=where, device_id_type=MESH)

    chip = x * TOK + tok

    def same_core(d):
        c = add(chip, d, N * TOK)
        greet((lax.rem(c, TOK), lax.div(c, TOK) * 2 + k))

    loop(1, N * TOK, same_core)

    def other_core(d):
        greet(dev(add(x, d, N), y, z, 1 - k))

    loop(0, N, other_core)

    def other_core_y(d):
        greet(dev(x, add(y, d, N), z, 1 - k))
        greet(dev(x, y, add(z, d, N), 1 - k))

    loop(1, N, other_core_y)
    pl.semaphore_wait(barrier, N * TOK - 1 + N + 2 * (N - 1))

    OM, GLS, GRS, XS, PX, BX, WG, PW, RBX, PX2, R3 = range(11)

    swap_l = x == y
    swap_r = x == z

    def om_left():
        return remote(om.at[pl.ds(0, half), :], wl, ssem.at[0], rsem.at[0], dev(y, x, z, k))

    def om_right():
        return remote(om.at[pl.ds(half, half), :], wr, ssem.at[1], rsem.at[1], dev(z, y, x, k))

    @pl.when(swap_l)
    def _():
        pltpu.make_async_copy(om.at[pl.ds(0, half), :], wl, rsem.at[0]).start()

    @pl.when(jnp.logical_not(swap_l))
    def _():
        om_left().start()

    @pl.when(swap_r)
    def _():
        pltpu.make_async_copy(om.at[pl.ds(half, half), :], wr, rsem.at[1]).start()

    @pl.when(jnp.logical_not(swap_r))
    def _():
        om_right().start()

    el, er = y * 2 + k, z * 2 + k

    def rows_of(e):
        return pl.ds(pl.multiple_of(e * CAP, CAP), CAP)

    def send_g(d):
        e = add(el, d, EXP)
        remote(
            gs.at[rows_of(e), pl.ds(0, half)], gl.at[rows_of(el), :], ssem.at[2], rsem.at[2],
            dev(x, lax.div(e, 2), z, lax.rem(e, 2)),
        ).start()
        e = add(er, d, EXP)
        remote(
            gs.at[rows_of(e), pl.ds(half, half)], gr.at[rows_of(er), :], ssem.at[3], rsem.at[3],
            dev(x, y, lax.div(e, 2), lax.rem(e, 2)),
        ).start()

    loop(1, EXP, send_g)
    pltpu.make_async_copy(
        gs.at[rows_of(el), pl.ds(0, half)], gl.at[rows_of(el), :], rsem.at[2]
    ).start()
    pltpu.make_async_copy(
        gs.at[rows_of(er), pl.ds(half, half)], gr.at[rows_of(er), :], rsem.at[3]
    ).start()

    def send_x(d):
        e = add(ex, d, EXP)
        remote(
            xs.at[rows_of(e), :], xr.at[rows_of(ex), :], ssem.at[4], rsem.at[4], (tok, e)
        ).start()

    loop(1, EXP, send_x)
    pltpu.make_async_copy(xs.at[rows_of(ex), :], xr.at[rows_of(ex), :], rsem.at[4]).start()

    def piece(i):
        return pl.ds(pl.multiple_of(i * PIECE, PIECE), PIECE)

    def to_x(left, right, dl, dr, phase):
        nls[phase] = left.astype(BF16)
        nrs[phase] = right.astype(BF16)
        sl, sr = ssem.at[5 + 2 * phase], ssem.at[6 + 2 * phase]
        rl_, rr_ = rsem.at[5 + 2 * phase], rsem.at[6 + 2 * phase]

        def go_l(d):
            b = add(y, d, N)
            remote(nls.at[phase, piece(b), :], dl.at[piece(x), :], sl, rl_, dev(y, b, z, k)).start()

        def go_r(d):
            c = add(z, d, N)
            remote(nrs.at[phase, piece(c), :], dr.at[piece(x), :], sr, rr_, dev(z, y, c, k)).start()

        loop(1, N, go_l)
        loop(1, N, go_r)
        own_l = selfsem.at[2 * phase]
        own_r = selfsem.at[2 * phase + 1]

        @pl.when(swap_l)
        def _():
            pltpu.make_async_copy(nls.at[phase, piece(y), :], dl.at[piece(x), :], rl_).start()

        @pl.when(jnp.logical_not(swap_l))
        def _():
            remote(
                nls.at[phase, piece(y), :], dl.at[piece(x), :], own_l, rl_, dev(y, y, z, k)
            ).start()

        @pl.when(swap_r)
        def _():
            pltpu.make_async_copy(nrs.at[phase, piece(z), :], dr.at[piece(x), :], rr_).start()

        @pl.when(jnp.logical_not(swap_r))
        def _():
            remote(
                nrs.at[phase, piece(z), :], dr.at[piece(x), :], own_r, rr_, dev(z, y, z, k)
            ).start()

        bytes_wait(dl, rl_)
        bytes_wait(dr, rr_)
        total = dl[...].astype(F32) + dr[...].astype(F32)
        three = nls.at[phase, pl.ds(0, 3 * PIECE), :]
        bytes_wait(three, sl)
        bytes_wait(nrs.at[phase, pl.ds(0, 3 * PIECE), :], sr)

        @pl.when(jnp.logical_not(swap_l))
        def _():
            bytes_wait(nls.at[phase, pl.ds(0, PIECE), :], own_l)

        @pl.when(jnp.logical_not(swap_r))
        def _():
            bytes_wait(nrs.at[phase, pl.ds(0, PIECE), :], own_r)

        return total

    def gram_all(s, phase):
        gm[phase] = dot_t(s, s, HIGH).astype(BF16)
        pltpu.make_async_copy(gm.at[phase], gb.at[phase, tok], gsem.at[2 * phase]).start()

        def go(d):
            t = add(tok, d, TOK)
            remote(
                gm.at[phase], gb.at[phase, tok], gsem.at[2 * phase + 1], gsem.at[2 * phase], (t, ex)
            ).start()

        loop(1, TOK, go)
        bytes_wait(gb.at[phase], gsem.at[2 * phase])
        c = lax.fori_loop(
            0, TOK, lambda i, c: c + gb[phase, i].astype(F32), jnp.zeros((RANK, RANK), F32)
        )
        bytes_wait(gb.at[phase, pl.ds(0, TOK - 1)], gsem.at[2 * phase + 1])
        return inverse_factor(c, cm, mm)

    def reduce_x(p, dst, s, r):
        pt = p.T.astype(BF16)

        def chunk(d):
            t = add(tok, d, TOK)
            cols = pl.ds(pl.multiple_of(t * wc, 128), wc)
            sp[t] = dot(pt, xr[:, cols]).astype(BF16)

            @pl.when(d < TOK)
            def _():
                remote(sp.at[t], dst.at[tok], s, r, (t, ex)).start()

        loop(1, TOK + 1, chunk)
        pltpu.make_async_copy(sp.at[tok], dst.at[tok], r).start()
        bytes_wait(dst, r)
        total = lax.fori_loop(
            0, TOK, lambda i, c: c + dst[i].astype(F32), jnp.zeros((RANK, wc), F32)
        )
        bytes_wait(sp.at[pl.ds(0, TOK - 1)], s)
        return total

    kc = 1024

    def g_dot(w_l, w_r):
        def step(j, acc):
            cols = pl.ds(pl.multiple_of(j * kc, kc), kc)
            a, b = acc
            return (
                a + dot(gl[:, cols], w_l[cols, :]),
                b + dot(gr[:, cols], w_r[cols, :]),
            )

        zero = jnp.zeros((ROWS, RANK), F32)
        return lax.fori_loop(0, half // kc, step, (zero, zero))

    bytes_wait(wl, rsem.at[0])
    bytes_wait(wr, rsem.at[1])
    bytes_wait(gl, rsem.at[2])
    bytes_wait(gr, rsem.at[3])
    left, right = g_dot(wl, wr)
    proj = to_x(left, right, pxl, pxr, 0).astype(BF16).astype(F32)
    bytes_wait(xr, rsem.at[4])

    s = reduce_x(proj, rb, ssem.at[9], rsem.at[9])
    inv = gram_all(s, 0)
    bt[tok] = jnp.dot(inv, s, precision=HIGH, preferred_element_type=F32).astype(BF16)

    def send_b(d):
        remote(
            bt.at[tok], bt.at[tok], ssem.at[10], rsem.at[10], (add(tok, d, TOK), ex)
        ).start()

    loop(1, TOK, send_b)
    bytes_wait(bt.at[pl.ds(0, TOK - 1)], rsem.at[10])

    def w_step(t, acc):
        cols = pl.ds(pl.multiple_of(t * wc, 128), wc)
        return acc + dot_t(xr[:, cols], bt[t])

    weights = lax.fori_loop(0, TOK, w_step, jnp.zeros((ROWS, RANK), F32))
    ws[...] = weights.astype(BF16)

    def go_w(d):
        a = add(x, d, N)
        remote(
            ws.at[piece(a), :], wgl.at[piece(y), :], ssem.at[11], rsem.at[11], dev(a, x, z, k)
        ).start()
        remote(
            ws.at[piece(a), :], wgr.at[piece(z), :], ssem.at[12], rsem.at[12], dev(a, y, x, k)
        ).start()

    loop(1, N, go_w)

    @pl.when(swap_l)
    def _():
        pltpu.make_async_copy(ws.at[piece(x), :], wgl.at[piece(y), :], rsem.at[11]).start()

    @pl.when(jnp.logical_not(swap_l))
    def _():
        remote(
            ws.at[piece(x), :], wgl.at[piece(y), :], selfsem.at[4], rsem.at[11], dev(x, x, z, k)
        ).start()

    @pl.when(swap_r)
    def _():
        pltpu.make_async_copy(ws.at[piece(x), :], wgr.at[piece(z), :], rsem.at[12]).start()

    @pl.when(jnp.logical_not(swap_r))
    def _():
        remote(
            ws.at[piece(x), :], wgr.at[piece(z), :], selfsem.at[5], rsem.at[12], dev(x, y, x, k)
        ).start()

    bytes_wait(wgl, rsem.at[11])
    bytes_wait(wgr, rsem.at[12])

    wlt = wgl[...].astype(F32).T.astype(BF16)
    wrt = wgr[...].astype(F32).T.astype(BF16)
    slot_l = x * N + z
    slot_r = x * N + y

    def power_chunk(d):
        t = add(tok, d, TOK)
        cols = pl.ds(pl.multiple_of(t * hc, 128), hc)
        pwl[t] = dot(wlt, gl[:, cols]).astype(BF16)
        pwr[t] = dot(wrt, gr[:, cols]).astype(BF16)

        @pl.when(d < TOK)
        def _():
            remote(
                pwl.at[t], rl.at[slot_l], ssem.at[13], rsem.at[13], (t, y * 2 + k)
            ).start()
            remote(
                pwr.at[t], rr.at[slot_r], ssem.at[14], rsem.at[14], (t, z * 2 + k)
            ).start()

    loop(1, TOK + 1, power_chunk)

    @pl.when(swap_l)
    def _():
        pltpu.make_async_copy(pwl.at[tok], rl.at[slot_l], rsem.at[13]).start()

    @pl.when(jnp.logical_not(swap_l))
    def _():
        remote(
            pwl.at[tok], rl.at[slot_l], selfsem.at[6], rsem.at[13], (tok, y * 2 + k)
        ).start()

    @pl.when(swap_r)
    def _():
        pltpu.make_async_copy(pwr.at[tok], rr.at[slot_r], rsem.at[14]).start()

    @pl.when(jnp.logical_not(swap_r))
    def _():
        remote(
            pwr.at[tok], rr.at[slot_r], selfsem.at[7], rsem.at[14], (tok, z * 2 + k)
        ).start()

    bytes_wait(rl, rsem.at[13])
    bytes_wait(rr, rsem.at[14])
    zero = jnp.zeros((RANK, hc), F32)
    sl = lax.fori_loop(0, TOK, lambda i, c: c + rl[i].astype(F32), zero)
    sr = lax.fori_loop(0, TOK, lambda i, c: c + rr[i].astype(F32), zero)
    s2 = jnp.concatenate([sl, sr], axis=1)
    inv = gram_all(s2, 1)
    right_basis = jnp.dot(inv, s2, precision=HIGH, preferred_element_type=F32).astype(BF16)

    bytes_wait(pwl.at[pl.ds(0, TOK - 1)], ssem.at[13])
    bytes_wait(pwr.at[pl.ds(0, TOK - 1)], ssem.at[14])

    @pl.when(jnp.logical_not(swap_l))
    def _():
        bytes_wait(pwl.at[0], selfsem.at[6])
        bytes_wait(ws.at[piece(0), :], selfsem.at[4])

    @pl.when(jnp.logical_not(swap_r))
    def _():
        bytes_wait(pwr.at[0], selfsem.at[7])
        bytes_wait(ws.at[piece(0), :], selfsem.at[5])

    pwl[0] = right_basis[:, :hc]
    pwr[0] = right_basis[:, hc:]

    def send_r(d):
        a = add(x, lax.div(d, N), N)
        c = add(z, lax.rem(d, N), N)
        remote(
            pwl.at[0], rbl.at[tok], ssem.at[15], rsem.at[15], dev(a, x, c, k)
        ).start()
        b = add(y, lax.rem(d, N), N)
        remote(
            pwr.at[0], rbr.at[tok], ssem.at[16], rsem.at[16], dev(a, b, x, k)
        ).start()

    loop(1, TOK, send_r)

    @pl.when(swap_l)
    def _():
        pltpu.make_async_copy(pwl.at[0], rbl.at[tok], rsem.at[15]).start()

    @pl.when(jnp.logical_not(swap_l))
    def _():
        remote(pwl.at[0], rbl.at[tok], selfsem.at[8], rsem.at[15], dev(x, x, z, k)).start()

    @pl.when(swap_r)
    def _():
        pltpu.make_async_copy(pwr.at[0], rbr.at[tok], rsem.at[16]).start()

    @pl.when(jnp.logical_not(swap_r))
    def _():
        remote(pwr.at[0], rbr.at[tok], selfsem.at[9], rsem.at[16], dev(x, y, x, k)).start()

    bytes_wait(rbl, rsem.at[15])
    bytes_wait(rbr, rsem.at[16])

    def s_step(t, acc):
        cols = pl.ds(pl.multiple_of(t * hc, 128), hc)
        a, b = acc
        return a + dot_t(gl[:, cols], rbl[t]), b + dot_t(gr[:, cols], rbr[t])

    zero = jnp.zeros((ROWS, RANK), F32)
    left, right = lax.fori_loop(0, TOK, s_step, (zero, zero))
    second = to_x(left, right, pxl2, pxr2, 1).astype(BF16).astype(F32)

    s3 = reduce_x(second, rb3, ssem.at[17], rsem.at[17])
    inv = gram_all(s3, 2)
    last = jnp.dot(inv, s3, precision=HIGH, preferred_element_type=F32)
    out[0] = last.T * scale

    @pl.when(jnp.logical_not(swap_l))
    def _():
        om_left().wait_send()
        bytes_wait(pwl.at[0], selfsem.at[8])

    @pl.when(jnp.logical_not(swap_r))
    def _():
        om_right().wait_send()
        bytes_wait(pwr.at[0], selfsem.at[9])

    part = pl.ds(0, ROWS - CAP)
    bytes_wait(gl.at[part, :], ssem.at[2])
    bytes_wait(gr.at[part, :], ssem.at[3])
    bytes_wait(xr.at[part, :], ssem.at[4])
    bytes_wait(bt.at[pl.ds(0, TOK - 1)], ssem.at[10])
    bytes_wait(ws.at[pl.ds(0, 3 * PIECE), :], ssem.at[11])
    bytes_wait(ws.at[pl.ds(0, 3 * PIECE), :], ssem.at[12])
    bytes_wait(rl.at[pl.ds(0, TOK - 1)], ssem.at[15])
    bytes_wait(rr.at[pl.ds(0, TOK - 1)], ssem.at[16])


def owners(gs, xs, om):
    hidden = gs.shape[1]
    width = xs.shape[1]
    half = hidden // 2
    wc, hc = width // TOK, half // TOK

    def vm(*shape, dtype=BF16):
        return pltpu.VMEM(shape, dtype)

    any_spec = pl.BlockSpec(memory_space=pl.ANY)
    return pl.pallas_call(
        functools.partial(body, float(width) ** 0.5),
        out_shape=jax.ShapeDtypeStruct((1, wc, RANK), F32),
        in_specs=[any_spec] * 3,
        out_specs=pl.BlockSpec(memory_space=pltpu.VMEM),
        scratch_shapes=[
            vm(ROWS, width), vm(ROWS, half), vm(ROWS, half), vm(half, RANK), vm(half, RANK),
            vm(2, ROWS, RANK), vm(2, ROWS, RANK),
            vm(ROWS, RANK), vm(ROWS, RANK), vm(ROWS, RANK), vm(ROWS, RANK),
            vm(TOK, RANK, wc), vm(TOK, RANK, wc), vm(TOK, RANK, wc), vm(TOK, RANK, wc),
            vm(ROWS, RANK), vm(ROWS, RANK), vm(ROWS, RANK),
            vm(TOK, RANK, hc), vm(TOK, RANK, hc), vm(TOK, RANK, hc), vm(TOK, RANK, hc),
            vm(TOK, RANK, hc), vm(TOK, RANK, hc),
            vm(3, RANK, RANK), vm(3, TOK, RANK, RANK),
            vm(RANK, RANK, dtype=F32), vm(RANK, RANK, dtype=F32),
            pltpu.SemaphoreType.DMA((18,)),
            pltpu.SemaphoreType.DMA((18,)),
            pltpu.SemaphoreType.DMA((6,)),
            pltpu.SemaphoreType.DMA((10,)),
        ],
        compiler_params=pltpu.CompilerParams(
            collective_id=0, has_side_effects=True, vmem_limit_bytes=58 * 1024 * 1024
        ),
        name="owners",
    )(gs, xs, om)


def shards(activations, expert_ids, out_grads, sketch_matrix):
    gs, xs = sort_rows(expert_ids, out_grads, activations)
    om = sketch_matrix.reshape(sketch_matrix.shape[1:])
    return owners(gs, xs, om)


def solution(mesh):
    return jax.shard_map(
        shards,
        mesh=mesh,
        in_specs=(
            P(("tok", "exp"), None),
            P(("tok", "exp"), None),
            P(("tok", "exp"), None, None),
            P("exp", None, None),
        ),
        out_specs=P("exp", "tok", None),
        check_vma=False,
    )
```

```python
import functools

import jax
import jax.numpy as jnp
from jax import lax
from jax.experimental import pallas as pl
from jax.experimental.pallas import tpu as pltpu
from jax.sharding import PartitionSpec as P

MESH = pl.DeviceIdType.MESH
HIGH = lax.Precision.HIGHEST
F32 = jnp.float32
BF16 = jnp.bfloat16

N = 4
TOK = N * N
EXP = 2 * N
CAP = 48
ROWS = EXP * CAP
PIECE = 2 * CAP
RANK = 128
PANEL = 16


def dot(a, b):
    return jnp.dot(a, b, preferred_element_type=F32)


def dot_t(a, b, precision=None):
    return lax.dot_general(
        a, b, (((1,), (1,)), ((), ())), precision=precision, preferred_element_type=F32
    )


def sort_kernel(row_ids, col_ids, g_ref, x_ref, gs_ref, xs_ref, pick):
    pairs = row_ids.shape[1]
    toks = x_ref.shape[0]

    @pl.when(pl.program_id(0) == 0)
    def _():
        ids = row_ids[...]
        same = (col_ids[...] == ids) & (
            lax.broadcasted_iota(jnp.int32, (pairs, pairs), 0)
            < lax.broadcasted_iota(jnp.int32, (pairs, pairs), 1)
        )
        rank = jnp.sum(same.astype(F32), axis=0, keepdims=True).astype(jnp.int32)
        slot = ids * CAP + rank
        hot = lax.broadcasted_iota(jnp.int32, (ROWS, pairs), 0) == slot
        pick[...] = hot.astype(F32).astype(BF16)

    first = pick[:, :toks]
    second = pick[:, toks:]
    gs = dot(first, g_ref[:, 0, :]) + dot(second, g_ref[:, 1, :])
    gs_ref[...] = gs.astype(BF16)
    xs_ref[...] = dot(first + second, x_ref[...]).astype(BF16)


def sort_rows(expert_ids, out_grads, activations, steps=16):
    toks, top = expert_ids.shape
    hidden = out_grads.shape[2]
    width = activations.shape[1]
    ids = expert_ids.T.reshape(1, toks * top)
    hc, wc = hidden // steps, width // steps
    return pl.pallas_call(
        sort_kernel,
        grid=(steps,),
        out_shape=(
            jax.ShapeDtypeStruct((ROWS, hidden), BF16),
            jax.ShapeDtypeStruct((ROWS, width), BF16),
        ),
        in_specs=[
            pl.BlockSpec((1, toks * top), lambda i: (0, 0)),
            pl.BlockSpec((toks * top, 1), lambda i: (0, 0)),
            pl.BlockSpec((toks, top, hc), lambda i: (0, 0, i)),
            pl.BlockSpec((toks, wc), lambda i: (0, i)),
        ],
        out_specs=(
            pl.BlockSpec((ROWS, hc), lambda i: (0, i)),
            pl.BlockSpec((ROWS, wc), lambda i: (0, i)),
        ),
        scratch_shapes=[pltpu.VMEM((ROWS, toks * top), BF16)],
        compiler_params=pltpu.CompilerParams(vmem_limit_bytes=40 * 1024 * 1024),
        name="sort",
    )(ids, ids.reshape(toks * top, 1), out_grads, activations)


def bytes_wait(ref, sem):
    pltpu.make_async_copy(ref, ref, sem).wait()


def inverse_factor(c, cm, mm):
    cm[...] = c
    rows = lax.broadcasted_iota(jnp.int32, (RANK, RANK), 0)
    cols = lax.broadcasted_iota(jnp.int32, (RANK, RANK), 1)
    mm[...] = (rows == cols).astype(F32)
    prow = lax.broadcasted_iota(jnp.int32, (PANEL, RANK), 0)
    pcol = lax.broadcasted_iota(jnp.int32, (PANEL, RANK), 1)
    srow = lax.broadcasted_iota(jnp.int32, (PANEL, 1), 0)

    def panel(p, carry):
        base = pl.multiple_of(p * PANEL, PANEL)
        a = pltpu.roll(cm[pl.ds(base, PANEL), :], lax.rem(RANK - base, RANK), 1)
        m = mm[pl.ds(base, PANEL), :]
        for i in range(PANEL):
            ra = a[i : i + 1, :]
            rm = m[i : i + 1, :]
            r = lax.rsqrt(a[i : i + 1, i : i + 1])
            col = jnp.where(srow > i, a[:, i : i + 1] * (r * r), 0.0)
            a = jnp.where(prow == i, a * r, a - col * ra)
            m = jnp.where(prow == i, m * r, m - col * rm)
        mm[pl.ds(base, PANEL), :] = m
        a = pltpu.roll(a, base, 1)
        left = jnp.where(pcol >= base + PANEL, a, 0.0)
        both = jnp.concatenate([a, m], axis=1)
        change = lax.dot_general(
            left, both, (((0,), (0,)), ((), ())), precision=HIGH, preferred_element_type=F32
        )
        cm[...] -= change[:, :RANK]
        mm[...] -= change[:, RANK:]
        return carry

    lax.fori_loop(0, RANK // PANEL, panel, 0)
    return mm[...]


def body(
    scale,
    gs, xs, om,
    out,
    xr, gl, gr, wl, wr,
    nls, nrs, pxl, pxr, pxl2, pxr2,
    sp, rb, rb3, bt,
    ws, wgl, wgr,
    pwl, pwr, rl, rr, rbl, rbr,
    gm, gb, cm, mm,
    ssem, rsem, gsem, selfsem,
):
    tok = lax.axis_index("tok")
    ex = lax.axis_index("exp")
    y, z = lax.div(tok, N), lax.rem(tok, N)
    x, k = lax.div(ex, 2), lax.rem(ex, 2)
    half = gl.shape[1]
    width = xr.shape[1]
    wc = width // TOK
    hc = half // TOK

    def dev(a, b, c, core):
        return (b * N + c, a * 2 + core)

    def add(a, b, n):
        return lax.rem(a + b, n)

    def remote(src, dst, s, r, where):
        return pltpu.make_async_remote_copy(
            src_ref=src, dst_ref=dst, send_sem=s, recv_sem=r, device_id=where, device_id_type=MESH
        )

    def loop(lo, hi, fn):
        lax.fori_loop(lo, hi, lambda i, c: (fn(i), c)[1], 0)

    barrier = pltpu.get_barrier_semaphore()

    def greet(where):
        pl.semaphore_signal(barrier, inc=1, device_id=where, device_id_type=MESH)

    chip = x * TOK + tok

    def same_core(d):
        c = add(chip, d, N * TOK)
        greet((lax.rem(c, TOK), lax.div(c, TOK) * 2 + k))

    loop(1, N * TOK, same_core)

    def other_core(d):
        greet(dev(add(x, d, N), y, z, 1 - k))

    loop(0, N, other_core)

    def other_core_y(d):
        greet(dev(x, add(y, d, N), z, 1 - k))
        greet(dev(x, y, add(z, d, N), 1 - k))

    loop(1, N, other_core_y)
    pl.semaphore_wait(barrier, N * TOK - 1 + N + 2 * (N - 1))

    OM, GLS, GRS, XS, PX, BX, WG, PW, RBX, PX2, R3 = range(11)

    shift_l = lax.rem(y - z + N, N)
    shift_r = lax.rem(y - z + N + 2, N)
    swap_l = shift_l == 0
    swap_r = shift_r == 0
    xl = add(x, shift_l, N)
    xd = add(x, shift_r, N)

    def left_y(at_x, to_x, c):
        return lax.rem(to_x - at_x + c + N, N)

    def right_z(at_x, to_x, b):
        return lax.rem(at_x + b + 2 - to_x + N, N)


    def om_left():
        return remote(om.at[pl.ds(0, half), :], wl, ssem.at[0], rsem.at[0], dev(add(x, N - shift_l, N), y, z, k))

    def om_right():
        return remote(om.at[pl.ds(half, half), :], wr, ssem.at[1], rsem.at[1], dev(add(x, N - shift_r, N), y, z, k))

    @pl.when(swap_l)
    def _():
        pltpu.make_async_copy(om.at[pl.ds(0, half), :], wl, rsem.at[0]).start()

    @pl.when(jnp.logical_not(swap_l))
    def _():
        om_left().start()

    @pl.when(swap_r)
    def _():
        pltpu.make_async_copy(om.at[pl.ds(half, half), :], wr, rsem.at[1]).start()

    @pl.when(jnp.logical_not(swap_r))
    def _():
        om_right().start()

    el, er = y * 2 + k, z * 2 + k
    own_el, own_er = xl * 2 + k, xd * 2 + k

    def rows_of(e):
        return pl.ds(pl.multiple_of(e * CAP, CAP), CAP)

    def send_g(d):
        e = add(own_el, d, EXP)
        remote(
            gs.at[rows_of(e), pl.ds(0, half)], gl.at[rows_of(el), :], ssem.at[2], rsem.at[2],
            dev(x, left_y(x, lax.div(e, 2), z), z, lax.rem(e, 2)),
        ).start()
        e = add(own_er, d, EXP)
        remote(
            gs.at[rows_of(e), pl.ds(half, half)], gr.at[rows_of(er), :], ssem.at[3], rsem.at[3],
            dev(x, y, right_z(x, lax.div(e, 2), y), lax.rem(e, 2)),
        ).start()

    loop(1, EXP, send_g)
    pltpu.make_async_copy(
        gs.at[rows_of(own_el), pl.ds(0, half)], gl.at[rows_of(el), :], rsem.at[2]
    ).start()
    pltpu.make_async_copy(
        gs.at[rows_of(own_er), pl.ds(half, half)], gr.at[rows_of(er), :], rsem.at[3]
    ).start()

    def send_x(d):
        e = add(ex, d, EXP)
        remote(
            xs.at[rows_of(e), :], xr.at[rows_of(ex), :], ssem.at[4], rsem.at[4], (tok, e)
        ).start()

    loop(1, EXP, send_x)
    pltpu.make_async_copy(xs.at[rows_of(ex), :], xr.at[rows_of(ex), :], rsem.at[4]).start()

    def piece(i):
        return pl.ds(pl.multiple_of(i * PIECE, PIECE), PIECE)

    def to_x(left, right, dl, dr, phase):
        nls[phase] = left.astype(BF16)
        nrs[phase] = right.astype(BF16)
        sl, sr = ssem.at[5 + 2 * phase], ssem.at[6 + 2 * phase]
        rl_, rr_ = rsem.at[5 + 2 * phase], rsem.at[6 + 2 * phase]

        def go_l(d):
            b = add(y, d, N)
            remote(nls.at[phase, piece(b), :], dl.at[piece(x), :], sl, rl_, dev(xl, b, z, k)).start()

        def go_r(d):
            c = add(z, d, N)
            remote(nrs.at[phase, piece(c), :], dr.at[piece(x), :], sr, rr_, dev(xd, y, c, k)).start()

        loop(1, N, go_l)
        loop(1, N, go_r)
        own_l = selfsem.at[2 * phase]
        own_r = selfsem.at[2 * phase + 1]

        @pl.when(swap_l)
        def _():
            pltpu.make_async_copy(nls.at[phase, piece(y), :], dl.at[piece(x), :], rl_).start()

        @pl.when(jnp.logical_not(swap_l))
        def _():
            remote(
                nls.at[phase, piece(y), :], dl.at[piece(x), :], own_l, rl_, dev(xl, y, z, k)
            ).start()

        @pl.when(swap_r)
        def _():
            pltpu.make_async_copy(nrs.at[phase, piece(z), :], dr.at[piece(x), :], rr_).start()

        @pl.when(jnp.logical_not(swap_r))
        def _():
            remote(
                nrs.at[phase, piece(z), :], dr.at[piece(x), :], own_r, rr_, dev(xd, y, z, k)
            ).start()

        bytes_wait(dl, rl_)
        bytes_wait(dr, rr_)
        total = dl[...].astype(F32) + dr[...].astype(F32)
        three = nls.at[phase, pl.ds(0, 3 * PIECE), :]
        bytes_wait(three, sl)
        bytes_wait(nrs.at[phase, pl.ds(0, 3 * PIECE), :], sr)

        @pl.when(jnp.logical_not(swap_l))
        def _():
            bytes_wait(nls.at[phase, pl.ds(0, PIECE), :], own_l)

        @pl.when(jnp.logical_not(swap_r))
        def _():
            bytes_wait(nrs.at[phase, pl.ds(0, PIECE), :], own_r)

        return total

    def gram_all(s, phase):
        gm[phase] = dot_t(s, s, HIGH).astype(BF16)
        pltpu.make_async_copy(gm.at[phase], gb.at[phase, tok], gsem.at[2 * phase]).start()

        def go(d):
            t = add(tok, d, TOK)
            remote(
                gm.at[phase], gb.at[phase, tok], gsem.at[2 * phase + 1], gsem.at[2 * phase], (t, ex)
            ).start()

        loop(1, TOK, go)
        bytes_wait(gb.at[phase], gsem.at[2 * phase])
        c = lax.fori_loop(
            0, TOK, lambda i, c: c + gb[phase, i].astype(F32), jnp.zeros((RANK, RANK), F32)
        )
        bytes_wait(gb.at[phase, pl.ds(0, TOK - 1)], gsem.at[2 * phase + 1])
        return inverse_factor(c, cm, mm)

    def reduce_x(p, dst, s, r):
        pt = p.T.astype(BF16)

        def chunk(d):
            t = add(tok, d, TOK)
            cols = pl.ds(pl.multiple_of(t * wc, 128), wc)
            sp[t] = dot(pt, xr[:, cols]).astype(BF16)

            @pl.when(d < TOK)
            def _():
                remote(sp.at[t], dst.at[tok], s, r, (t, ex)).start()

        loop(1, TOK + 1, chunk)
        pltpu.make_async_copy(sp.at[tok], dst.at[tok], r).start()
        bytes_wait(dst, r)
        total = lax.fori_loop(
            0, TOK, lambda i, c: c + dst[i].astype(F32), jnp.zeros((RANK, wc), F32)
        )
        bytes_wait(sp.at[pl.ds(0, TOK - 1)], s)
        return total

    kc = 1024

    def g_dot(w_l, w_r):
        def step(j, acc):
            cols = pl.ds(pl.multiple_of(j * kc, kc), kc)
            a, b = acc
            return (
                a + dot(gl[:, cols], w_l[cols, :]),
                b + dot(gr[:, cols], w_r[cols, :]),
            )

        zero = jnp.zeros((ROWS, RANK), F32)
        return lax.fori_loop(0, half // kc, step, (zero, zero))

    bytes_wait(wl, rsem.at[0])
    bytes_wait(wr, rsem.at[1])
    bytes_wait(gl, rsem.at[2])
    bytes_wait(gr, rsem.at[3])
    left, right = g_dot(wl, wr)
    proj = to_x(left, right, pxl, pxr, 0).astype(BF16).astype(F32)
    bytes_wait(xr, rsem.at[4])

    s = reduce_x(proj, rb, ssem.at[9], rsem.at[9])
    inv = gram_all(s, 0)
    bt[tok] = jnp.dot(inv, s, precision=HIGH, preferred_element_type=F32).astype(BF16)

    def send_b(d):
        remote(
            bt.at[tok], bt.at[tok], ssem.at[10], rsem.at[10], (add(tok, d, TOK), ex)
        ).start()

    loop(1, TOK, send_b)
    bytes_wait(bt.at[pl.ds(0, TOK - 1)], rsem.at[10])

    def w_step(t, acc):
        cols = pl.ds(pl.multiple_of(t * wc, 128), wc)
        return acc + dot_t(xr[:, cols], bt[t])

    weights = lax.fori_loop(0, TOK, w_step, jnp.zeros((ROWS, RANK), F32))
    ws[...] = weights.astype(BF16)

    def go_w(d):
        a = add(x, d, N)
        remote(
            ws.at[piece(a), :], wgl.at[piece(y), :], ssem.at[11], rsem.at[11],
            dev(a, left_y(a, x, z), z, k),
        ).start()
        remote(
            ws.at[piece(a), :], wgr.at[piece(z), :], ssem.at[12], rsem.at[12],
            dev(a, y, right_z(a, x, y), k),
        ).start()

    loop(1, N, go_w)

    @pl.when(swap_l)
    def _():
        pltpu.make_async_copy(ws.at[piece(x), :], wgl.at[piece(y), :], rsem.at[11]).start()

    @pl.when(jnp.logical_not(swap_l))
    def _():
        remote(
            ws.at[piece(x), :], wgl.at[piece(y), :], selfsem.at[4], rsem.at[11],
            dev(x, left_y(x, x, z), z, k),
        ).start()

    @pl.when(swap_r)
    def _():
        pltpu.make_async_copy(ws.at[piece(x), :], wgr.at[piece(z), :], rsem.at[12]).start()

    @pl.when(jnp.logical_not(swap_r))
    def _():
        remote(
            ws.at[piece(x), :], wgr.at[piece(z), :], selfsem.at[5], rsem.at[12],
            dev(x, y, right_z(x, x, y), k),
        ).start()

    bytes_wait(wgl, rsem.at[11])
    bytes_wait(wgr, rsem.at[12])

    wlt = wgl[...].astype(F32).T.astype(BF16)
    wrt = wgr[...].astype(F32).T.astype(BF16)
    slot_l = x * N + z
    slot_r = x * N + y

    def power_chunk(d):
        t = add(tok, d, TOK)
        cols = pl.ds(pl.multiple_of(t * hc, 128), hc)
        pwl[t] = dot(wlt, gl[:, cols]).astype(BF16)
        pwr[t] = dot(wrt, gr[:, cols]).astype(BF16)

        @pl.when(d < TOK)
        def _():
            remote(
                pwl.at[t], rl.at[slot_l], ssem.at[13], rsem.at[13], (t, own_el)
            ).start()
            remote(
                pwr.at[t], rr.at[slot_r], ssem.at[14], rsem.at[14], (t, own_er)
            ).start()

    loop(1, TOK + 1, power_chunk)

    @pl.when(swap_l)
    def _():
        pltpu.make_async_copy(pwl.at[tok], rl.at[slot_l], rsem.at[13]).start()

    @pl.when(jnp.logical_not(swap_l))
    def _():
        remote(
            pwl.at[tok], rl.at[slot_l], selfsem.at[6], rsem.at[13], (tok, own_el)
        ).start()

    @pl.when(swap_r)
    def _():
        pltpu.make_async_copy(pwr.at[tok], rr.at[slot_r], rsem.at[14]).start()

    @pl.when(jnp.logical_not(swap_r))
    def _():
        remote(
            pwr.at[tok], rr.at[slot_r], selfsem.at[7], rsem.at[14], (tok, own_er)
        ).start()

    bytes_wait(rl, rsem.at[13])
    bytes_wait(rr, rsem.at[14])
    zero = jnp.zeros((RANK, hc), F32)
    sl = lax.fori_loop(0, TOK, lambda i, c: c + rl[i].astype(F32), zero)
    sr = lax.fori_loop(0, TOK, lambda i, c: c + rr[i].astype(F32), zero)
    s2 = jnp.concatenate([sl, sr], axis=1)
    inv = gram_all(s2, 1)
    right_basis = jnp.dot(inv, s2, precision=HIGH, preferred_element_type=F32).astype(BF16)

    bytes_wait(pwl.at[pl.ds(0, TOK - 1)], ssem.at[13])
    bytes_wait(pwr.at[pl.ds(0, TOK - 1)], ssem.at[14])

    @pl.when(jnp.logical_not(swap_l))
    def _():
        bytes_wait(pwl.at[0], selfsem.at[6])
        bytes_wait(ws.at[piece(0), :], selfsem.at[4])

    @pl.when(jnp.logical_not(swap_r))
    def _():
        bytes_wait(pwr.at[0], selfsem.at[7])
        bytes_wait(ws.at[piece(0), :], selfsem.at[5])

    pwl[0] = right_basis[:, :hc]
    pwr[0] = right_basis[:, hc:]

    def send_r(d):
        a = add(x, lax.div(d, N), N)
        c = add(z, lax.rem(d, N), N)
        remote(
            pwl.at[0], rbl.at[tok], ssem.at[15], rsem.at[15],
            dev(a, left_y(a, x, c), c, k),
        ).start()
        b = add(y, lax.rem(d, N), N)
        remote(
            pwr.at[0], rbr.at[tok], ssem.at[16], rsem.at[16],
            dev(a, b, right_z(a, x, b), k),
        ).start()

    loop(1, TOK, send_r)

    @pl.when(swap_l)
    def _():
        pltpu.make_async_copy(pwl.at[0], rbl.at[tok], rsem.at[15]).start()

    @pl.when(jnp.logical_not(swap_l))
    def _():
        remote(pwl.at[0], rbl.at[tok], selfsem.at[8], rsem.at[15], dev(x, left_y(x, x, z), z, k)).start()

    @pl.when(swap_r)
    def _():
        pltpu.make_async_copy(pwr.at[0], rbr.at[tok], rsem.at[16]).start()

    @pl.when(jnp.logical_not(swap_r))
    def _():
        remote(pwr.at[0], rbr.at[tok], selfsem.at[9], rsem.at[16], dev(x, y, right_z(x, x, y), k)).start()

    bytes_wait(rbl, rsem.at[15])
    bytes_wait(rbr, rsem.at[16])

    def s_step(t, acc):
        cols = pl.ds(pl.multiple_of(t * hc, 128), hc)
        a, b = acc
        return a + dot_t(gl[:, cols], rbl[t]), b + dot_t(gr[:, cols], rbr[t])

    zero = jnp.zeros((ROWS, RANK), F32)
    left, right = lax.fori_loop(0, TOK, s_step, (zero, zero))
    second = to_x(left, right, pxl2, pxr2, 1).astype(BF16).astype(F32)

    s3 = reduce_x(second, rb3, ssem.at[17], rsem.at[17])
    inv = gram_all(s3, 2)
    last = jnp.dot(inv, s3, precision=HIGH, preferred_element_type=F32)
    out[0] = last.T * scale

    @pl.when(jnp.logical_not(swap_l))
    def _():
        om_left().wait_send()
        bytes_wait(pwl.at[0], selfsem.at[8])

    @pl.when(jnp.logical_not(swap_r))
    def _():
        om_right().wait_send()
        bytes_wait(pwr.at[0], selfsem.at[9])

    part = pl.ds(0, ROWS - CAP)
    bytes_wait(gl.at[part, :], ssem.at[2])
    bytes_wait(gr.at[part, :], ssem.at[3])
    bytes_wait(xr.at[part, :], ssem.at[4])
    bytes_wait(bt.at[pl.ds(0, TOK - 1)], ssem.at[10])
    bytes_wait(ws.at[pl.ds(0, 3 * PIECE), :], ssem.at[11])
    bytes_wait(ws.at[pl.ds(0, 3 * PIECE), :], ssem.at[12])
    bytes_wait(rl.at[pl.ds(0, TOK - 1)], ssem.at[15])
    bytes_wait(rr.at[pl.ds(0, TOK - 1)], ssem.at[16])


def owners(gs, xs, om):
    hidden = gs.shape[1]
    width = xs.shape[1]
    half = hidden // 2
    wc, hc = width // TOK, half // TOK

    def vm(*shape, dtype=BF16):
        return pltpu.VMEM(shape, dtype)

    any_spec = pl.BlockSpec(memory_space=pl.ANY)
    return pl.pallas_call(
        functools.partial(body, float(width) ** 0.5),
        out_shape=jax.ShapeDtypeStruct((1, wc, RANK), F32),
        in_specs=[any_spec] * 3,
        out_specs=pl.BlockSpec(memory_space=pltpu.VMEM),
        scratch_shapes=[
            vm(ROWS, width), vm(ROWS, half), vm(ROWS, half), vm(half, RANK), vm(half, RANK),
            vm(2, ROWS, RANK), vm(2, ROWS, RANK),
            vm(ROWS, RANK), vm(ROWS, RANK), vm(ROWS, RANK), vm(ROWS, RANK),
            vm(TOK, RANK, wc), vm(TOK, RANK, wc), vm(TOK, RANK, wc), vm(TOK, RANK, wc),
            vm(ROWS, RANK), vm(ROWS, RANK), vm(ROWS, RANK),
            vm(TOK, RANK, hc), vm(TOK, RANK, hc), vm(TOK, RANK, hc), vm(TOK, RANK, hc),
            vm(TOK, RANK, hc), vm(TOK, RANK, hc),
            vm(3, RANK, RANK), vm(3, TOK, RANK, RANK),
            vm(RANK, RANK, dtype=F32), vm(RANK, RANK, dtype=F32),
            pltpu.SemaphoreType.DMA((18,)),
            pltpu.SemaphoreType.DMA((18,)),
            pltpu.SemaphoreType.DMA((6,)),
            pltpu.SemaphoreType.DMA((10,)),
        ],
        compiler_params=pltpu.CompilerParams(
            collective_id=0, has_side_effects=True, vmem_limit_bytes=58 * 1024 * 1024
        ),
        name="owners",
    )(gs, xs, om)


def shards(activations, expert_ids, out_grads, sketch_matrix):
    gs, xs = sort_rows(expert_ids, out_grads, activations)
    om = sketch_matrix.reshape(sketch_matrix.shape[1:])
    return owners(gs, xs, om)


def solution(mesh):
    return jax.shard_map(
        shards,
        mesh=mesh,
        in_specs=(
            P(("tok", "exp"), None),
            P(("tok", "exp"), None),
            P(("tok", "exp"), None, None),
            P("exp", None, None),
        ),
        out_specs=P("exp", "tok", None),
        check_vma=False,
    )
```

```python
import functools

import jax
import jax.numpy as jnp
from jax import lax
from jax.experimental import pallas as pl
from jax.experimental.pallas import tpu as pltpu
from jax.sharding import PartitionSpec as P

MESH = pl.DeviceIdType.MESH
HIGH = lax.Precision.HIGHEST
F32 = jnp.float32
BF16 = jnp.bfloat16

N = 4
TOK = N * N
EXP = 2 * N
CAP = 48
ROWS = EXP * CAP
PIECE = 2 * CAP
RANK = 128
PANEL = 16


def dot(a, b):
    return jnp.dot(a, b, preferred_element_type=F32)


def dot_t(a, b, precision=None):
    return lax.dot_general(
        a, b, (((1,), (1,)), ((), ())), precision=precision, preferred_element_type=F32
    )


def sort_kernel(row_ids, col_ids, g_ref, x_ref, gs_ref, xs_ref, pick, pick_x):
    pairs = row_ids.shape[1]
    toks, top, hc = g_ref.shape

    @pl.when(pl.program_id(0) == 0)
    def _():
        ids = row_ids[...]
        same = (col_ids[...] == ids) & (
            lax.broadcasted_iota(jnp.int32, (pairs, pairs), 0)
            < lax.broadcasted_iota(jnp.int32, (pairs, pairs), 1)
        )
        rank = jnp.sum(same.astype(F32), axis=0, keepdims=True).astype(jnp.int32)
        slot = ids * CAP + rank
        hot = lax.broadcasted_iota(jnp.int32, (ROWS, pairs), 0) == slot
        pick[...] = hot.astype(F32).astype(BF16)
        token = lax.broadcasted_iota(jnp.int32, (pairs, toks), 0) - top * lax.broadcasted_iota(
            jnp.int32, (pairs, toks), 1
        )
        of_token = ((token >= 0) & (token < top)).astype(F32).astype(BF16)
        pick_x[...] = dot(pick[...], of_token).astype(BF16)

    gs_ref[...] = dot(pick[...], g_ref[...].reshape(pairs, hc)).astype(BF16)
    xs_ref[...] = dot(pick_x[...], x_ref[...]).astype(BF16)


def sort_rows(expert_ids, out_grads, activations, steps=8):
    toks, top = expert_ids.shape
    pairs = toks * top
    hidden = out_grads.shape[2]
    width = activations.shape[1]
    ids = expert_ids.reshape(1, pairs)
    hc, wc = hidden // steps, width // steps
    return pl.pallas_call(
        sort_kernel,
        grid=(steps,),
        out_shape=(
            jax.ShapeDtypeStruct((ROWS, hidden), BF16),
            jax.ShapeDtypeStruct((ROWS, width), BF16),
        ),
        in_specs=[
            pl.BlockSpec((1, pairs), lambda i: (0, 0)),
            pl.BlockSpec((pairs, 1), lambda i: (0, 0)),
            pl.BlockSpec((toks, top, hc), lambda i: (0, 0, i)),
            pl.BlockSpec((toks, wc), lambda i: (0, i)),
        ],
        out_specs=(
            pl.BlockSpec((ROWS, hc), lambda i: (0, i)),
            pl.BlockSpec((ROWS, wc), lambda i: (0, i)),
        ),
        scratch_shapes=[pltpu.VMEM((ROWS, pairs), BF16), pltpu.VMEM((ROWS, toks), BF16)],
        compiler_params=pltpu.CompilerParams(vmem_limit_bytes=40 * 1024 * 1024),
        name="sort",
    )(ids, ids.reshape(pairs, 1), out_grads, activations)


def bytes_wait(ref, sem):
    pltpu.make_async_copy(ref, ref, sem).wait()


def inverse_factor(c, cm, mm):
    cm[...] = c
    rows = lax.broadcasted_iota(jnp.int32, (RANK, RANK), 0)
    cols = lax.broadcasted_iota(jnp.int32, (RANK, RANK), 1)
    mm[...] = (rows == cols).astype(F32)
    prow = lax.broadcasted_iota(jnp.int32, (PANEL, RANK), 0)
    pcol = lax.broadcasted_iota(jnp.int32, (PANEL, RANK), 1)

    def panel(p, carry):
        base = pl.multiple_of(p * PANEL, PANEL)
        a = cm[pl.ds(base, PANEL), :]
        m = mm[pl.ds(base, PANEL), :]
        near = pltpu.roll(a, lax.rem(RANK - base, RANK), 1)
        block = [jnp.broadcast_to(near[:, i : i + 1], (PANEL, RANK)) for i in range(PANEL)]
        for i in range(PANEL):
            r = lax.rsqrt(block[i][i : i + 1, :])
            mult = jnp.where(prow > i, block[i] * (r * r), 0.0)
            for j in range(i + 1, PANEL):
                block[j] = block[j] - mult * block[j][i : i + 1, :]
            a = jnp.where(prow == i, a * r, a - mult * a[i : i + 1, :])
            m = jnp.where(prow == i, m * r, m - mult * m[i : i + 1, :])
        mm[pl.ds(base, PANEL), :] = m
        left = jnp.where(pcol >= base + PANEL, a, 0.0)
        both = jnp.concatenate([a, m], axis=1)
        change = lax.dot_general(
            left, both, (((0,), (0,)), ((), ())), precision=HIGH, preferred_element_type=F32
        )
        cm[...] -= change[:, :RANK]
        mm[...] -= change[:, RANK:]
        return carry

    lax.fori_loop(0, RANK // PANEL, panel, 0)
    return mm[...]


def body(
    scale,
    gs, xs, om,
    out,
    xr, gl, gr, wl, wr,
    nls, nrs, pxl, pxr, pxl2, pxr2,
    sp, rb, rb3, bt,
    ws, wgl, wgr,
    pwl, pwr, rl1, rr1, mid_l, mid_r, rl2, rr2, own_rl, own_rr, rbl, rbr,
    gm, gb, cm, mm,
    ssem, rsem, gsem, selfsem,
):
    tok = lax.axis_index("tok")
    ex = lax.axis_index("exp")
    y, z = lax.div(tok, N), lax.rem(tok, N)
    x, k = lax.div(ex, 2), lax.rem(ex, 2)
    half = gl.shape[1]
    width = xr.shape[1]
    wc = width // TOK
    hc = half // TOK

    def dev(a, b, c, core):
        return (b * N + c, a * 2 + core)

    def add(a, b, n):
        return lax.rem(a + b, n)

    def remote(src, dst, s, r, where):
        return pltpu.make_async_remote_copy(
            src_ref=src, dst_ref=dst, send_sem=s, recv_sem=r, device_id=where, device_id_type=MESH
        )

    def loop(lo, hi, fn):
        lax.fori_loop(lo, hi, lambda i, c: (fn(i), c)[1], 0)

    barrier = pltpu.get_barrier_semaphore()

    def greet(where):
        pl.semaphore_signal(barrier, inc=1, device_id=where, device_id_type=MESH)

    chip = x * TOK + tok

    def same_core(d):
        c = add(chip, d, N * TOK)
        greet((lax.rem(c, TOK), lax.div(c, TOK) * 2 + k))

    loop(1, N * TOK, same_core)

    def other_core(d):
        greet(dev(add(x, d, N), y, z, 1 - k))

    loop(0, N, other_core)

    def other_core_y(d):
        greet(dev(x, add(y, d, N), z, 1 - k))
        greet(dev(x, y, add(z, d, N), 1 - k))

    loop(1, N, other_core_y)
    pl.semaphore_wait(barrier, N * TOK - 1 + N + 2 * (N - 1))

    shift_r = lax.rem(N - z, N)
    swap_l = y == 0
    swap_r = z == 0
    xl = add(x, y, N)
    xd = add(x, shift_r, N)
    own_el, own_er = xl * 2 + k, xd * 2 + k

    def left_y(at_x, to_x):
        return lax.rem(to_x - at_x + N, N)

    def right_z(at_x, to_x):
        return lax.rem(at_x - to_x + N, N)

    quarter = half // N

    def om_rows(i):
        return pl.ds(pl.multiple_of(i * quarter, quarter), quarter)

    def om_right_rows(i):
        return pl.ds(pl.multiple_of(half + i * quarter, quarter), quarter)

    def om_left():
        return remote(
            om.at[om_rows(z), :], wl.at[om_rows(z), :], ssem.at[0], rsem.at[0],
            dev(add(x, N - y, N), y, z, k),
        )

    def om_right():
        return remote(
            om.at[om_right_rows(y), :], wr.at[om_rows(y), :], ssem.at[1], rsem.at[1],
            dev(add(x, z, N), y, z, k),
        )

    @pl.when(swap_l)
    def _():
        pltpu.make_async_copy(om.at[om_rows(z), :], wl.at[om_rows(z), :], rsem.at[0]).start()

    @pl.when(jnp.logical_not(swap_l))
    def _():
        om_left().start()

    @pl.when(swap_r)
    def _():
        pltpu.make_async_copy(om.at[om_right_rows(y), :], wr.at[om_rows(y), :], rsem.at[1]).start()

    @pl.when(jnp.logical_not(swap_r))
    def _():
        om_right().start()

    el, er = y * 2 + k, z * 2 + k

    def rows_of(e):
        return pl.ds(pl.multiple_of(e * CAP, CAP), CAP)

    def send_g(d):
        e = add(own_el, d, EXP)
        remote(
            gs.at[rows_of(e), pl.ds(0, half)], gl.at[rows_of(el), :], ssem.at[2], rsem.at[2],
            dev(x, left_y(x, lax.div(e, 2)), z, lax.rem(e, 2)),
        ).start()
        e = add(own_er, d, EXP)
        remote(
            gs.at[rows_of(e), pl.ds(half, half)], gr.at[rows_of(er), :], ssem.at[3], rsem.at[3],
            dev(x, y, right_z(x, lax.div(e, 2)), lax.rem(e, 2)),
        ).start()

    loop(1, EXP, send_g)
    pltpu.make_async_copy(
        gs.at[rows_of(own_el), pl.ds(0, half)], gl.at[rows_of(el), :], rsem.at[2]
    ).start()
    pltpu.make_async_copy(
        gs.at[rows_of(own_er), pl.ds(half, half)], gr.at[rows_of(er), :], rsem.at[3]
    ).start()

    def send_x(d):
        e = add(ex, d, EXP)
        remote(
            xs.at[rows_of(e), :], xr.at[rows_of(ex), :], ssem.at[4], rsem.at[4], (tok, e)
        ).start()

    loop(1, EXP, send_x)
    pltpu.make_async_copy(xs.at[rows_of(ex), :], xr.at[rows_of(ex), :], rsem.at[4]).start()

    bytes_wait(wl.at[om_rows(z), :], rsem.at[0])
    bytes_wait(wr.at[om_rows(y), :], rsem.at[1])

    def om_share(d):
        remote(
            wl.at[om_rows(z), :], wl.at[om_rows(z), :], ssem.at[18], rsem.at[18],
            dev(x, y, add(z, d, N), k),
        ).start()
        remote(
            wr.at[om_rows(y), :], wr.at[om_rows(y), :], ssem.at[19], rsem.at[19],
            dev(x, add(y, d, N), z, k),
        ).start()

    loop(1, N, om_share)

    def piece(i):
        return pl.ds(pl.multiple_of(i * PIECE, PIECE), PIECE)

    def to_x(left, right, dl, dr, phase):
        nls[phase] = left.astype(BF16)
        nrs[phase] = right.astype(BF16)
        sl, sr = ssem.at[5 + 2 * phase], ssem.at[6 + 2 * phase]
        rl_, rr_ = rsem.at[5 + 2 * phase], rsem.at[6 + 2 * phase]

        def go_l(d):
            b = add(y, d, N)
            remote(nls.at[phase, piece(b), :], dl.at[piece(x), :], sl, rl_, dev(xl, b, z, k)).start()

        def go_r(d):
            c = add(z, d, N)
            remote(nrs.at[phase, piece(c), :], dr.at[piece(x), :], sr, rr_, dev(xd, y, c, k)).start()

        loop(1, N, go_l)
        loop(1, N, go_r)
        own_l = selfsem.at[12 + 2 * phase]
        own_r = selfsem.at[13 + 2 * phase]

        @pl.when(swap_l)
        def _():
            pltpu.make_async_copy(nls.at[phase, piece(y), :], dl.at[piece(x), :], rl_).start()

        @pl.when(jnp.logical_not(swap_l))
        def _():
            remote(
                nls.at[phase, piece(y), :], dl.at[piece(x), :], own_l, rl_, dev(xl, y, z, k)
            ).start()

        @pl.when(swap_r)
        def _():
            pltpu.make_async_copy(nrs.at[phase, piece(z), :], dr.at[piece(x), :], rr_).start()

        @pl.when(jnp.logical_not(swap_r))
        def _():
            remote(
                nrs.at[phase, piece(z), :], dr.at[piece(x), :], own_r, rr_, dev(xd, y, z, k)
            ).start()

        bytes_wait(dl, rl_)
        bytes_wait(dr, rr_)
        total = dl[...].astype(F32) + dr[...].astype(F32)
        three = nls.at[phase, pl.ds(0, 3 * PIECE), :]
        bytes_wait(three, sl)
        bytes_wait(nrs.at[phase, pl.ds(0, 3 * PIECE), :], sr)

        @pl.when(jnp.logical_not(swap_l))
        def _():
            bytes_wait(nls.at[phase, pl.ds(0, PIECE), :], own_l)

        @pl.when(jnp.logical_not(swap_r))
        def _():
            bytes_wait(nrs.at[phase, pl.ds(0, PIECE), :], own_r)

        return total

    def gram_all(s, phase):
        gm[phase] = dot_t(s, s, HIGH).astype(BF16)
        pltpu.make_async_copy(gm.at[phase], gb.at[phase, tok], gsem.at[2 * phase]).start()

        def go(d):
            t = add(tok, d, TOK)
            remote(
                gm.at[phase], gb.at[phase, tok], gsem.at[2 * phase + 1], gsem.at[2 * phase], (t, ex)
            ).start()

        loop(1, TOK, go)
        bytes_wait(gb.at[phase], gsem.at[2 * phase])
        c = lax.fori_loop(
            0, TOK, lambda i, c: c + gb[phase, i].astype(F32), jnp.zeros((RANK, RANK), F32)
        )
        bytes_wait(gb.at[phase, pl.ds(0, TOK - 1)], gsem.at[2 * phase + 1])
        return inverse_factor(c, cm, mm)

    def reduce_x(p, dst, s, r):
        pt = p.T.astype(BF16)

        def chunk(d):
            t = add(tok, d, TOK)
            cols = pl.ds(pl.multiple_of(t * wc, 128), wc)
            sp[t] = dot(pt, xr[:, cols]).astype(BF16)

            @pl.when(d < TOK)
            def _():
                remote(sp.at[t], dst.at[tok], s, r, (t, ex)).start()

        loop(1, TOK + 1, chunk)
        pltpu.make_async_copy(sp.at[tok], dst.at[tok], r).start()
        bytes_wait(dst, r)
        total = lax.fori_loop(
            0, TOK, lambda i, c: c + dst[i].astype(F32), jnp.zeros((RANK, wc), F32)
        )
        bytes_wait(sp.at[pl.ds(0, TOK - 1)], s)
        return total

    kc = 1024

    def g_dot(w_l, w_r):
        def step(j, acc):
            cols = pl.ds(pl.multiple_of(j * kc, kc), kc)
            a, b = acc
            return (
                a + dot(gl[:, cols], w_l[cols, :]),
                b + dot(gr[:, cols], w_r[cols, :]),
            )

        zero = jnp.zeros((ROWS, RANK), F32)
        return lax.fori_loop(0, half // kc, step, (zero, zero))

    most = pl.ds(0, 3 * quarter)
    bytes_wait(wl.at[most, :], rsem.at[18])
    bytes_wait(wr.at[most, :], rsem.at[19])
    bytes_wait(gl, rsem.at[2])
    bytes_wait(gr, rsem.at[3])
    left, right = g_dot(wl, wr)
    proj = to_x(left, right, pxl, pxr, 0).astype(BF16).astype(F32)
    bytes_wait(xr, rsem.at[4])

    s = reduce_x(proj, rb, ssem.at[9], rsem.at[9])
    inv = gram_all(s, 0)
    bt[tok] = jnp.dot(inv, s, precision=HIGH, preferred_element_type=F32).astype(BF16)

    def send_b(d):
        remote(
            bt.at[tok], bt.at[tok], ssem.at[10], rsem.at[10], (add(tok, d, TOK), ex)
        ).start()

    loop(1, TOK, send_b)
    bytes_wait(bt.at[pl.ds(0, TOK - 1)], rsem.at[10])

    def w_step(t, acc):
        cols = pl.ds(pl.multiple_of(t * wc, 128), wc)
        return acc + dot_t(xr[:, cols], bt[t])

    weights = lax.fori_loop(0, TOK, w_step, jnp.zeros((ROWS, RANK), F32))
    ws[...] = weights.astype(BF16)

    def go_w(d):
        a = add(x, d, N)
        remote(
            ws.at[piece(a), :], wgl.at[piece(y), :], ssem.at[11], rsem.at[11],
            dev(a, left_y(a, x), z, k),
        ).start()
        remote(
            ws.at[piece(a), :], wgr.at[piece(z), :], ssem.at[12], rsem.at[12],
            dev(a, y, right_z(a, x), k),
        ).start()

    loop(1, N, go_w)

    @pl.when(swap_l)
    def _():
        pltpu.make_async_copy(ws.at[piece(x), :], wgl.at[piece(y), :], rsem.at[11]).start()

    @pl.when(jnp.logical_not(swap_l))
    def _():
        remote(
            ws.at[piece(x), :], wgl.at[piece(y), :], selfsem.at[16], rsem.at[11],
            dev(x, left_y(x, x), z, k),
        ).start()

    @pl.when(swap_r)
    def _():
        pltpu.make_async_copy(ws.at[piece(x), :], wgr.at[piece(z), :], rsem.at[12]).start()

    @pl.when(jnp.logical_not(swap_r))
    def _():
        remote(
            ws.at[piece(x), :], wgr.at[piece(z), :], selfsem.at[17], rsem.at[12],
            dev(x, y, right_z(x, x), k),
        ).start()

    bytes_wait(wgl, rsem.at[11])
    bytes_wait(wgr, rsem.at[12])

    wlt = wgl[...].astype(F32).T.astype(BF16)
    wrt = wgr[...].astype(F32).T.astype(BF16)

    def cols_of(b, c):
        return pl.ds(pl.multiple_of((b * N + c) * hc, 128), hc)

    def power_group(d):
        g = add(z, d, N)

        def left_one(b):
            pwl[g, b] = dot(wlt, gl[:, cols_of(b, g)]).astype(BF16)

        loop(0, N, left_one)

        @pl.when(d < N)
        def _():
            remote(pwl.at[g], rl1.at[z], ssem.at[13], rsem.at[13], dev(x, y, g, k)).start()

        g2 = add(y, d, N)

        def right_one(c):
            pwr[g2, c] = dot(wrt, gr[:, cols_of(g2, c)]).astype(BF16)

        loop(0, N, right_one)

        @pl.when(d < N)
        def _():
            remote(pwr.at[g2], rr1.at[y], ssem.at[14], rsem.at[14], dev(x, g2, z, k)).start()

    loop(1, N + 1, power_group)
    part3 = pl.ds(0, N - 1)
    bytes_wait(rl1.at[part3], rsem.at[13])

    def sum_along(d, own, got, me, other):
        def term(i, acc):
            return acc + got[add(me, i, N), other].astype(F32)

        return lax.fori_loop(1, N, term, own[me, other].astype(F32))

    def stage2_left(i):
        b = add(y, i, N)
        mid_l[b] = sum_along(i, pwl, rl1, z, b).astype(BF16)

        @pl.when(jnp.logical_or(i < N, jnp.logical_not(swap_l)))
        def _():
            remote(
                mid_l.at[b], rl2.at[x], selfsem.at[i], rsem.at[20], dev(xl, b, z, k)
            ).start()

    def stage2_right(i):
        c = add(z, i, N)
        mid_r[c] = sum_along(i, pwr, rr1, y, c).astype(BF16)

        @pl.when(jnp.logical_or(i < N, jnp.logical_not(swap_r)))
        def _():
            remote(
                mid_r.at[c], rr2.at[x], selfsem.at[N + 1 + i], rsem.at[21], dev(xd, y, c, k)
            ).start()

    loop(1, N + 1, stage2_left)

    @pl.when(swap_l)
    def _():
        pltpu.make_async_copy(mid_l.at[y], rl2.at[x], rsem.at[20]).start()

    bytes_wait(rr1.at[part3], rsem.at[14])
    loop(1, N + 1, stage2_right)

    @pl.when(swap_r)
    def _():
        pltpu.make_async_copy(mid_r.at[z], rr2.at[x], rsem.at[21]).start()

    bytes_wait(rl2, rsem.at[20])
    bytes_wait(rr2, rsem.at[21])
    zero = jnp.zeros((RANK, hc), F32)
    sl = lax.fori_loop(0, N, lambda i, c: c + rl2[i].astype(F32), zero)
    sr = lax.fori_loop(0, N, lambda i, c: c + rr2[i].astype(F32), zero)
    s2 = jnp.concatenate([sl, sr], axis=1)
    inv = gram_all(s2, 1)
    right_basis = jnp.dot(inv, s2, precision=HIGH, preferred_element_type=F32).astype(BF16)

    own_rl[...] = right_basis[:, :hc]
    own_rr[...] = right_basis[:, hc:]

    def send_r(d):
        a = add(x, d, N)
        remote(
            own_rl, rbl.at[z, y], ssem.at[15], rsem.at[15], dev(a, left_y(a, x), z, k)
        ).start()
        remote(
            own_rr, rbr.at[y, z], ssem.at[16], rsem.at[16], dev(a, y, right_z(a, x), k)
        ).start()

    loop(1, N, send_r)

    @pl.when(swap_l)
    def _():
        pltpu.make_async_copy(own_rl, rbl.at[z, y], rsem.at[15]).start()

    @pl.when(jnp.logical_not(swap_l))
    def _():
        remote(own_rl, rbl.at[z, y], selfsem.at[10], rsem.at[15], dev(x, 0, z, k)).start()

    @pl.when(swap_r)
    def _():
        pltpu.make_async_copy(own_rr, rbr.at[y, z], rsem.at[16]).start()

    @pl.when(jnp.logical_not(swap_r))
    def _():
        remote(own_rr, rbr.at[y, z], selfsem.at[11], rsem.at[16], dev(x, y, 0, k)).start()

    bytes_wait(rbl.at[z], rsem.at[15])

    def share_l(d):
        remote(
            rbl.at[z], rbl.at[z], ssem.at[22], rsem.at[22], dev(x, y, add(z, d, N), k)
        ).start()

    loop(1, N, share_l)
    bytes_wait(rbr.at[y], rsem.at[16])

    def share_r(d):
        remote(
            rbr.at[y], rbr.at[y], ssem.at[23], rsem.at[23], dev(x, add(y, d, N), z, k)
        ).start()

    loop(1, N, share_r)

    def left_group(g, acc):
        return lax.fori_loop(
            0, N, lambda b, t: t + dot_t(gl[:, cols_of(b, g)], rbl[g, b]), acc
        )

    def right_group(g, acc):
        return lax.fori_loop(
            0, N, lambda c, t: t + dot_t(gr[:, cols_of(g, c)], rbr[g, c]), acc
        )

    zero = jnp.zeros((ROWS, RANK), F32)
    left = left_group(z, zero)
    right = right_group(y, zero)
    bytes_wait(rbl.at[part3], rsem.at[22])
    bytes_wait(rbr.at[part3], rsem.at[23])
    left = lax.fori_loop(1, N, lambda d, t: left_group(add(z, d, N), t), left)
    right = lax.fori_loop(1, N, lambda d, t: right_group(add(y, d, N), t), right)
    second = to_x(left, right, pxl2, pxr2, 1).astype(BF16).astype(F32)

    s3 = reduce_x(second, rb3, ssem.at[17], rsem.at[17])
    inv = gram_all(s3, 2)
    last = jnp.dot(inv, s3, precision=HIGH, preferred_element_type=F32)
    out[0] = last.T * scale

    @pl.when(jnp.logical_not(swap_l))
    def _():
        om_left().wait_send()
        bytes_wait(ws.at[piece(0), :], selfsem.at[16])
        bytes_wait(mid_l.at[0], selfsem.at[N])
        bytes_wait(own_rl, selfsem.at[10])

    @pl.when(jnp.logical_not(swap_r))
    def _():
        om_right().wait_send()
        bytes_wait(ws.at[piece(0), :], selfsem.at[17])
        bytes_wait(mid_r.at[0], selfsem.at[2 * N + 1])
        bytes_wait(own_rr, selfsem.at[11])

    def drain_mid(i):
        bytes_wait(mid_l.at[0], selfsem.at[i])
        bytes_wait(mid_r.at[0], selfsem.at[N + 1 + i])

    loop(1, N, drain_mid)
    bytes_wait(wl.at[most, :], ssem.at[18])
    bytes_wait(wr.at[most, :], ssem.at[19])
    bytes_wait(rl1.at[part3], ssem.at[13])
    bytes_wait(rr1.at[part3], ssem.at[14])
    bytes_wait(rbl.at[part3], ssem.at[22])
    bytes_wait(rbr.at[part3], ssem.at[23])
    part = pl.ds(0, ROWS - CAP)
    bytes_wait(gl.at[part, :], ssem.at[2])
    bytes_wait(gr.at[part, :], ssem.at[3])
    bytes_wait(xr.at[part, :], ssem.at[4])
    bytes_wait(bt.at[pl.ds(0, TOK - 1)], ssem.at[10])
    bytes_wait(ws.at[pl.ds(0, 3 * PIECE), :], ssem.at[11])
    bytes_wait(ws.at[pl.ds(0, 3 * PIECE), :], ssem.at[12])
    bytes_wait(rl2.at[part3], ssem.at[15])
    bytes_wait(rr2.at[part3], ssem.at[16])


def owners(gs, xs, om):
    hidden = gs.shape[1]
    width = xs.shape[1]
    half = hidden // 2
    wc, hc = width // TOK, half // TOK

    def vm(*shape, dtype=BF16):
        return pltpu.VMEM(shape, dtype)

    any_spec = pl.BlockSpec(memory_space=pl.ANY)
    return pl.pallas_call(
        functools.partial(body, float(width) ** 0.5),
        out_shape=jax.ShapeDtypeStruct((1, wc, RANK), F32),
        in_specs=[any_spec] * 3,
        out_specs=pl.BlockSpec(memory_space=pltpu.VMEM),
        scratch_shapes=[
            vm(ROWS, width), vm(ROWS, half), vm(ROWS, half), vm(half, RANK), vm(half, RANK),
            vm(2, ROWS, RANK), vm(2, ROWS, RANK),
            vm(ROWS, RANK), vm(ROWS, RANK), vm(ROWS, RANK), vm(ROWS, RANK),
            vm(TOK, RANK, wc), vm(TOK, RANK, wc), vm(TOK, RANK, wc), vm(TOK, RANK, wc),
            vm(ROWS, RANK), vm(ROWS, RANK), vm(ROWS, RANK),
            vm(N, N, RANK, hc), vm(N, N, RANK, hc), vm(N, N, RANK, hc), vm(N, N, RANK, hc),
            vm(N, RANK, hc), vm(N, RANK, hc), vm(N, RANK, hc), vm(N, RANK, hc),
            vm(RANK, hc), vm(RANK, hc), vm(N, N, RANK, hc), vm(N, N, RANK, hc),
            vm(3, RANK, RANK), vm(3, TOK, RANK, RANK),
            vm(RANK, RANK, dtype=F32), vm(RANK, RANK, dtype=F32),
            pltpu.SemaphoreType.DMA((24,)),
            pltpu.SemaphoreType.DMA((24,)),
            pltpu.SemaphoreType.DMA((6,)),
            pltpu.SemaphoreType.DMA((18,)),
        ],
        compiler_params=pltpu.CompilerParams(
            collective_id=0, has_side_effects=True, vmem_limit_bytes=58 * 1024 * 1024
        ),
        name="owners",
    )(gs, xs, om)


def shards(activations, expert_ids, out_grads, sketch_matrix):
    gs, xs = sort_rows(expert_ids, out_grads, activations)
    om = sketch_matrix.reshape(sketch_matrix.shape[1:])
    return owners(gs, xs, om)


def solution(mesh):
    return jax.shard_map(
        shards,
        mesh=mesh,
        in_specs=(
            P(("tok", "exp"), None),
            P(("tok", "exp"), None),
            P(("tok", "exp"), None, None),
            P("exp", None, None),
        ),
        out_specs=P("exp", "tok", None),
        check_vma=False,
    )
```

```python
import functools

import jax
import jax.numpy as jnp
from jax import lax
from jax.experimental import pallas as pl
from jax.experimental.pallas import tpu as pltpu
from jax.sharding import PartitionSpec as P

MESH = pl.DeviceIdType.MESH
HIGH = lax.Precision.HIGHEST
F32 = jnp.float32
BF16 = jnp.bfloat16

N = 4
TOK = N * N
EXP = 2 * N
CAP = 48
ROWS = EXP * CAP
PIECE = 2 * CAP
RANK = 128
PANEL = 16


def dot(a, b):
    return jnp.dot(a, b, preferred_element_type=F32)


def dot_t(a, b, precision=None):
    return lax.dot_general(
        a, b, (((1,), (1,)), ((), ())), precision=precision, preferred_element_type=F32
    )


def picks(row_ids, col_ids, pick, pick_x):
    pairs = row_ids.shape[1]
    toks = pick_x.shape[1]
    top = pairs // toks
    ids = row_ids[...]
    same = (col_ids[...] == ids) & (
        lax.broadcasted_iota(jnp.int32, (pairs, pairs), 0)
        < lax.broadcasted_iota(jnp.int32, (pairs, pairs), 1)
    )
    rank = jnp.sum(same.astype(F32), axis=0, keepdims=True).astype(jnp.int32)
    slot = ids * CAP + rank
    hot = lax.broadcasted_iota(jnp.int32, (ROWS, pairs), 0) == slot
    pick[...] = hot.astype(F32).astype(BF16)
    token = lax.broadcasted_iota(jnp.int32, (pairs, toks), 0) - top * lax.broadcasted_iota(
        jnp.int32, (pairs, toks), 1
    )
    of_token = ((token >= 0) & (token < top)).astype(F32).astype(BF16)
    pick_x[...] = dot(pick[...], of_token).astype(BF16)


def bytes_wait(ref, sem):
    pltpu.make_async_copy(ref, ref, sem).wait()


def inverse_factor(c, cm, mm):
    cm[...] = c
    rows = lax.broadcasted_iota(jnp.int32, (RANK, RANK), 0)
    cols = lax.broadcasted_iota(jnp.int32, (RANK, RANK), 1)
    mm[...] = (rows == cols).astype(F32)
    prow = lax.broadcasted_iota(jnp.int32, (PANEL, RANK), 0)
    pcol = lax.broadcasted_iota(jnp.int32, (PANEL, RANK), 1)

    def panel(p, carry):
        base = pl.multiple_of(p * PANEL, PANEL)
        a = cm[pl.ds(base, PANEL), :]
        m = mm[pl.ds(base, PANEL), :]
        near = pltpu.roll(a, lax.rem(RANK - base, RANK), 1)
        block = [jnp.broadcast_to(near[:, i : i + 1], (PANEL, RANK)) for i in range(PANEL)]
        for i in range(PANEL):
            r = lax.rsqrt(block[i][i : i + 1, :])
            mult = jnp.where(prow > i, block[i] * (r * r), 0.0)
            for j in range(i + 1, PANEL):
                block[j] = block[j] - mult * block[j][i : i + 1, :]
            a = jnp.where(prow == i, a * r, a - mult * a[i : i + 1, :])
            m = jnp.where(prow == i, m * r, m - mult * m[i : i + 1, :])
        mm[pl.ds(base, PANEL), :] = m
        left = jnp.where(pcol >= base + PANEL, a, 0.0)
        both = jnp.concatenate([a, m], axis=1)
        change = lax.dot_general(
            left, both, (((0,), (0,)), ((), ())), precision=HIGH, preferred_element_type=F32
        )
        cm[...] -= change[:, :RANK]
        mm[...] -= change[:, RANK:]
        return carry

    lax.fori_loop(0, RANK // PANEL, panel, 0)
    return mm[...]


def body(
    scale,
    row_ids, col_ids, grads, acts, om,
    out,
    pick, pick_x, g_in, x_in, gs, xs,
    xr, gl, gr, wl, wr,
    nls, nrs, pxl, pxr, pxl2, pxr2,
    spa, spb, ra1, rb1, mid_a, mid_b, ra2, rb2, bta, btb,
    ws, wgl, wgr,
    pwl, pwr, rl1, rr1, mid_l, mid_r, rl2, rr2, own_rl, own_rr, rbl, rbr,
    gm, gb, cm, mm,
    ssem, rsem, gsem, selfsem, in_sem, slot_sem, left_sem, right_sem,
    line_send, line_recv, share_recv,
):
    tok = lax.axis_index("tok")
    ex = lax.axis_index("exp")
    y, z = lax.div(tok, N), lax.rem(tok, N)
    x, k = lax.div(ex, 2), lax.rem(ex, 2)
    half = gl.shape[1]
    width = xr.shape[1]
    wc = width // TOK
    hc = half // TOK

    def dev(a, b, c, core):
        return (b * N + c, a * 2 + core)

    def add(a, b, n):
        return lax.rem(a + b, n)

    def remote(src, dst, s, r, where):
        return pltpu.make_async_remote_copy(
            src_ref=src, dst_ref=dst, send_sem=s, recv_sem=r, device_id=where, device_id_type=MESH
        )

    def loop(lo, hi, fn):
        lax.fori_loop(lo, hi, lambda i, c: (fn(i), c)[1], 0)

    pending = []

    def later(ref, sem, when=None):
        if when is None:
            pending.append(lambda: bytes_wait(ref, sem))
        else:
            pending.append(lambda: pl.when(when)(lambda: bytes_wait(ref, sem)))

    chunk = gs.shape[3]
    chunks = half // chunk
    pairs = pick.shape[1]

    def load(side, i):
        cols = pl.ds(pl.multiple_of(side * half + i * chunk, chunk), chunk)
        slot = lax.rem(i, 2)
        return pltpu.make_async_copy(
            grads.at[:, :, cols], g_in.at[side, slot], in_sem.at[side, slot]
        )

    x_load = pltpu.make_async_copy(acts, x_in, in_sem.at[2, 0])
    for i in range(2):
        load(0, i).start()
        load(1, i).start()
    x_load.start()

    barrier = pltpu.get_barrier_semaphore()

    def greet(where):
        pl.semaphore_signal(barrier, inc=1, device_id=where, device_id_type=MESH)

    chip = x * TOK + tok

    def same_core(d):
        c = add(chip, d, N * TOK)
        greet((lax.rem(c, TOK), lax.div(c, TOK) * 2 + k))

    loop(1, N * TOK, same_core)

    def other_core(d):
        greet(dev(add(x, d, N), y, z, 1 - k))

    loop(0, N, other_core)

    def other_core_y(d):
        greet(dev(x, add(y, d, N), z, 1 - k))
        greet(dev(x, y, add(z, d, N), 1 - k))

    loop(1, N, other_core_y)
    picks(row_ids, col_ids, pick, pick_x)
    pl.semaphore_wait(barrier, N * TOK - 1 + N + 2 * (N - 1))

    shift_r = lax.rem(N - z, N)
    swap_l = y == 0
    swap_r = z == 0
    xl = add(x, y, N)
    xd = add(x, shift_r, N)
    own_el, own_er = xl * 2 + k, xd * 2 + k

    def left_y(at_x, to_x):
        return lax.rem(to_x - at_x + N, N)

    def right_z(at_x, to_x):
        return lax.rem(at_x - to_x + N, N)

    quarter = half // N

    def om_rows(i):
        return pl.ds(pl.multiple_of(i * quarter, quarter), quarter)

    def om_right_rows(i):
        return pl.ds(pl.multiple_of(half + i * quarter, quarter), quarter)

    def om_left():
        return remote(
            om.at[om_rows(z), :], wl.at[om_rows(z), :], ssem.at[0], rsem.at[0],
            dev(add(x, N - y, N), y, z, k),
        )

    def om_right():
        return remote(
            om.at[om_right_rows(y), :], wr.at[om_rows(y), :], ssem.at[1], rsem.at[1],
            dev(add(x, z, N), y, z, k),
        )

    @pl.when(swap_l)
    def _():
        pltpu.make_async_copy(om.at[om_rows(z), :], wl.at[om_rows(z), :], rsem.at[0]).start()

    @pl.when(jnp.logical_not(swap_l))
    def _():
        om_left().start()

    @pl.when(swap_r)
    def _():
        pltpu.make_async_copy(om.at[om_right_rows(y), :], wr.at[om_rows(y), :], rsem.at[1]).start()

    @pl.when(jnp.logical_not(swap_r))
    def _():
        om_right().start()

    later(wl.at[om_rows(0), :], ssem.at[0], jnp.logical_not(swap_l))
    later(wr.at[om_rows(0), :], ssem.at[1], jnp.logical_not(swap_r))

    el, er = y * 2 + k, z * 2 + k

    def rows_of(e):
        return pl.ds(pl.multiple_of(e * CAP, CAP), CAP)

    def send_chunk(i, first):
        slot = lax.rem(i, 2)
        cols = pl.ds(pl.multiple_of(i * chunk, chunk), chunk)
        for side, dst, own, here, sems in (
            (0, gl, own_el, el, left_sem), (1, gr, own_er, er, right_sem),
        ):
            load(side, i).wait()
            if not first:
                bytes_wait(gs.at[side, slot, part, :], slot_sem.at[side, slot])
            block = g_in[side, slot].reshape(pairs, chunk)
            gs[side, slot] = dot(pick[...], block).astype(BF16)

            @pl.when(i + 2 < chunks)
            def _():
                load(side, i + 2).start()

            def send_g(d):
                e = add(own, d, EXP)
                to, core = lax.div(e, 2), lax.rem(e, 2)
                if side == 0:
                    where = dev(x, left_y(x, to), z, core)
                else:
                    where = dev(x, y, right_z(x, to), core)
                remote(
                    gs.at[side, slot, rows_of(e), :], dst.at[rows_of(here), cols],
                    slot_sem.at[side, slot], sems.at[i], where,
                ).start()

            loop(1, EXP, send_g)
            dst[rows_of(here), cols] = gs[side, slot, rows_of(own), :]

    part = pl.ds(0, ROWS - CAP)
    send_chunk(0, True)

    x_load.wait()

    def sort_x(t):
        cols = pl.ds(pl.multiple_of(t * wc, 128), wc)
        xs[:, cols] = dot(pick_x[...], x_in[:, cols]).astype(BF16)

    loop(0, TOK, sort_x)

    def send_x(d):
        e = add(ex, d, EXP)
        remote(
            xs.at[rows_of(e), :], xr.at[rows_of(ex), :], ssem.at[4], rsem.at[4], (tok, e)
        ).start()

    loop(1, EXP, send_x)
    later(xr.at[part, :], ssem.at[4])
    pltpu.make_async_copy(xs.at[rows_of(ex), :], xr.at[rows_of(ex), :], rsem.at[4]).start()

    send_chunk(1, True)
    bytes_wait(wl.at[om_rows(z), :], rsem.at[0])
    bytes_wait(wr.at[om_rows(y), :], rsem.at[1])

    def om_share(d):
        remote(
            wl.at[om_rows(z), :], wl.at[om_rows(z), :], ssem.at[18], rsem.at[18],
            dev(x, y, add(z, d, N), k),
        ).start()
        remote(
            wr.at[om_rows(y), :], wr.at[om_rows(y), :], ssem.at[19], rsem.at[19],
            dev(x, add(y, d, N), z, k),
        ).start()

    loop(1, N, om_share)
    most = pl.ds(0, 3 * quarter)
    later(wl.at[most, :], ssem.at[18])
    later(wr.at[most, :], ssem.at[19])

    loop(2, chunks, lambda i: send_chunk(i, False))
    for slot in range(2):
        later(gs.at[0, slot, part, :], slot_sem.at[0, slot])
        later(gs.at[1, slot, part, :], slot_sem.at[1, slot])

    def piece(i):
        return pl.ds(pl.multiple_of(i * PIECE, PIECE), PIECE)

    def to_x(left, right, dl, dr, phase):
        nls[phase] = left.astype(BF16)
        nrs[phase] = right.astype(BF16)
        sl, sr = ssem.at[5 + 2 * phase], ssem.at[6 + 2 * phase]
        rl_, rr_ = rsem.at[5 + 2 * phase], rsem.at[6 + 2 * phase]

        def go_l(d):
            b = add(y, d, N)
            remote(nls.at[phase, piece(b), :], dl.at[piece(x), :], sl, rl_, dev(xl, b, z, k)).start()

        def go_r(d):
            c = add(z, d, N)
            remote(nrs.at[phase, piece(c), :], dr.at[piece(x), :], sr, rr_, dev(xd, y, c, k)).start()

        loop(1, N, go_l)
        loop(1, N, go_r)
        own_l = selfsem.at[12 + 2 * phase]
        own_r = selfsem.at[13 + 2 * phase]

        @pl.when(swap_l)
        def _():
            pltpu.make_async_copy(nls.at[phase, piece(y), :], dl.at[piece(x), :], rl_).start()

        @pl.when(jnp.logical_not(swap_l))
        def _():
            remote(
                nls.at[phase, piece(y), :], dl.at[piece(x), :], own_l, rl_, dev(xl, y, z, k)
            ).start()

        @pl.when(swap_r)
        def _():
            pltpu.make_async_copy(nrs.at[phase, piece(z), :], dr.at[piece(x), :], rr_).start()

        @pl.when(jnp.logical_not(swap_r))
        def _():
            remote(
                nrs.at[phase, piece(z), :], dr.at[piece(x), :], own_r, rr_, dev(xd, y, z, k)
            ).start()

        bytes_wait(dl, rl_)
        bytes_wait(dr, rr_)
        total = dl[...].astype(F32) + dr[...].astype(F32)
        three = nls.at[phase, pl.ds(0, 3 * PIECE), :]
        bytes_wait(three, sl)
        bytes_wait(nrs.at[phase, pl.ds(0, 3 * PIECE), :], sr)

        @pl.when(jnp.logical_not(swap_l))
        def _():
            bytes_wait(nls.at[phase, pl.ds(0, PIECE), :], own_l)

        @pl.when(jnp.logical_not(swap_r))
        def _():
            bytes_wait(nrs.at[phase, pl.ds(0, PIECE), :], own_r)

        return total

    def gram_all(s, phase):
        gm[phase] = dot_t(s, s, HIGH).astype(BF16)
        pltpu.make_async_copy(gm.at[phase], gb.at[phase, tok], gsem.at[2 * phase]).start()

        def go(d):
            t = add(tok, d, TOK)
            remote(
                gm.at[phase], gb.at[phase, tok], gsem.at[2 * phase + 1], gsem.at[2 * phase], (t, ex)
            ).start()

        loop(1, TOK, go)
        bytes_wait(gb.at[phase], gsem.at[2 * phase])
        c = lax.fori_loop(
            0, TOK, lambda i, c: c + gb[phase, i].astype(F32), jnp.zeros((RANK, RANK), F32)
        )
        bytes_wait(gb.at[phase, pl.ds(0, TOK - 1)], gsem.at[2 * phase + 1])
        return inverse_factor(c, cm, mm)

    part3 = pl.ds(0, N - 1)

    def sum_along(own, got, me, other):
        def term(i, acc):
            return acc + got[add(me, i, N), other].astype(F32)

        return lax.fori_loop(1, N, term, own[me, other].astype(F32))

    def sum_last(own, got, me):
        def term(i, acc):
            return acc + got[add(me, i, N)].astype(F32)

        return lax.fori_loop(1, N, term, own[me].astype(F32))

    def x_cols(b, c):
        return pl.ds(pl.multiple_of((b * N + c) * wc, 128), wc)

    rh = RANK // 2

    def reduce_x(p, phase):
        pt = p.T.astype(BF16)
        s, r = line_send.at[phase], line_recv.at[phase]
        ra, rb = ra1.at[phase], rb1.at[phase]
        ra_last, rb_last = ra2.at[phase], rb2.at[phase]

        def group(d):
            b = add(y, d, N)

            def one(c):
                v = dot(pt, xr[:, x_cols(b, c)]).astype(BF16)
                spa[b, c] = v[:rh]
                spb[c, b] = v[rh:]

            loop(0, N, one)

            @pl.when(d < N)
            def _():
                remote(spa.at[b], ra.at[y], s.at[0], r.at[0], dev(x, b, z, k)).start()

        loop(1, N + 1, group)

        def send_b(d):
            c = add(z, d, N)
            remote(spb.at[c], rb.at[z], s.at[1], r.at[1], dev(x, y, c, k)).start()

        loop(1, N, send_b)
        bytes_wait(ra.at[part3], r.at[0])

        def second_a(d):
            c = add(z, d, N)
            mid_a[c] = sum_along(spa, ra, y, c).astype(BF16)

            @pl.when(d < N)
            def _():
                remote(mid_a.at[c], ra_last.at[z], s.at[2], r.at[2], dev(x, y, c, k)).start()

        loop(1, N + 1, second_a)
        bytes_wait(rb.at[part3], r.at[1])

        def second_b(d):
            b = add(y, d, N)
            mid_b[b] = sum_along(spb, rb, z, b).astype(BF16)

            @pl.when(d < N)
            def _():
                remote(mid_b.at[b], rb_last.at[y], s.at[3], r.at[3], dev(x, b, z, k)).start()

        loop(1, N + 1, second_b)
        bytes_wait(ra_last.at[part3], r.at[2])
        top = sum_last(mid_a, ra_last, z)
        bytes_wait(rb_last.at[part3], r.at[3])
        low = sum_last(mid_b, rb_last, y)
        bytes_wait(spa.at[part3], s.at[0])
        bytes_wait(spb.at[part3], s.at[1])
        bytes_wait(mid_a.at[part3], s.at[2])
        bytes_wait(mid_b.at[part3], s.at[3])
        return jnp.concatenate([top, low], axis=0)

    bytes_wait(wl.at[most, :], rsem.at[18])
    bytes_wait(wr.at[most, :], rsem.at[19])

    def proj_chunk(i, acc):
        cols = pl.ds(pl.multiple_of(i * chunk, chunk), chunk)
        a, b = acc
        bytes_wait(gl.at[part, cols], left_sem.at[i])
        a = a + dot(gl[:, cols], wl[cols, :])
        bytes_wait(gr.at[part, cols], right_sem.at[i])
        b = b + dot(gr[:, cols], wr[cols, :])
        return a, b

    zero = jnp.zeros((ROWS, RANK), F32)
    left, right = lax.fori_loop(0, chunks, proj_chunk, (zero, zero))
    proj = to_x(left, right, pxl, pxr, 0).astype(BF16).astype(F32)
    bytes_wait(xr, rsem.at[4])

    s = reduce_x(proj, 0)
    inv = gram_all(s, 0)
    basis = jnp.dot(inv, s, precision=HIGH, preferred_element_type=F32).astype(BF16)
    bta[y, z] = basis[:rh]
    btb[z, y] = basis[rh:]

    def first_b(d):
        c, b = add(z, d, N), add(y, d, N)
        remote(
            bta.at[y, z], bta.at[y, z], line_send.at[2, 0], line_recv.at[2, 0], dev(x, y, c, k)
        ).start()
        remote(
            btb.at[z, y], btb.at[z, y], line_send.at[2, 1], line_recv.at[2, 1], dev(x, b, z, k)
        ).start()

    loop(1, N, first_b)
    bytes_wait(bta.at[y, part3], line_recv.at[2, 0])

    def then_a(d):
        remote(
            bta.at[y], bta.at[y], line_send.at[2, 2], line_recv.at[2, 2], dev(x, add(y, d, N), z, k)
        ).start()

    loop(1, N, then_a)
    bytes_wait(btb.at[z, part3], line_recv.at[2, 1])

    def then_b(d):
        remote(
            btb.at[z], btb.at[z], line_send.at[2, 3], line_recv.at[2, 3], dev(x, y, add(z, d, N), k)
        ).start()

    loop(1, N, then_b)
    later(bta.at[0, part3], line_send.at[2, 0])
    later(btb.at[0, part3], line_send.at[2, 1])
    later(bta.at[part3], line_send.at[2, 2])
    later(btb.at[part3], line_send.at[2, 3])
    bytes_wait(bta.at[part3], line_recv.at[2, 2])
    bytes_wait(btb.at[part3], line_recv.at[2, 3])

    def w_step(t, acc):
        b, c = lax.div(t, N), lax.rem(t, N)
        both = jnp.concatenate([bta[b, c], btb[c, b]], axis=0)
        return acc + dot_t(xr[:, x_cols(b, c)], both)

    weights = lax.fori_loop(0, TOK, w_step, jnp.zeros((ROWS, RANK), F32))
    ws[...] = weights.astype(BF16)

    def go_w(d):
        a = add(x, d, N)
        remote(
            ws.at[piece(a), :], wgl.at[piece(y), :], ssem.at[11], rsem.at[11],
            dev(a, left_y(a, x), z, k),
        ).start()
        remote(
            ws.at[piece(a), :], wgr.at[piece(z), :], ssem.at[12], rsem.at[12],
            dev(a, y, right_z(a, x), k),
        ).start()

    loop(1, N, go_w)
    later(ws.at[pl.ds(0, 3 * PIECE), :], ssem.at[11])
    later(ws.at[pl.ds(0, 3 * PIECE), :], ssem.at[12])
    later(ws.at[piece(0), :], selfsem.at[16], jnp.logical_not(swap_l))
    later(ws.at[piece(0), :], selfsem.at[17], jnp.logical_not(swap_r))

    @pl.when(swap_l)
    def _():
        pltpu.make_async_copy(ws.at[piece(x), :], wgl.at[piece(y), :], rsem.at[11]).start()

    @pl.when(jnp.logical_not(swap_l))
    def _():
        remote(
            ws.at[piece(x), :], wgl.at[piece(y), :], selfsem.at[16], rsem.at[11],
            dev(x, left_y(x, x), z, k),
        ).start()

    @pl.when(swap_r)
    def _():
        pltpu.make_async_copy(ws.at[piece(x), :], wgr.at[piece(z), :], rsem.at[12]).start()

    @pl.when(jnp.logical_not(swap_r))
    def _():
        remote(
            ws.at[piece(x), :], wgr.at[piece(z), :], selfsem.at[17], rsem.at[12],
            dev(x, y, right_z(x, x), k),
        ).start()

    bytes_wait(wgl, rsem.at[11])
    bytes_wait(wgr, rsem.at[12])

    wlt = wgl[...].astype(F32).T.astype(BF16)
    wrt = wgr[...].astype(F32).T.astype(BF16)

    def cols_of(b, c):
        return pl.ds(pl.multiple_of((b * N + c) * hc, 128), hc)

    def power_group(d):
        g = add(z, d, N)

        def left_one(b):
            pwl[g, b] = dot(wlt, gl[:, cols_of(b, g)]).astype(BF16)

        loop(0, N, left_one)

        @pl.when(d < N)
        def _():
            remote(pwl.at[g], rl1.at[z], ssem.at[13], rsem.at[13], dev(x, y, g, k)).start()

        g2 = add(y, d, N)

        def right_one(c):
            pwr[g2, c] = dot(wrt, gr[:, cols_of(g2, c)]).astype(BF16)

        loop(0, N, right_one)

        @pl.when(d < N)
        def _():
            remote(pwr.at[g2], rr1.at[y], ssem.at[14], rsem.at[14], dev(x, g2, z, k)).start()

    loop(1, N + 1, power_group)
    later(rl1.at[part3], ssem.at[13])
    later(rr1.at[part3], ssem.at[14])
    bytes_wait(rl1.at[part3], rsem.at[13])

    def stage2_left(i):
        b = add(y, i, N)
        mid_l[b] = sum_along(pwl, rl1, z, b).astype(BF16)

        @pl.when(jnp.logical_or(i < N, jnp.logical_not(swap_l)))
        def _():
            remote(
                mid_l.at[b], rl2.at[x], selfsem.at[i], rsem.at[20], dev(xl, b, z, k)
            ).start()

    def stage2_right(i):
        c = add(z, i, N)
        mid_r[c] = sum_along(pwr, rr1, y, c).astype(BF16)

        @pl.when(jnp.logical_or(i < N, jnp.logical_not(swap_r)))
        def _():
            remote(
                mid_r.at[c], rr2.at[x], selfsem.at[N + 1 + i], rsem.at[21], dev(xd, y, c, k)
            ).start()

    loop(1, N + 1, stage2_left)
    for i in range(1, N):
        later(mid_l.at[0], selfsem.at[i])
    later(mid_l.at[0], selfsem.at[N], jnp.logical_not(swap_l))

    @pl.when(swap_l)
    def _():
        pltpu.make_async_copy(mid_l.at[y], rl2.at[x], rsem.at[20]).start()

    bytes_wait(rr1.at[part3], rsem.at[14])
    loop(1, N + 1, stage2_right)
    for i in range(1, N):
        later(mid_r.at[0], selfsem.at[N + 1 + i])
    later(mid_r.at[0], selfsem.at[2 * N + 1], jnp.logical_not(swap_r))

    @pl.when(swap_r)
    def _():
        pltpu.make_async_copy(mid_r.at[z], rr2.at[x], rsem.at[21]).start()

    bytes_wait(rl2, rsem.at[20])
    bytes_wait(rr2, rsem.at[21])
    zero = jnp.zeros((RANK, hc), F32)
    sl = lax.fori_loop(0, N, lambda i, c: c + rl2[i].astype(F32), zero)
    sr = lax.fori_loop(0, N, lambda i, c: c + rr2[i].astype(F32), zero)
    s2 = jnp.concatenate([sl, sr], axis=1)
    inv = gram_all(s2, 1)
    right_basis = jnp.dot(inv, s2, precision=HIGH, preferred_element_type=F32).astype(BF16)

    own_rl[...] = right_basis[:, :hc]
    own_rr[...] = right_basis[:, hc:]

    def send_r(d):
        a = add(x, d, N)
        remote(
            own_rl, rbl.at[z, y], ssem.at[15], rsem.at[15], dev(a, left_y(a, x), z, k)
        ).start()
        remote(
            own_rr, rbr.at[y, z], ssem.at[16], rsem.at[16], dev(a, y, right_z(a, x), k)
        ).start()

    loop(1, N, send_r)
    later(rl2.at[part3], ssem.at[15])
    later(rr2.at[part3], ssem.at[16])
    later(own_rl, selfsem.at[10], jnp.logical_not(swap_l))
    later(own_rr, selfsem.at[11], jnp.logical_not(swap_r))

    @pl.when(swap_l)
    def _():
        pltpu.make_async_copy(own_rl, rbl.at[z, y], rsem.at[15]).start()

    @pl.when(jnp.logical_not(swap_l))
    def _():
        remote(own_rl, rbl.at[z, y], selfsem.at[10], rsem.at[15], dev(x, 0, z, k)).start()

    @pl.when(swap_r)
    def _():
        pltpu.make_async_copy(own_rr, rbr.at[y, z], rsem.at[16]).start()

    @pl.when(jnp.logical_not(swap_r))
    def _():
        remote(own_rr, rbr.at[y, z], selfsem.at[11], rsem.at[16], dev(x, y, 0, k)).start()

    bytes_wait(rbl.at[z], rsem.at[15])

    def share_l(d):
        remote(
            rbl.at[z], rbl.at[z], ssem.at[22], share_recv.at[0, d], dev(x, y, add(z, d, N), k)
        ).start()

    loop(1, N, share_l)
    later(rbl.at[part3], ssem.at[22])
    bytes_wait(rbr.at[y], rsem.at[16])

    def share_r(d):
        remote(
            rbr.at[y], rbr.at[y], ssem.at[23], share_recv.at[1, d], dev(x, add(y, d, N), z, k)
        ).start()

    loop(1, N, share_r)
    later(rbr.at[part3], ssem.at[23])

    def left_group(g, acc):
        return lax.fori_loop(
            0, N, lambda b, t: t + dot_t(gl[:, cols_of(b, g)], rbl[g, b]), acc
        )

    def right_group(g, acc):
        return lax.fori_loop(
            0, N, lambda c, t: t + dot_t(gr[:, cols_of(g, c)], rbr[g, c]), acc
        )

    zero = jnp.zeros((ROWS, RANK), F32)
    left = left_group(z, zero)
    right = right_group(y, zero)

    def next_groups(d, acc):
        a, b = acc
        g = add(z, N - d, N)
        bytes_wait(rbl.at[g], share_recv.at[0, d])
        a = left_group(g, a)
        g = add(y, N - d, N)
        bytes_wait(rbr.at[g], share_recv.at[1, d])
        b = right_group(g, b)
        return a, b

    left, right = lax.fori_loop(1, N, next_groups, (left, right))
    second = to_x(left, right, pxl2, pxr2, 1).astype(BF16).astype(F32)

    s3 = reduce_x(second, 1)
    inv = gram_all(s3, 2)
    last = jnp.dot(inv, s3, precision=HIGH, preferred_element_type=F32)
    out[0] = last.T * scale

    for drain in pending:
        drain()


def owners(row_ids, col_ids, grads, acts, om):
    toks, top, hidden = grads.shape
    width = acts.shape[1]
    half = hidden // 2
    wc, hc = width // TOK, half // TOK
    chunk = half // 8
    rh = RANK // 2

    def vm(*shape, dtype=BF16):
        return pltpu.VMEM(shape, dtype)

    any_spec = pl.BlockSpec(memory_space=pl.ANY)
    return pl.pallas_call(
        functools.partial(body, float(width) ** 0.5),
        out_shape=jax.ShapeDtypeStruct((1, wc, RANK), F32),
        in_specs=[pl.BlockSpec(memory_space=pltpu.VMEM)] * 2 + [any_spec] * 3,
        out_specs=pl.BlockSpec(memory_space=pltpu.VMEM),
        scratch_shapes=[
            vm(ROWS, toks * top), vm(ROWS, toks), vm(2, 2, toks, top, chunk), vm(toks, width),
            vm(2, 2, ROWS, chunk), vm(ROWS, width),
            vm(ROWS, width), vm(ROWS, half), vm(ROWS, half), vm(half, RANK), vm(half, RANK),
            vm(2, ROWS, RANK), vm(2, ROWS, RANK),
            vm(ROWS, RANK), vm(ROWS, RANK), vm(ROWS, RANK), vm(ROWS, RANK),
            vm(N, N, rh, wc), vm(N, N, rh, wc), vm(2, N, N, rh, wc), vm(2, N, N, rh, wc),
            vm(N, rh, wc), vm(N, rh, wc), vm(2, N, rh, wc), vm(2, N, rh, wc),
            vm(N, N, rh, wc), vm(N, N, rh, wc),
            vm(ROWS, RANK), vm(ROWS, RANK), vm(ROWS, RANK),
            vm(N, N, RANK, hc), vm(N, N, RANK, hc), vm(N, N, RANK, hc), vm(N, N, RANK, hc),
            vm(N, RANK, hc), vm(N, RANK, hc), vm(N, RANK, hc), vm(N, RANK, hc),
            vm(RANK, hc), vm(RANK, hc), vm(N, N, RANK, hc), vm(N, N, RANK, hc),
            vm(3, RANK, RANK), vm(3, TOK, RANK, RANK),
            vm(RANK, RANK, dtype=F32), vm(RANK, RANK, dtype=F32),
            pltpu.SemaphoreType.DMA((24,)),
            pltpu.SemaphoreType.DMA((24,)),
            pltpu.SemaphoreType.DMA((6,)),
            pltpu.SemaphoreType.DMA((18,)),
            pltpu.SemaphoreType.DMA((3, 2)),
            pltpu.SemaphoreType.DMA((2, 2)),
            pltpu.SemaphoreType.DMA((8,)),
            pltpu.SemaphoreType.DMA((8,)),
            pltpu.SemaphoreType.DMA((3, 4)),
            pltpu.SemaphoreType.DMA((3, 4)),
            pltpu.SemaphoreType.DMA((2, N)),
        ],
        compiler_params=pltpu.CompilerParams(
            collective_id=0, has_side_effects=True, vmem_limit_bytes=60 * 1024 * 1024
        ),
        name="owners",
    )(row_ids, col_ids, grads, acts, om)


def shards(activations, expert_ids, out_grads, sketch_matrix):
    ids = expert_ids.reshape(1, -1)
    om = sketch_matrix.reshape(sketch_matrix.shape[1:])
    return owners(ids, ids.reshape(-1, 1), out_grads, activations, om)


def solution(mesh):
    return jax.shard_map(
        shards,
        mesh=mesh,
        in_specs=(
            P(("tok", "exp"), None),
            P(("tok", "exp"), None),
            P(("tok", "exp"), None, None),
            P("exp", None, None),
        ),
        out_specs=P("exp", "tok", None),
        check_vma=False,
    )
```

```python
import functools

import jax
import jax.numpy as jnp
from jax import lax
from jax.experimental import pallas as pl
from jax.experimental.pallas import tpu as pltpu
from jax.sharding import PartitionSpec as P

MESH = pl.DeviceIdType.MESH
HIGH = lax.Precision.HIGHEST
F32 = jnp.float32
BF16 = jnp.bfloat16

N = 4
TOK = N * N
EXP = 2 * N
CAP = 48
ROWS = EXP * CAP
PIECE = 2 * CAP
RANK = 128
PANEL = 16


def dot(a, b):
    return jnp.dot(a, b, preferred_element_type=F32)


def dot_t(a, b, precision=None):
    return lax.dot_general(
        a, b, (((1,), (1,)), ((), ())), precision=precision, preferred_element_type=F32
    )


def picks(row_ids, col_ids, pick, pick_x):
    pairs = row_ids.shape[1]
    toks = pick_x.shape[1]
    top = pairs // toks
    ids = row_ids[...]
    same = (col_ids[...] == ids) & (
        lax.broadcasted_iota(jnp.int32, (pairs, pairs), 0)
        < lax.broadcasted_iota(jnp.int32, (pairs, pairs), 1)
    )
    rank = jnp.sum(same.astype(F32), axis=0, keepdims=True).astype(jnp.int32)
    slot = ids * CAP + rank
    hot = lax.broadcasted_iota(jnp.int32, (ROWS, pairs), 0) == slot
    pick[...] = hot.astype(F32).astype(BF16)
    token = lax.broadcasted_iota(jnp.int32, (pairs, toks), 0) - top * lax.broadcasted_iota(
        jnp.int32, (pairs, toks), 1
    )
    of_token = ((token >= 0) & (token < top)).astype(F32).astype(BF16)
    pick_x[...] = dot(pick[...], of_token).astype(BF16)


def bytes_wait(ref, sem):
    pltpu.make_async_copy(ref, ref, sem).wait()


def inverse_factor(c, cm, mm):
    cm[...] = c
    rows = lax.broadcasted_iota(jnp.int32, (RANK, RANK), 0)
    cols = lax.broadcasted_iota(jnp.int32, (RANK, RANK), 1)
    mm[...] = (rows == cols).astype(F32)
    prow = lax.broadcasted_iota(jnp.int32, (PANEL, RANK), 0)
    pcol = lax.broadcasted_iota(jnp.int32, (PANEL, RANK), 1)

    def panel(p, carry):
        base = pl.multiple_of(p * PANEL, PANEL)
        a = cm[pl.ds(base, PANEL), :]
        m = mm[pl.ds(base, PANEL), :]
        near = pltpu.roll(a, lax.rem(RANK - base, RANK), 1)
        block = [jnp.broadcast_to(near[:, i : i + 1], (PANEL, RANK)) for i in range(PANEL)]
        for i in range(PANEL):
            r = lax.rsqrt(block[i][i : i + 1, :])
            mult = jnp.where(prow > i, block[i] * (r * r), 0.0)
            for j in range(i + 1, PANEL):
                block[j] = block[j] - mult * block[j][i : i + 1, :]
            a = jnp.where(prow == i, a * r, a - mult * a[i : i + 1, :])
            m = jnp.where(prow == i, m * r, m - mult * m[i : i + 1, :])
        mm[pl.ds(base, PANEL), :] = m
        left = jnp.where(pcol >= base + PANEL, a, 0.0)
        both = jnp.concatenate([a, m], axis=1)
        change = lax.dot_general(
            left, both, (((0,), (0,)), ((), ())), precision=HIGH, preferred_element_type=F32
        )
        cm[...] -= change[:, :RANK]
        mm[...] -= change[:, RANK:]
        return carry

    lax.fori_loop(0, RANK // PANEL, panel, 0)
    return mm[...]


def body(
    scale,
    row_ids, col_ids, grads, acts, om,
    out,
    pick, pick_x, g_in, x_in, gs, xs,
    xr, gl, gr, wl, wr,
    nls, nrs, pxl, pxr, pxl2, pxr2,
    spa, spb, ra1, rb1, mid_a, mid_b, ra2, rb2, bta, btb,
    ws, wgl, wgr,
    pwl, pwr, rl1, rr1, mid_l, mid_r, rl2, rr2, own_rl, own_rr, rbl, rbr,
    gm, gb, cm, mm,
    ssem, rsem, gsem, selfsem, in_sem, slot_sem, left_sem, right_sem,
    line_send, line_recv, share_recv,
):
    tok = lax.axis_index("tok")
    ex = lax.axis_index("exp")
    y, z = lax.div(tok, N), lax.rem(tok, N)
    x, k = lax.div(ex, 2), lax.rem(ex, 2)
    half = gl.shape[1]
    width = xr.shape[1]
    wc = width // TOK
    hc = half // TOK

    def dev(a, b, c, core):
        return (b * N + c, a * 2 + core)

    def add(a, b, n):
        return lax.rem(a + b, n)

    def remote(src, dst, s, r, where):
        return pltpu.make_async_remote_copy(
            src_ref=src, dst_ref=dst, send_sem=s, recv_sem=r, device_id=where, device_id_type=MESH
        )

    def loop(lo, hi, fn):
        lax.fori_loop(lo, hi, lambda i, c: (fn(i), c)[1], 0)

    pending = []

    def later(ref, sem, when=None):
        if when is None:
            pending.append(lambda: bytes_wait(ref, sem))
        else:
            pending.append(lambda: pl.when(when)(lambda: bytes_wait(ref, sem)))

    chunk = gs.shape[3]
    chunks = half // chunk
    pairs = pick.shape[1]

    def load(side, i):
        cols = pl.ds(pl.multiple_of(side * half + i * chunk, chunk), chunk)
        slot = lax.rem(i, 2)
        return pltpu.make_async_copy(
            grads.at[:, :, cols], g_in.at[side, slot], in_sem.at[side, slot]
        )

    x_load = pltpu.make_async_copy(acts, x_in, in_sem.at[2, 0])
    for i in range(2):
        load(0, i).start()
        load(1, i).start()
    x_load.start()

    barrier = pltpu.get_barrier_semaphore()

    def greet(where):
        pl.semaphore_signal(barrier, inc=1, device_id=where, device_id_type=MESH)

    chip = x * TOK + tok

    def same_core(d):
        c = add(chip, d, N * TOK)
        greet((lax.rem(c, TOK), lax.div(c, TOK) * 2 + k))

    loop(1, N * TOK, same_core)

    def other_core(d):
        greet(dev(add(x, d, N), y, z, 1 - k))

    loop(0, N, other_core)

    def other_core_y(d):
        greet(dev(x, add(y, d, N), z, 1 - k))
        greet(dev(x, y, add(z, d, N), 1 - k))

    loop(1, N, other_core_y)
    picks(row_ids, col_ids, pick, pick_x)
    part = pl.ds(0, ROWS - CAP)

    def sort_side(i, side, first):
        slot = lax.rem(i, 2)
        load(side, i).wait()
        if not first:
            bytes_wait(gs.at[side, slot, part, :], slot_sem.at[side, slot])
        block = g_in[side, slot].reshape(pairs, chunk)
        gs[side, slot] = dot(pick[...], block).astype(BF16)

        @pl.when(i + 2 < chunks)
        def _():
            load(side, i + 2).start()

    sort_side(0, 0, True)
    sort_side(0, 1, True)
    pl.semaphore_wait(barrier, N * TOK - 1 + N + 2 * (N - 1))

    shift_r = lax.rem(N - z, N)
    swap_l = y == 0
    swap_r = z == 0
    xl = add(x, y, N)
    xd = add(x, shift_r, N)
    own_el, own_er = xl * 2 + k, xd * 2 + k

    def left_y(at_x, to_x):
        return lax.rem(to_x - at_x + N, N)

    def right_z(at_x, to_x):
        return lax.rem(at_x - to_x + N, N)

    quarter = half // N

    def om_rows(i):
        return pl.ds(pl.multiple_of(i * quarter, quarter), quarter)

    def om_right_rows(i):
        return pl.ds(pl.multiple_of(half + i * quarter, quarter), quarter)

    def om_left():
        return remote(
            om.at[om_rows(z), :], wl.at[om_rows(z), :], ssem.at[0], rsem.at[0],
            dev(add(x, N - y, N), y, z, k),
        )

    def om_right():
        return remote(
            om.at[om_right_rows(y), :], wr.at[om_rows(y), :], ssem.at[1], rsem.at[1],
            dev(add(x, z, N), y, z, k),
        )

    @pl.when(swap_l)
    def _():
        pltpu.make_async_copy(om.at[om_rows(z), :], wl.at[om_rows(z), :], rsem.at[0]).start()

    @pl.when(jnp.logical_not(swap_l))
    def _():
        om_left().start()

    @pl.when(swap_r)
    def _():
        pltpu.make_async_copy(om.at[om_right_rows(y), :], wr.at[om_rows(y), :], rsem.at[1]).start()

    @pl.when(jnp.logical_not(swap_r))
    def _():
        om_right().start()

    later(wl.at[om_rows(0), :], ssem.at[0], jnp.logical_not(swap_l))
    later(wr.at[om_rows(0), :], ssem.at[1], jnp.logical_not(swap_r))

    el, er = y * 2 + k, z * 2 + k

    def rows_of(e):
        return pl.ds(pl.multiple_of(e * CAP, CAP), CAP)

    def send_side(i, side):
        slot = lax.rem(i, 2)
        cols = pl.ds(pl.multiple_of(i * chunk, chunk), chunk)
        dst, own, here, sems = (
            (gl, own_el, el, left_sem) if side == 0 else (gr, own_er, er, right_sem)
        )

        def send_g(d):
            e = add(own, d, EXP)
            to, core = lax.div(e, 2), lax.rem(e, 2)
            if side == 0:
                where = dev(x, left_y(x, to), z, core)
            else:
                where = dev(x, y, right_z(x, to), core)
            remote(
                gs.at[side, slot, rows_of(e), :], dst.at[rows_of(here), cols],
                slot_sem.at[side, slot], sems.at[i], where,
            ).start()

        loop(1, EXP, send_g)
        dst[rows_of(here), cols] = gs[side, slot, rows_of(own), :]

    def send_chunk(i, first):
        for side in range(2):
            sort_side(i, side, first)
            send_side(i, side)

    send_side(0, 0)
    send_side(0, 1)

    x_load.wait()

    def sort_x(t):
        cols = pl.ds(pl.multiple_of(t * wc, 128), wc)
        xs[:, cols] = dot(pick_x[...], x_in[:, cols]).astype(BF16)

    loop(0, TOK, sort_x)

    def send_x(d):
        e = add(ex, d, EXP)
        remote(
            xs.at[rows_of(e), :], xr.at[rows_of(ex), :], ssem.at[4], rsem.at[4], (tok, e)
        ).start()

    loop(1, EXP, send_x)
    later(xr.at[part, :], ssem.at[4])
    pltpu.make_async_copy(xs.at[rows_of(ex), :], xr.at[rows_of(ex), :], rsem.at[4]).start()

    send_chunk(1, True)
    bytes_wait(wl.at[om_rows(z), :], rsem.at[0])
    bytes_wait(wr.at[om_rows(y), :], rsem.at[1])

    def om_share(d):
        remote(
            wl.at[om_rows(z), :], wl.at[om_rows(z), :], ssem.at[18], rsem.at[18],
            dev(x, y, add(z, d, N), k),
        ).start()
        remote(
            wr.at[om_rows(y), :], wr.at[om_rows(y), :], ssem.at[19], rsem.at[19],
            dev(x, add(y, d, N), z, k),
        ).start()

    loop(1, N, om_share)
    most = pl.ds(0, 3 * quarter)
    later(wl.at[most, :], ssem.at[18])
    later(wr.at[most, :], ssem.at[19])

    loop(2, chunks, lambda i: send_chunk(i, False))
    for slot in range(2):
        later(gs.at[0, slot, part, :], slot_sem.at[0, slot])
        later(gs.at[1, slot, part, :], slot_sem.at[1, slot])

    def piece(i):
        return pl.ds(pl.multiple_of(i * PIECE, PIECE), PIECE)

    def to_x(left, right, dl, dr, phase):
        nls[phase] = left.astype(BF16)
        nrs[phase] = right.astype(BF16)
        sl, sr = ssem.at[5 + 2 * phase], ssem.at[6 + 2 * phase]
        rl_, rr_ = rsem.at[5 + 2 * phase], rsem.at[6 + 2 * phase]

        def go_l(d):
            b = add(y, d, N)
            remote(nls.at[phase, piece(b), :], dl.at[piece(x), :], sl, rl_, dev(xl, b, z, k)).start()

        def go_r(d):
            c = add(z, d, N)
            remote(nrs.at[phase, piece(c), :], dr.at[piece(x), :], sr, rr_, dev(xd, y, c, k)).start()

        loop(1, N, go_l)
        loop(1, N, go_r)
        own_l = selfsem.at[12 + 2 * phase]
        own_r = selfsem.at[13 + 2 * phase]

        @pl.when(swap_l)
        def _():
            pltpu.make_async_copy(nls.at[phase, piece(y), :], dl.at[piece(x), :], rl_).start()

        @pl.when(jnp.logical_not(swap_l))
        def _():
            remote(
                nls.at[phase, piece(y), :], dl.at[piece(x), :], own_l, rl_, dev(xl, y, z, k)
            ).start()

        @pl.when(swap_r)
        def _():
            pltpu.make_async_copy(nrs.at[phase, piece(z), :], dr.at[piece(x), :], rr_).start()

        @pl.when(jnp.logical_not(swap_r))
        def _():
            remote(
                nrs.at[phase, piece(z), :], dr.at[piece(x), :], own_r, rr_, dev(xd, y, z, k)
            ).start()

        bytes_wait(dl, rl_)
        bytes_wait(dr, rr_)
        total = dl[...].astype(F32) + dr[...].astype(F32)
        three = nls.at[phase, pl.ds(0, 3 * PIECE), :]
        bytes_wait(three, sl)
        bytes_wait(nrs.at[phase, pl.ds(0, 3 * PIECE), :], sr)

        @pl.when(jnp.logical_not(swap_l))
        def _():
            bytes_wait(nls.at[phase, pl.ds(0, PIECE), :], own_l)

        @pl.when(jnp.logical_not(swap_r))
        def _():
            bytes_wait(nrs.at[phase, pl.ds(0, PIECE), :], own_r)

        return total

    def gram_all(s, phase):
        gm[phase] = dot_t(s, s, HIGH).astype(BF16)
        pltpu.make_async_copy(gm.at[phase], gb.at[phase, tok], gsem.at[2 * phase]).start()

        def go(d):
            t = add(tok, d, TOK)
            remote(
                gm.at[phase], gb.at[phase, tok], gsem.at[2 * phase + 1], gsem.at[2 * phase], (t, ex)
            ).start()

        loop(1, TOK, go)
        bytes_wait(gb.at[phase], gsem.at[2 * phase])
        c = lax.fori_loop(
            0, TOK, lambda i, c: c + gb[phase, i].astype(F32), jnp.zeros((RANK, RANK), F32)
        )
        bytes_wait(gb.at[phase, pl.ds(0, TOK - 1)], gsem.at[2 * phase + 1])
        return inverse_factor(c, cm, mm)

    part3 = pl.ds(0, N - 1)

    def sum_along(own, got, me, cols):
        total = own[me, :, cols].astype(F32)
        for i in range(1, N):
            total = total + got[add(me, i, N), :, cols].astype(F32)
        return total

    def sum_last(own, got, me):
        def term(i, acc):
            return acc + got[add(me, i, N)].astype(F32)

        return lax.fori_loop(1, N, term, own[me].astype(F32))

    def span(i, n):
        return pl.ds(pl.multiple_of(i * n, 128), n)

    wg, hg = N * wc, N * hc

    rh = RANK // 2

    def reduce_x(p, phase):
        pt = p.T.astype(BF16)
        s, r = line_send.at[phase], line_recv.at[phase]
        ra, rb = ra1.at[phase], rb1.at[phase]
        ra_last, rb_last = ra2.at[phase], rb2.at[phase]

        def group(d):
            b = add(y, d, N)
            v = dot(pt, xr[:, span(b, wg)]).astype(BF16)
            spa[b] = v[:rh]
            for c in range(N):
                spb[c, :, span(b, wc)] = v[rh:, c * wc : (c + 1) * wc]

            @pl.when(d < N)
            def _():
                remote(spa.at[b], ra.at[y], s.at[0], r.at[0], dev(x, b, z, k)).start()

        loop(1, N + 1, group)

        def send_b(d):
            c = add(z, d, N)
            remote(spb.at[c], rb.at[z], s.at[1], r.at[1], dev(x, y, c, k)).start()

        loop(1, N, send_b)
        bytes_wait(ra.at[part3], r.at[0])

        def second_a(d):
            c = add(z, d, N)
            mid_a[c] = sum_along(spa, ra, y, span(c, wc)).astype(BF16)

            @pl.when(d < N)
            def _():
                remote(mid_a.at[c], ra_last.at[z], s.at[2], r.at[2], dev(x, y, c, k)).start()

        loop(1, N + 1, second_a)
        bytes_wait(rb.at[part3], r.at[1])

        def second_b(d):
            b = add(y, d, N)
            mid_b[b] = sum_along(spb, rb, z, span(b, wc)).astype(BF16)

            @pl.when(d < N)
            def _():
                remote(mid_b.at[b], rb_last.at[y], s.at[3], r.at[3], dev(x, b, z, k)).start()

        loop(1, N + 1, second_b)
        bytes_wait(ra_last.at[part3], r.at[2])
        top = sum_last(mid_a, ra_last, z)
        bytes_wait(rb_last.at[part3], r.at[3])
        low = sum_last(mid_b, rb_last, y)
        bytes_wait(spa.at[part3], s.at[0])
        bytes_wait(spb.at[part3], s.at[1])
        bytes_wait(mid_a.at[part3], s.at[2])
        bytes_wait(mid_b.at[part3], s.at[3])
        return jnp.concatenate([top, low], axis=0)

    bytes_wait(wl.at[most, :], rsem.at[18])
    bytes_wait(wr.at[most, :], rsem.at[19])

    def proj_chunk(i, acc):
        cols = pl.ds(pl.multiple_of(i * chunk, chunk), chunk)
        a, b = acc
        bytes_wait(gl.at[part, cols], left_sem.at[i])
        a = a + dot(gl[:, cols], wl[cols, :])
        bytes_wait(gr.at[part, cols], right_sem.at[i])
        b = b + dot(gr[:, cols], wr[cols, :])
        return a, b

    zero = jnp.zeros((ROWS, RANK), F32)
    left, right = lax.fori_loop(0, chunks, proj_chunk, (zero, zero))
    proj = to_x(left, right, pxl, pxr, 0).astype(BF16).astype(F32)
    bytes_wait(xr, rsem.at[4])

    s = reduce_x(proj, 0)
    inv = gram_all(s, 0)
    basis = jnp.dot(inv, s, precision=HIGH, preferred_element_type=F32).astype(BF16)
    bta[y, :, span(z, wc)] = basis[:rh]
    btb[z, :, span(y, wc)] = basis[rh:]
    own_a, own_b = bta.at[y, :, span(z, wc)], btb.at[z, :, span(y, wc)]
    three = pl.ds(0, (N - 1) * wc)

    def first_b(d):
        c, b = add(z, d, N), add(y, d, N)
        remote(
            own_a, own_a, line_send.at[2, 0], line_recv.at[2, 0], dev(x, y, c, k)
        ).start()
        remote(
            own_b, own_b, line_send.at[2, 1], line_recv.at[2, 1], dev(x, b, z, k)
        ).start()

    loop(1, N, first_b)
    bytes_wait(bta.at[y, :, three], line_recv.at[2, 0])

    def then_a(d):
        remote(
            bta.at[y], bta.at[y], line_send.at[2, 2], line_recv.at[2, 2], dev(x, add(y, d, N), z, k)
        ).start()

    loop(1, N, then_a)
    bytes_wait(btb.at[z, :, three], line_recv.at[2, 1])

    def then_b(d):
        remote(
            btb.at[z], btb.at[z], line_send.at[2, 3], line_recv.at[2, 3], dev(x, y, add(z, d, N), k)
        ).start()

    loop(1, N, then_b)
    later(bta.at[0, :, three], line_send.at[2, 0])
    later(btb.at[0, :, three], line_send.at[2, 1])
    later(bta.at[part3], line_send.at[2, 2])
    later(btb.at[part3], line_send.at[2, 3])
    bytes_wait(bta.at[part3], line_recv.at[2, 2])
    bytes_wait(btb.at[part3], line_recv.at[2, 3])

    def w_step(b, acc):
        low = jnp.concatenate([btb[c, :, span(b, wc)] for c in range(N)], axis=1)
        both = jnp.concatenate([bta[b], low], axis=0)
        return acc + dot_t(xr[:, span(b, wg)], both)

    weights = lax.fori_loop(0, N, w_step, jnp.zeros((ROWS, RANK), F32))
    ws[...] = weights.astype(BF16)

    def go_w(d):
        a = add(x, d, N)
        remote(
            ws.at[piece(a), :], wgl.at[piece(y), :], ssem.at[11], rsem.at[11],
            dev(a, left_y(a, x), z, k),
        ).start()
        remote(
            ws.at[piece(a), :], wgr.at[piece(z), :], ssem.at[12], rsem.at[12],
            dev(a, y, right_z(a, x), k),
        ).start()

    loop(1, N, go_w)
    later(ws.at[pl.ds(0, 3 * PIECE), :], ssem.at[11])
    later(ws.at[pl.ds(0, 3 * PIECE), :], ssem.at[12])
    later(ws.at[piece(0), :], selfsem.at[16], jnp.logical_not(swap_l))
    later(ws.at[piece(0), :], selfsem.at[17], jnp.logical_not(swap_r))

    @pl.when(swap_l)
    def _():
        pltpu.make_async_copy(ws.at[piece(x), :], wgl.at[piece(y), :], rsem.at[11]).start()

    @pl.when(jnp.logical_not(swap_l))
    def _():
        remote(
            ws.at[piece(x), :], wgl.at[piece(y), :], selfsem.at[16], rsem.at[11],
            dev(x, left_y(x, x), z, k),
        ).start()

    @pl.when(swap_r)
    def _():
        pltpu.make_async_copy(ws.at[piece(x), :], wgr.at[piece(z), :], rsem.at[12]).start()

    @pl.when(jnp.logical_not(swap_r))
    def _():
        remote(
            ws.at[piece(x), :], wgr.at[piece(z), :], selfsem.at[17], rsem.at[12],
            dev(x, y, right_z(x, x), k),
        ).start()

    bytes_wait(wgl, rsem.at[11])
    bytes_wait(wgr, rsem.at[12])

    wlt = wgl[...].astype(F32).T.astype(BF16)
    wrt = wgr[...].astype(F32).T.astype(BF16)

    def power_group(d):
        g = add(z, d, N)
        pwl[g] = dot(wlt, gl[:, span(g, hg)]).astype(BF16)

        @pl.when(d < N)
        def _():
            remote(pwl.at[g], rl1.at[z], ssem.at[13], rsem.at[13], dev(x, y, g, k)).start()

        g2 = add(y, d, N)
        pwr[g2] = dot(wrt, gr[:, span(g2, hg)]).astype(BF16)

        @pl.when(d < N)
        def _():
            remote(pwr.at[g2], rr1.at[y], ssem.at[14], rsem.at[14], dev(x, g2, z, k)).start()

    loop(1, N + 1, power_group)
    later(rl1.at[part3], ssem.at[13])
    later(rr1.at[part3], ssem.at[14])
    bytes_wait(rl1.at[part3], rsem.at[13])

    def stage2_left(i):
        b = add(y, i, N)
        mid_l[b] = sum_along(pwl, rl1, z, span(b, hc)).astype(BF16)

        @pl.when(jnp.logical_or(i < N, jnp.logical_not(swap_l)))
        def _():
            remote(
                mid_l.at[b], rl2.at[x], selfsem.at[i], rsem.at[20], dev(xl, b, z, k)
            ).start()

    def stage2_right(i):
        c = add(z, i, N)
        mid_r[c] = sum_along(pwr, rr1, y, span(c, hc)).astype(BF16)

        @pl.when(jnp.logical_or(i < N, jnp.logical_not(swap_r)))
        def _():
            remote(
                mid_r.at[c], rr2.at[x], selfsem.at[N + 1 + i], rsem.at[21], dev(xd, y, c, k)
            ).start()

    loop(1, N + 1, stage2_left)
    for i in range(1, N):
        later(mid_l.at[0], selfsem.at[i])
    later(mid_l.at[0], selfsem.at[N], jnp.logical_not(swap_l))

    @pl.when(swap_l)
    def _():
        pltpu.make_async_copy(mid_l.at[y], rl2.at[x], rsem.at[20]).start()

    bytes_wait(rr1.at[part3], rsem.at[14])
    loop(1, N + 1, stage2_right)
    for i in range(1, N):
        later(mid_r.at[0], selfsem.at[N + 1 + i])
    later(mid_r.at[0], selfsem.at[2 * N + 1], jnp.logical_not(swap_r))

    @pl.when(swap_r)
    def _():
        pltpu.make_async_copy(mid_r.at[z], rr2.at[x], rsem.at[21]).start()

    bytes_wait(rl2, rsem.at[20])
    bytes_wait(rr2, rsem.at[21])
    zero = jnp.zeros((RANK, hc), F32)
    sl = lax.fori_loop(0, N, lambda i, c: c + rl2[i].astype(F32), zero)
    sr = lax.fori_loop(0, N, lambda i, c: c + rr2[i].astype(F32), zero)
    s2 = jnp.concatenate([sl, sr], axis=1)
    inv = gram_all(s2, 1)
    right_basis = jnp.dot(inv, s2, precision=HIGH, preferred_element_type=F32).astype(BF16)

    own_rl[...] = right_basis[:, :hc]
    own_rr[...] = right_basis[:, hc:]

    at_l, at_r = rbl.at[z, :, span(y, hc)], rbr.at[y, :, span(z, hc)]

    def send_r(d):
        a = add(x, d, N)
        remote(
            own_rl, at_l, ssem.at[15], rsem.at[15], dev(a, left_y(a, x), z, k)
        ).start()
        remote(
            own_rr, at_r, ssem.at[16], rsem.at[16], dev(a, y, right_z(a, x), k)
        ).start()

    loop(1, N, send_r)
    later(rl2.at[part3], ssem.at[15])
    later(rr2.at[part3], ssem.at[16])
    later(own_rl, selfsem.at[10], jnp.logical_not(swap_l))
    later(own_rr, selfsem.at[11], jnp.logical_not(swap_r))

    @pl.when(swap_l)
    def _():
        pltpu.make_async_copy(own_rl, at_l, rsem.at[15]).start()

    @pl.when(jnp.logical_not(swap_l))
    def _():
        remote(own_rl, at_l, selfsem.at[10], rsem.at[15], dev(x, 0, z, k)).start()

    @pl.when(swap_r)
    def _():
        pltpu.make_async_copy(own_rr, at_r, rsem.at[16]).start()

    @pl.when(jnp.logical_not(swap_r))
    def _():
        remote(own_rr, at_r, selfsem.at[11], rsem.at[16], dev(x, y, 0, k)).start()

    bytes_wait(rbl.at[z], rsem.at[15])

    def share_l(d):
        remote(
            rbl.at[z], rbl.at[z], ssem.at[22], share_recv.at[0, d], dev(x, y, add(z, d, N), k)
        ).start()

    loop(1, N, share_l)
    later(rbl.at[part3], ssem.at[22])
    bytes_wait(rbr.at[y], rsem.at[16])

    def share_r(d):
        remote(
            rbr.at[y], rbr.at[y], ssem.at[23], share_recv.at[1, d], dev(x, add(y, d, N), z, k)
        ).start()

    loop(1, N, share_r)
    later(rbr.at[part3], ssem.at[23])

    def left_group(g, acc):
        return acc + dot_t(gl[:, span(g, hg)], rbl[g])

    def right_group(g, acc):
        return acc + dot_t(gr[:, span(g, hg)], rbr[g])

    zero = jnp.zeros((ROWS, RANK), F32)
    left = left_group(z, zero)
    right = right_group(y, zero)

    def next_groups(d, acc):
        a, b = acc
        g = add(z, N - d, N)
        bytes_wait(rbl.at[g], share_recv.at[0, d])
        a = left_group(g, a)
        g = add(y, N - d, N)
        bytes_wait(rbr.at[g], share_recv.at[1, d])
        b = right_group(g, b)
        return a, b

    left, right = lax.fori_loop(1, N, next_groups, (left, right))
    second = to_x(left, right, pxl2, pxr2, 1).astype(BF16).astype(F32)

    s3 = reduce_x(second, 1)
    inv = gram_all(s3, 2)
    last = jnp.dot(inv, s3, precision=HIGH, preferred_element_type=F32)
    out[0] = last.T * scale

    for drain in pending:
        drain()


def owners(row_ids, col_ids, grads, acts, om):
    toks, top, hidden = grads.shape
    width = acts.shape[1]
    half = hidden // 2
    wc, hc = width // TOK, half // TOK
    chunk = half // 8
    rh = RANK // 2

    def vm(*shape, dtype=BF16):
        return pltpu.VMEM(shape, dtype)

    any_spec = pl.BlockSpec(memory_space=pl.ANY)
    return pl.pallas_call(
        functools.partial(body, float(width) ** 0.5),
        out_shape=jax.ShapeDtypeStruct((1, wc, RANK), F32),
        in_specs=[pl.BlockSpec(memory_space=pltpu.VMEM)] * 2 + [any_spec] * 3,
        out_specs=pl.BlockSpec(memory_space=pltpu.VMEM),
        scratch_shapes=[
            vm(ROWS, toks * top), vm(ROWS, toks), vm(2, 2, toks, top, chunk), vm(toks, width),
            vm(2, 2, ROWS, chunk), vm(ROWS, width),
            vm(ROWS, width), vm(ROWS, half), vm(ROWS, half), vm(half, RANK), vm(half, RANK),
            vm(2, ROWS, RANK), vm(2, ROWS, RANK),
            vm(ROWS, RANK), vm(ROWS, RANK), vm(ROWS, RANK), vm(ROWS, RANK),
            vm(N, rh, N * wc), vm(N, rh, N * wc), vm(2, N, rh, N * wc), vm(2, N, rh, N * wc),
            vm(N, rh, wc), vm(N, rh, wc), vm(2, N, rh, wc), vm(2, N, rh, wc),
            vm(N, rh, N * wc), vm(N, rh, N * wc),
            vm(ROWS, RANK), vm(ROWS, RANK), vm(ROWS, RANK),
            vm(N, RANK, N * hc), vm(N, RANK, N * hc), vm(N, RANK, N * hc), vm(N, RANK, N * hc),
            vm(N, RANK, hc), vm(N, RANK, hc), vm(N, RANK, hc), vm(N, RANK, hc),
            vm(RANK, hc), vm(RANK, hc), vm(N, RANK, N * hc), vm(N, RANK, N * hc),
            vm(3, RANK, RANK), vm(3, TOK, RANK, RANK),
            vm(RANK, RANK, dtype=F32), vm(RANK, RANK, dtype=F32),
            pltpu.SemaphoreType.DMA((24,)),
            pltpu.SemaphoreType.DMA((24,)),
            pltpu.SemaphoreType.DMA((6,)),
            pltpu.SemaphoreType.DMA((18,)),
            pltpu.SemaphoreType.DMA((3, 2)),
            pltpu.SemaphoreType.DMA((2, 2)),
            pltpu.SemaphoreType.DMA((8,)),
            pltpu.SemaphoreType.DMA((8,)),
            pltpu.SemaphoreType.DMA((3, 4)),
            pltpu.SemaphoreType.DMA((3, 4)),
            pltpu.SemaphoreType.DMA((2, N)),
        ],
        compiler_params=pltpu.CompilerParams(
            collective_id=0, has_side_effects=True, vmem_limit_bytes=60 * 1024 * 1024
        ),
        name="owners",
    )(row_ids, col_ids, grads, acts, om)


def shards(activations, expert_ids, out_grads, sketch_matrix):
    ids = expert_ids.reshape(1, -1)
    om = sketch_matrix.reshape(sketch_matrix.shape[1:])
    return owners(ids, ids.reshape(-1, 1), out_grads, activations, om)


def solution(mesh):
    return jax.shard_map(
        shards,
        mesh=mesh,
        in_specs=(
            P(("tok", "exp"), None),
            P(("tok", "exp"), None),
            P(("tok", "exp"), None, None),
            P("exp", None, None),
        ),
        out_specs=P("exp", "tok", None),
        check_vma=False,
    )
```

```python
import functools

import jax
import jax.numpy as jnp
from jax import lax
from jax.experimental import pallas as pl
from jax.experimental.pallas import tpu as pltpu
from jax.sharding import PartitionSpec as P

MESH = pl.DeviceIdType.MESH
HIGH = lax.Precision.HIGHEST
F32 = jnp.float32
BF16 = jnp.bfloat16

N = 4
TOK = N * N
EXP = 2 * N
CAP = 48
ROWS = EXP * CAP
PIECE = 2 * CAP
RANK = 128
PANEL = 16


def dot(a, b):
    return jnp.dot(a, b, preferred_element_type=F32)


def dot_t(a, b, precision=None):
    return lax.dot_general(
        a, b, (((1,), (1,)), ((), ())), precision=precision, preferred_element_type=F32
    )


def picks(row_ids, col_ids, pick, pick_x):
    pairs = row_ids.shape[1]
    toks = pick_x.shape[1]
    top = pairs // toks
    ids = row_ids[...]
    same = (col_ids[...] == ids) & (
        lax.broadcasted_iota(jnp.int32, (pairs, pairs), 0)
        < lax.broadcasted_iota(jnp.int32, (pairs, pairs), 1)
    )
    rank = jnp.sum(same.astype(F32), axis=0, keepdims=True).astype(jnp.int32)
    slot = ids * CAP + rank
    hot = lax.broadcasted_iota(jnp.int32, (ROWS, pairs), 0) == slot
    pick[...] = hot.astype(F32).astype(BF16)
    token = lax.broadcasted_iota(jnp.int32, (pairs, toks), 0) - top * lax.broadcasted_iota(
        jnp.int32, (pairs, toks), 1
    )
    of_token = ((token >= 0) & (token < top)).astype(F32).astype(BF16)
    pick_x[...] = dot(pick[...], of_token).astype(BF16)


def bytes_wait(ref, sem):
    pltpu.make_async_copy(ref, ref, sem).wait()


def terms(v):
    high = v.astype(BF16)
    rest = v - high.astype(F32)
    mid = rest.astype(BF16)
    return high, mid, (rest - mid.astype(F32)).astype(BF16)


def inverse_factor(c, cm, mm):
    cm[...] = c
    rows = lax.broadcasted_iota(jnp.int32, (RANK, RANK), 0)
    cols = lax.broadcasted_iota(jnp.int32, (RANK, RANK), 1)
    mm[...] = (rows == cols).astype(F32)
    prow = lax.broadcasted_iota(jnp.int32, (PANEL, RANK), 0)
    pcol = lax.broadcasted_iota(jnp.int32, (PANEL, RANK), 1)

    def panel(p, carry):
        base = pl.multiple_of(p * PANEL, PANEL)
        a = cm[pl.ds(base, PANEL), :]
        m = mm[pl.ds(base, PANEL), :]
        near = pltpu.roll(a, lax.rem(RANK - base, RANK), 1)
        block = [jnp.broadcast_to(near[:, i : i + 1], (PANEL, RANK)) for i in range(PANEL)]
        for i in range(PANEL):
            r = lax.rsqrt(block[i][i : i + 1, :])
            mult = jnp.where(prow > i, block[i] * (r * r), 0.0)
            for j in range(i + 1, PANEL):
                block[j] = block[j] - mult * block[j][i : i + 1, :]
            a = jnp.where(prow == i, a * r, a - mult * a[i : i + 1, :])
            m = jnp.where(prow == i, m * r, m - mult * m[i : i + 1, :])
        mm[pl.ds(base, PANEL), :] = m
        left = jnp.where(pcol >= base + PANEL, a, 0.0)
        both = jnp.concatenate([a, m], axis=1)
        a_high, a_mid, a_low = terms(left)
        b_high, b_mid, b_low = terms(both)
        deep_a = jnp.concatenate([a_high, a_high, a_mid, a_high, a_low, a_mid], axis=0)
        deep_b = jnp.concatenate([b_high, b_mid, b_high, b_low, b_high, b_mid], axis=0)
        change = lax.dot_general(
            deep_a, deep_b, (((0,), (0,)), ((), ())), preferred_element_type=F32
        )
        cm[...] -= change[:, :RANK]
        mm[...] -= change[:, RANK:]
        return carry

    lax.fori_loop(0, RANK // PANEL, panel, 0)
    return mm[...]


def body(
    scale,
    row_ids, col_ids, grads, acts, om,
    out,
    pick, pick_x, g_in, gs, xs,
    xr, gl, gr, wl, wr,
    nls, nrs, pxl, pxr, pxl2, pxr2,
    spa, spb, ra1, rb1, mid_a, mid_b, ra2, rb2, bta, btb,
    ws, wgl, wgr,
    pwl, pwr, rl1, rr1, mid_l, mid_r, turn_l, turn_r, rl2, rr2, own_rl, own_rr, rbl, rbr,
    gm, gb, cm, mm,
    ssem, rsem, gsem, selfsem, in_sem, slot_sem, left_sem, right_sem,
    line_send, line_recv, share_recv, piece_recv,
):
    tok = lax.axis_index("tok")
    ex = lax.axis_index("exp")
    y, z = lax.div(tok, N), lax.rem(tok, N)
    x, k = lax.div(ex, 2), lax.rem(ex, 2)
    half = gl.shape[1]
    width = xr.shape[1]
    wc = width // TOK
    hc = half // TOK

    def dev(a, b, c, core):
        return (b * N + c, a * 2 + core)

    def add(a, b, n):
        return lax.rem(a + b, n)

    def remote(src, dst, s, r, where):
        return pltpu.make_async_remote_copy(
            src_ref=src, dst_ref=dst, send_sem=s, recv_sem=r, device_id=where, device_id_type=MESH
        )

    def loop(lo, hi, fn):
        lax.fori_loop(lo, hi, lambda i, c: (fn(i), c)[1], 0)

    pending = []

    def later(ref, sem, when=None):
        if when is None:
            pending.append(lambda: bytes_wait(ref, sem))
        else:
            pending.append(lambda: pl.when(when)(lambda: bytes_wait(ref, sem)))

    chunk = gs.shape[3]
    chunks = half // chunk
    pairs = pick.shape[1]

    def load(side, i):
        cols = pl.ds(pl.multiple_of(side * half + i * chunk, chunk), chunk)
        slot = lax.rem(i, 2)
        return pltpu.make_async_copy(
            grads.at[:, :, cols], g_in.at[side, slot], in_sem.at[side, slot]
        )

    x_block = pwl.shape[2]
    x_blocks = width // x_block

    def load_x(i):
        cols = pl.ds(i * x_block, x_block)
        return pltpu.make_async_copy(acts.at[:, cols], pwl.at[i], in_sem.at[2, i])

    for i in range(2):
        load(0, i).start()
        load(1, i).start()
    for i in range(x_blocks):
        load_x(i).start()

    barrier = pltpu.get_barrier_semaphore()

    def greet(where):
        pl.semaphore_signal(barrier, inc=1, device_id=where, device_id_type=MESH)

    chip = x * TOK + tok

    def same_core(d):
        c = add(chip, d, N * TOK)
        greet((lax.rem(c, TOK), lax.div(c, TOK) * 2 + k))

    loop(1, N * TOK, same_core)

    def other_core(d):
        greet(dev(add(x, d, N), y, z, 1 - k))

    loop(0, N, other_core)

    def other_core_y(d):
        greet(dev(x, add(y, d, N), z, 1 - k))
        greet(dev(x, y, add(z, d, N), 1 - k))

    loop(1, N, other_core_y)
    picks(row_ids, col_ids, pick, pick_x)
    part = pl.ds(0, ROWS - CAP)

    def sort_side(i, side, first):
        slot = lax.rem(i, 2)
        load(side, i).wait()
        if not first:
            bytes_wait(gs.at[side, slot, part, :], slot_sem.at[side, slot])
        block = g_in[side, slot].reshape(pairs, chunk)
        gs[side, slot] = dot(pick[...], block).astype(BF16)

        @pl.when(i + 2 < chunks)
        def _():
            load(side, i + 2).start()

    sort_side(0, 0, True)
    sort_side(0, 1, True)
    pl.semaphore_wait(barrier, N * TOK - 1 + N + 2 * (N - 1))

    shift_r = lax.rem(N - z, N)
    swap_l = y == 0
    swap_r = z == 0
    xl = add(x, y, N)
    xd = add(x, shift_r, N)
    own_el, own_er = xl * 2 + k, xd * 2 + k

    def left_y(at_x, to_x):
        return lax.rem(to_x - at_x + N, N)

    def right_z(at_x, to_x):
        return lax.rem(at_x - to_x + N, N)

    quarter = half // N

    def om_rows(i):
        return pl.ds(pl.multiple_of(i * quarter, quarter), quarter)

    def om_right_rows(i):
        return pl.ds(pl.multiple_of(half + i * quarter, quarter), quarter)

    def om_left():
        return remote(
            om.at[om_rows(z), :], wl.at[om_rows(z), :], ssem.at[0], rsem.at[0],
            dev(add(x, N - y, N), y, z, k),
        )

    def om_right():
        return remote(
            om.at[om_right_rows(y), :], wr.at[om_rows(y), :], ssem.at[1], rsem.at[1],
            dev(add(x, z, N), y, z, k),
        )

    @pl.when(swap_l)
    def _():
        pltpu.make_async_copy(om.at[om_rows(z), :], wl.at[om_rows(z), :], rsem.at[0]).start()

    @pl.when(jnp.logical_not(swap_l))
    def _():
        om_left().start()

    @pl.when(swap_r)
    def _():
        pltpu.make_async_copy(om.at[om_right_rows(y), :], wr.at[om_rows(y), :], rsem.at[1]).start()

    @pl.when(jnp.logical_not(swap_r))
    def _():
        om_right().start()

    later(wl.at[om_rows(0), :], ssem.at[0], jnp.logical_not(swap_l))
    later(wr.at[om_rows(0), :], ssem.at[1], jnp.logical_not(swap_r))

    el, er = y * 2 + k, z * 2 + k

    def rows_of(e):
        return pl.ds(pl.multiple_of(e * CAP, CAP), CAP)

    def send_side(i, side):
        slot = lax.rem(i, 2)
        cols = pl.ds(pl.multiple_of(i * chunk, chunk), chunk)
        dst, own, here, sems = (
            (gl, own_el, el, left_sem) if side == 0 else (gr, own_er, er, right_sem)
        )

        def send_g(d):
            e = add(own, d, EXP)
            to, core = lax.div(e, 2), lax.rem(e, 2)
            if side == 0:
                where = dev(x, left_y(x, to), z, core)
            else:
                where = dev(x, y, right_z(x, to), core)
            remote(
                gs.at[side, slot, rows_of(e), :], dst.at[rows_of(here), cols],
                slot_sem.at[side, slot], sems.at[i], where,
            ).start()

        loop(1, EXP, send_g)
        dst[rows_of(here), cols] = gs[side, slot, rows_of(own), :]

    def send_chunk(i, first):
        for side in range(2):
            sort_side(i, side, first)
            send_side(i, side)

    send_side(0, 0)
    send_side(0, 1)

    for i in range(x_blocks):
        load_x(i).wait()
        xs[:, pl.ds(i * x_block, x_block)] = dot(pick_x[...], pwl[i]).astype(BF16)

    def send_x(d):
        e = add(ex, d, EXP)
        remote(
            xs.at[rows_of(e), :], xr.at[rows_of(ex), :], ssem.at[4], rsem.at[4], (tok, e)
        ).start()

    loop(1, EXP, send_x)
    later(xr.at[part, :], ssem.at[4])
    pltpu.make_async_copy(xs.at[rows_of(ex), :], xr.at[rows_of(ex), :], rsem.at[4]).start()

    send_chunk(1, True)
    loop(2, chunks // 2, lambda i: send_chunk(i, False))
    bytes_wait(wl.at[om_rows(z), :], rsem.at[0])
    bytes_wait(wr.at[om_rows(y), :], rsem.at[1])

    def om_share(d):
        remote(
            wl.at[om_rows(z), :], wl.at[om_rows(z), :], ssem.at[18], rsem.at[18],
            dev(x, y, add(z, d, N), k),
        ).start()
        remote(
            wr.at[om_rows(y), :], wr.at[om_rows(y), :], ssem.at[19], rsem.at[19],
            dev(x, add(y, d, N), z, k),
        ).start()

    loop(1, N, om_share)
    most = pl.ds(0, 3 * quarter)
    later(wl.at[most, :], ssem.at[18])
    later(wr.at[most, :], ssem.at[19])
    loop(chunks // 2, chunks, lambda i: send_chunk(i, False))
    for slot in range(2):
        later(gs.at[0, slot, part, :], slot_sem.at[0, slot])
        later(gs.at[1, slot, part, :], slot_sem.at[1, slot])

    def piece(i):
        return pl.ds(pl.multiple_of(i * PIECE, PIECE), PIECE)

    def to_x(left, right, dl, dr, phase):
        nls[phase] = left.astype(BF16)
        nrs[phase] = right.astype(BF16)
        sl, sr = ssem.at[5 + 2 * phase], ssem.at[6 + 2 * phase]
        rl_, rr_ = rsem.at[5 + 2 * phase], rsem.at[6 + 2 * phase]

        def go_l(d):
            b = add(y, d, N)
            remote(nls.at[phase, piece(b), :], dl.at[piece(x), :], sl, rl_, dev(xl, b, z, k)).start()

        def go_r(d):
            c = add(z, d, N)
            remote(nrs.at[phase, piece(c), :], dr.at[piece(x), :], sr, rr_, dev(xd, y, c, k)).start()

        loop(1, N, go_l)
        loop(1, N, go_r)
        own_l = selfsem.at[12 + 2 * phase]
        own_r = selfsem.at[13 + 2 * phase]

        @pl.when(swap_l)
        def _():
            pltpu.make_async_copy(nls.at[phase, piece(y), :], dl.at[piece(x), :], rl_).start()

        @pl.when(jnp.logical_not(swap_l))
        def _():
            remote(
                nls.at[phase, piece(y), :], dl.at[piece(x), :], own_l, rl_, dev(xl, y, z, k)
            ).start()

        @pl.when(swap_r)
        def _():
            pltpu.make_async_copy(nrs.at[phase, piece(z), :], dr.at[piece(x), :], rr_).start()

        @pl.when(jnp.logical_not(swap_r))
        def _():
            remote(
                nrs.at[phase, piece(z), :], dr.at[piece(x), :], own_r, rr_, dev(xd, y, z, k)
            ).start()

        bytes_wait(dl, rl_)
        bytes_wait(dr, rr_)
        total = dl[...].astype(F32) + dr[...].astype(F32)
        three = nls.at[phase, pl.ds(0, 3 * PIECE), :]
        bytes_wait(three, sl)
        bytes_wait(nrs.at[phase, pl.ds(0, 3 * PIECE), :], sr)

        @pl.when(jnp.logical_not(swap_l))
        def _():
            bytes_wait(nls.at[phase, pl.ds(0, PIECE), :], own_l)

        @pl.when(jnp.logical_not(swap_r))
        def _():
            bytes_wait(nrs.at[phase, pl.ds(0, PIECE), :], own_r)

        return total

    def gram_all(s, phase):
        gm[phase] = dot_t(s, s, HIGH).astype(BF16)
        pltpu.make_async_copy(gm.at[phase], gb.at[phase, tok], gsem.at[2 * phase]).start()

        def go(d):
            t = add(tok, d, TOK)
            remote(
                gm.at[phase], gb.at[phase, tok], gsem.at[2 * phase + 1], gsem.at[2 * phase], (t, ex)
            ).start()

        loop(1, TOK, go)
        bytes_wait(gb.at[phase], gsem.at[2 * phase])
        c = lax.fori_loop(
            0, TOK, lambda i, c: c + gb[phase, i].astype(F32), jnp.zeros((RANK, RANK), F32)
        )
        bytes_wait(gb.at[phase, pl.ds(0, TOK - 1)], gsem.at[2 * phase + 1])
        return inverse_factor(c, cm, mm)

    part3 = pl.ds(0, N - 1)

    def sum_along(own, got, me, cols):
        total = own[me, :, cols].astype(F32)
        for i in range(1, N):
            total = total + got[add(me, i, N), :, cols].astype(F32)
        return total

    def sum_last(own, got, me):
        def term(i, acc):
            return acc + got[add(me, i, N)].astype(F32)

        return lax.fori_loop(1, N, term, own[me].astype(F32))

    def span(i, n):
        return pl.ds(pl.multiple_of(i * n, 128), n)

    wg, hg = N * wc, N * hc

    rh = RANK // 2

    def reduce_x(p, phase):
        pt = p.T.astype(BF16)
        s, r = line_send.at[phase], line_recv.at[phase]
        ra, rb = ra1.at[phase], rb1.at[phase]
        ra_last, rb_last = ra2.at[phase], rb2.at[phase]

        def group(d):
            b = add(y, d, N)
            v = dot(pt, xr[:, span(b, wg)]).astype(BF16)
            spa[b] = v[:rh]
            for c in range(N):
                spb[c, :, span(b, wc)] = v[rh:, c * wc : (c + 1) * wc]

            @pl.when(d < N)
            def _():
                remote(spa.at[b], ra.at[y], s.at[0], r.at[0], dev(x, b, z, k)).start()

        loop(1, N + 1, group)

        def send_b(d):
            c = add(z, d, N)
            remote(spb.at[c], rb.at[z], s.at[1], r.at[1], dev(x, y, c, k)).start()

        loop(1, N, send_b)
        bytes_wait(ra.at[part3], r.at[0])

        def second_a(d):
            c = add(z, d, N)
            mid_a[c] = sum_along(spa, ra, y, span(c, wc)).astype(BF16)

            @pl.when(d < N)
            def _():
                remote(mid_a.at[c], ra_last.at[z], s.at[2], r.at[2], dev(x, y, c, k)).start()

        loop(1, N + 1, second_a)
        bytes_wait(rb.at[part3], r.at[1])

        def second_b(d):
            b = add(y, d, N)
            mid_b[b] = sum_along(spb, rb, z, span(b, wc)).astype(BF16)

            @pl.when(d < N)
            def _():
                remote(mid_b.at[b], rb_last.at[y], s.at[3], r.at[3], dev(x, b, z, k)).start()

        loop(1, N + 1, second_b)
        bytes_wait(ra_last.at[part3], r.at[2])
        top = sum_last(mid_a, ra_last, z)
        bytes_wait(rb_last.at[part3], r.at[3])
        low = sum_last(mid_b, rb_last, y)
        bytes_wait(spa.at[part3], s.at[0])
        bytes_wait(spb.at[part3], s.at[1])
        bytes_wait(mid_a.at[part3], s.at[2])
        bytes_wait(mid_b.at[part3], s.at[3])
        return jnp.concatenate([top, low], axis=0)

    bytes_wait(wl.at[most, :], rsem.at[18])
    bytes_wait(wr.at[most, :], rsem.at[19])

    def proj_chunk(i, acc):
        cols = pl.ds(pl.multiple_of(i * chunk, chunk), chunk)
        a, b = acc
        bytes_wait(gl.at[part, cols], left_sem.at[i])
        a = a + dot(gl[:, cols], wl[cols, :])
        bytes_wait(gr.at[part, cols], right_sem.at[i])
        b = b + dot(gr[:, cols], wr[cols, :])
        return a, b

    zero = jnp.zeros((ROWS, RANK), F32)
    left, right = lax.fori_loop(0, chunks, proj_chunk, (zero, zero))
    proj = to_x(left, right, pxl, pxr, 0).astype(BF16).astype(F32)
    bytes_wait(xr, rsem.at[4])

    s = reduce_x(proj, 0)
    inv = gram_all(s, 0)
    basis = jnp.dot(inv, s, precision=HIGH, preferred_element_type=F32).astype(BF16)
    bta[y, :, span(z, wc)] = basis[:rh]
    btb[z, :, span(y, wc)] = basis[rh:]
    own_a, own_b = bta.at[y, :, span(z, wc)], btb.at[z, :, span(y, wc)]
    three = pl.ds(0, (N - 1) * wc)

    def first_b(d):
        c, b = add(z, d, N), add(y, d, N)
        remote(
            own_a, own_a, line_send.at[2, 0], line_recv.at[2, 0], dev(x, y, c, k)
        ).start()
        remote(
            own_b, own_b, line_send.at[2, 1], line_recv.at[2, 1], dev(x, b, z, k)
        ).start()

    loop(1, N, first_b)
    bytes_wait(bta.at[y, :, three], line_recv.at[2, 0])

    def then_a(d):
        remote(
            bta.at[y], bta.at[y], line_send.at[2, 2], line_recv.at[2, 2], dev(x, add(y, d, N), z, k)
        ).start()

    loop(1, N, then_a)
    bytes_wait(btb.at[z, :, three], line_recv.at[2, 1])

    def then_b(d):
        remote(
            btb.at[z], btb.at[z], line_send.at[2, 3], line_recv.at[2, 3], dev(x, y, add(z, d, N), k)
        ).start()

    loop(1, N, then_b)
    later(bta.at[0, :, three], line_send.at[2, 0])
    later(btb.at[0, :, three], line_send.at[2, 1])
    later(bta.at[part3], line_send.at[2, 2])
    later(btb.at[part3], line_send.at[2, 3])
    bytes_wait(bta.at[part3], line_recv.at[2, 2])
    bytes_wait(btb.at[part3], line_recv.at[2, 3])

    def w_step(b, acc):
        low = jnp.concatenate([btb[c, :, span(b, wc)] for c in range(N)], axis=1)
        both = jnp.concatenate([bta[b], low], axis=0)
        return acc + dot_t(xr[:, span(b, wg)], both)

    weights = lax.fori_loop(0, N, w_step, jnp.zeros((ROWS, RANK), F32))
    ws[...] = weights.astype(BF16)

    def go_w(d):
        a = add(x, d, N)
        remote(
            ws.at[piece(a), :], wgl.at[piece(y), :], ssem.at[11], rsem.at[11],
            dev(a, left_y(a, x), z, k),
        ).start()
        remote(
            ws.at[piece(a), :], wgr.at[piece(z), :], ssem.at[12], rsem.at[12],
            dev(a, y, right_z(a, x), k),
        ).start()

    loop(1, N, go_w)
    later(ws.at[pl.ds(0, 3 * PIECE), :], ssem.at[11])
    later(ws.at[pl.ds(0, 3 * PIECE), :], ssem.at[12])
    later(ws.at[piece(0), :], selfsem.at[16], jnp.logical_not(swap_l))
    later(ws.at[piece(0), :], selfsem.at[17], jnp.logical_not(swap_r))

    @pl.when(swap_l)
    def _():
        pltpu.make_async_copy(ws.at[piece(x), :], wgl.at[piece(y), :], rsem.at[11]).start()

    @pl.when(jnp.logical_not(swap_l))
    def _():
        remote(
            ws.at[piece(x), :], wgl.at[piece(y), :], selfsem.at[16], rsem.at[11],
            dev(x, left_y(x, x), z, k),
        ).start()

    @pl.when(swap_r)
    def _():
        pltpu.make_async_copy(ws.at[piece(x), :], wgr.at[piece(z), :], rsem.at[12]).start()

    @pl.when(jnp.logical_not(swap_r))
    def _():
        remote(
            ws.at[piece(x), :], wgr.at[piece(z), :], selfsem.at[17], rsem.at[12],
            dev(x, y, right_z(x, x), k),
        ).start()

    bytes_wait(wgl, rsem.at[11])
    bytes_wait(wgr, rsem.at[12])

    wlt = wgl[...].astype(F32).T.astype(BF16)
    wrt = wgr[...].astype(F32).T.astype(BF16)

    def power_group(d):
        g = add(z, d, N)
        pwl[g] = dot(wlt, gl[:, span(g, hg)]).astype(BF16)

        @pl.when(d < N)
        def _():
            remote(pwl.at[g], rl1.at[z], ssem.at[13], rsem.at[13], dev(x, y, g, k)).start()

        g2 = add(y, d, N)
        pwr[g2] = dot(wrt, gr[:, span(g2, hg)]).astype(BF16)

        @pl.when(d < N)
        def _():
            remote(pwr.at[g2], rr1.at[y], ssem.at[14], rsem.at[14], dev(x, g2, z, k)).start()

    loop(1, N + 1, power_group)
    later(rl1.at[part3], ssem.at[13])
    later(rr1.at[part3], ssem.at[14])
    bytes_wait(rl1.at[part3], rsem.at[13])

    def stage2_left(i):
        b = add(y, i, N)
        mid_l[b] = sum_along(pwl, rl1, z, span(b, hc)).astype(BF16)

        @pl.when(i < N)
        def _():
            remote(
                mid_l.at[b], turn_l.at[y], ssem.at[20], rsem.at[20], dev(x, b, z, k)
            ).start()

    def stage2_right(i):
        c = add(z, i, N)
        mid_r[c] = sum_along(pwr, rr1, y, span(c, hc)).astype(BF16)

        @pl.when(i < N)
        def _():
            remote(
                mid_r.at[c], turn_r.at[z], ssem.at[21], rsem.at[21], dev(x, y, c, k)
            ).start()

    loop(1, N + 1, stage2_left)
    turn_l[y] = mid_l[y]
    later(mid_l.at[part3], ssem.at[20])
    bytes_wait(rr1.at[part3], rsem.at[14])
    loop(1, N + 1, stage2_right)
    turn_r[z] = mid_r[z]
    later(mid_r.at[part3], ssem.at[21])
    bytes_wait(turn_l.at[part3], rsem.at[20])

    def along_x_left(i):
        remote(
            turn_l.at[i], rl2.at[x], selfsem.at[0], rsem.at[24], dev(add(x, i, N), y, z, k)
        ).start()

    loop(1, N, along_x_left)
    rl2[x] = turn_l[0]
    later(rl2.at[part3], selfsem.at[0])
    bytes_wait(turn_r.at[part3], rsem.at[21])

    def along_x_right(i):
        remote(
            turn_r.at[i], rr2.at[x], selfsem.at[1], rsem.at[25], dev(add(x, N - i, N), y, z, k)
        ).start()

    loop(1, N, along_x_right)
    rr2[x] = turn_r[0]
    later(rr2.at[part3], selfsem.at[1])
    bytes_wait(rl2.at[part3], rsem.at[24])
    bytes_wait(rr2.at[part3], rsem.at[25])
    zero = jnp.zeros((RANK, hc), F32)
    sl = lax.fori_loop(0, N, lambda i, c: c + rl2[i].astype(F32), zero)
    sr = lax.fori_loop(0, N, lambda i, c: c + rr2[i].astype(F32), zero)
    s2 = jnp.concatenate([sl, sr], axis=1)
    inv = gram_all(s2, 1)
    right_basis = jnp.dot(inv, s2, precision=HIGH, preferred_element_type=F32).astype(BF16)

    own_rl[...] = right_basis[:, :hc]
    own_rr[...] = right_basis[:, hc:]

    at_l, at_r = rbl.at[z, :, span(y, hc)], rbr.at[y, :, span(z, hc)]

    def send_r(d):
        a = add(x, d, N)
        remote(
            own_rl, at_l, ssem.at[15], piece_recv.at[0, y], dev(a, left_y(a, x), z, k)
        ).start()
        remote(
            own_rr, at_r, ssem.at[16], piece_recv.at[1, z], dev(a, y, right_z(a, x), k)
        ).start()

    loop(1, N, send_r)
    later(rl2.at[part3], ssem.at[15])
    later(rr2.at[part3], ssem.at[16])
    later(own_rl, selfsem.at[10], jnp.logical_not(swap_l))
    later(own_rr, selfsem.at[11], jnp.logical_not(swap_r))

    @pl.when(swap_l)
    def _():
        pltpu.make_async_copy(own_rl, at_l, piece_recv.at[0, y]).start()

    @pl.when(jnp.logical_not(swap_l))
    def _():
        remote(own_rl, at_l, selfsem.at[10], piece_recv.at[0, y], dev(x, 0, z, k)).start()

    @pl.when(swap_r)
    def _():
        pltpu.make_async_copy(own_rr, at_r, piece_recv.at[1, z]).start()

    @pl.when(jnp.logical_not(swap_r))
    def _():
        remote(own_rr, at_r, selfsem.at[11], piece_recv.at[1, z], dev(x, y, 0, k)).start()

    def forward(i):
        b, c = add(y, i, N), add(z, i, N)
        left_piece = rbl.at[z, :, span(b, hc)]
        right_piece = rbr.at[y, :, span(c, hc)]
        bytes_wait(left_piece, piece_recv.at[0, b])

        def share_l(d):
            remote(
                left_piece, left_piece, ssem.at[22], share_recv.at[0, d], dev(x, y, add(z, d, N), k)
            ).start()

        loop(1, N, share_l)
        bytes_wait(right_piece, piece_recv.at[1, c])

        def share_r(d):
            remote(
                right_piece, right_piece, ssem.at[23], share_recv.at[1, d],
                dev(x, add(y, d, N), z, k),
            ).start()

        loop(1, N, share_r)

    loop(0, N, forward)
    later(rbl.at[part3], ssem.at[22])
    later(rbr.at[part3], ssem.at[23])

    def left_group(g, acc):
        return acc + dot_t(gl[:, span(g, hg)], rbl[g])

    def right_group(g, acc):
        return acc + dot_t(gr[:, span(g, hg)], rbr[g])

    zero = jnp.zeros((ROWS, RANK), F32)
    left = left_group(z, zero)
    right = right_group(y, zero)

    def next_groups(d, acc):
        a, b = acc
        g = add(z, N - d, N)
        bytes_wait(rbl.at[g], share_recv.at[0, d])
        a = left_group(g, a)
        g = add(y, N - d, N)
        bytes_wait(rbr.at[g], share_recv.at[1, d])
        b = right_group(g, b)
        return a, b

    left, right = lax.fori_loop(1, N, next_groups, (left, right))
    second = to_x(left, right, pxl2, pxr2, 1).astype(BF16).astype(F32)

    s3 = reduce_x(second, 1)
    inv = gram_all(s3, 2)
    last = jnp.dot(inv, s3, precision=HIGH, preferred_element_type=F32)
    out[0] = last.T * scale

    for drain in pending:
        drain()


def owners(row_ids, col_ids, grads, acts, om):
    toks, top, hidden = grads.shape
    width = acts.shape[1]
    half = hidden // 2
    wc, hc = width // TOK, half // TOK
    chunk = half // 8
    rh = RANK // 2

    def vm(*shape, dtype=BF16):
        return pltpu.VMEM(shape, dtype)

    any_spec = pl.BlockSpec(memory_space=pl.ANY)
    return pl.pallas_call(
        functools.partial(body, float(width) ** 0.5),
        out_shape=jax.ShapeDtypeStruct((1, wc, RANK), F32),
        in_specs=[pl.BlockSpec(memory_space=pltpu.VMEM)] * 2 + [any_spec] * 3,
        out_specs=pl.BlockSpec(memory_space=pltpu.VMEM),
        scratch_shapes=[
            vm(ROWS, toks * top), vm(ROWS, toks), vm(2, 2, toks, top, chunk),
            vm(2, 2, ROWS, chunk), vm(ROWS, width),
            vm(ROWS, width), vm(ROWS, half), vm(ROWS, half), vm(half, RANK), vm(half, RANK),
            vm(2, ROWS, RANK), vm(2, ROWS, RANK),
            vm(ROWS, RANK), vm(ROWS, RANK), vm(ROWS, RANK), vm(ROWS, RANK),
            vm(N, rh, N * wc), vm(N, rh, N * wc), vm(2, N, rh, N * wc), vm(2, N, rh, N * wc),
            vm(N, rh, wc), vm(N, rh, wc), vm(2, N, rh, wc), vm(2, N, rh, wc),
            vm(N, rh, N * wc), vm(N, rh, N * wc),
            vm(ROWS, RANK), vm(ROWS, RANK), vm(ROWS, RANK),
            vm(N, RANK, N * hc), vm(N, RANK, N * hc), vm(N, RANK, N * hc), vm(N, RANK, N * hc),
            vm(N, RANK, hc), vm(N, RANK, hc), vm(N, RANK, hc), vm(N, RANK, hc),
            vm(N, RANK, hc), vm(N, RANK, hc),
            vm(RANK, hc), vm(RANK, hc), vm(N, RANK, N * hc), vm(N, RANK, N * hc),
            vm(3, RANK, RANK), vm(3, TOK, RANK, RANK),
            vm(RANK, RANK, dtype=F32), vm(RANK, RANK, dtype=F32),
            pltpu.SemaphoreType.DMA((24,)),
            pltpu.SemaphoreType.DMA((26,)),
            pltpu.SemaphoreType.DMA((6,)),
            pltpu.SemaphoreType.DMA((18,)),
            pltpu.SemaphoreType.DMA((3, N)),
            pltpu.SemaphoreType.DMA((2, 2)),
            pltpu.SemaphoreType.DMA((8,)),
            pltpu.SemaphoreType.DMA((8,)),
            pltpu.SemaphoreType.DMA((3, 4)),
            pltpu.SemaphoreType.DMA((3, 4)),
            pltpu.SemaphoreType.DMA((2, N)),
            pltpu.SemaphoreType.DMA((2, N)),
        ],
        compiler_params=pltpu.CompilerParams(
            collective_id=0, has_side_effects=True, vmem_limit_bytes=60 * 1024 * 1024
        ),
        name="owners",
    )(row_ids, col_ids, grads, acts, om)


def shards(activations, expert_ids, out_grads, sketch_matrix):
    ids = expert_ids.reshape(1, -1)
    om = sketch_matrix.reshape(sketch_matrix.shape[1:])
    return owners(ids, ids.reshape(-1, 1), out_grads, activations, om)


def solution(mesh):
    return jax.shard_map(
        shards,
        mesh=mesh,
        in_specs=(
            P(("tok", "exp"), None),
            P(("tok", "exp"), None),
            P(("tok", "exp"), None, None),
            P("exp", None, None),
        ),
        out_specs=P("exp", "tok", None),
        check_vma=False,
    )
```

```python
import functools

import jax
import jax.numpy as jnp
from jax import lax
from jax.experimental import pallas as pl
from jax.experimental.pallas import tpu as pltpu
from jax.sharding import PartitionSpec as P

MESH = pl.DeviceIdType.MESH
HIGH = lax.Precision.HIGHEST
F32 = jnp.float32
BF16 = jnp.bfloat16

N = 4
TOK = N * N
EXP = 2 * N
CAP = 48
ROWS = EXP * CAP
PIECE = 2 * CAP
RANK = 128
PANEL = 16


def dot(a, b):
    return jnp.dot(a, b, preferred_element_type=F32)


def dot_t(a, b, precision=None):
    return lax.dot_general(
        a, b, (((1,), (1,)), ((), ())), precision=precision, preferred_element_type=F32
    )


def picks(row_ids, col_ids, pick, pick_x):
    pairs = row_ids.shape[1]
    toks = pick_x.shape[1]
    top = pairs // toks
    ids = row_ids[...]
    same = (col_ids[...] == ids) & (
        lax.broadcasted_iota(jnp.int32, (pairs, pairs), 0)
        < lax.broadcasted_iota(jnp.int32, (pairs, pairs), 1)
    )
    rank = jnp.sum(same.astype(F32), axis=0, keepdims=True).astype(jnp.int32)
    slot = ids * CAP + rank
    hot = lax.broadcasted_iota(jnp.int32, (ROWS, pairs), 0) == slot
    pick[...] = hot.astype(F32).astype(BF16)
    token = lax.broadcasted_iota(jnp.int32, (pairs, toks), 0) - top * lax.broadcasted_iota(
        jnp.int32, (pairs, toks), 1
    )
    of_token = ((token >= 0) & (token < top)).astype(F32).astype(BF16)
    pick_x[...] = dot(pick[...], of_token).astype(BF16)


def bytes_wait(ref, sem):
    pltpu.make_async_copy(ref, ref, sem).wait()


def terms(v):
    high = v.astype(BF16)
    rest = v - high.astype(F32)
    mid = rest.astype(BF16)
    return high, mid, (rest - mid.astype(F32)).astype(BF16)


def inverse_factor(c, cm, mm):
    cm[...] = c
    rows = lax.broadcasted_iota(jnp.int32, (RANK, RANK), 0)
    cols = lax.broadcasted_iota(jnp.int32, (RANK, RANK), 1)
    mm[...] = (rows == cols).astype(F32)
    prow = lax.broadcasted_iota(jnp.int32, (PANEL, RANK), 0)
    pcol = lax.broadcasted_iota(jnp.int32, (PANEL, RANK), 1)

    def panel(p, carry):
        base = pl.multiple_of(p * PANEL, PANEL)
        a = cm[pl.ds(base, PANEL), :]
        m = mm[pl.ds(base, PANEL), :]
        near = pltpu.roll(a, lax.rem(RANK - base, RANK), 1)
        block = [jnp.broadcast_to(near[:, i : i + 1], (PANEL, RANK)) for i in range(PANEL)]
        for i in range(PANEL):
            r = lax.rsqrt(block[i][i : i + 1, :])
            mult = jnp.where(prow > i, block[i] * (r * r), 0.0)
            for j in range(i + 1, PANEL):
                block[j] = block[j] - mult * block[j][i : i + 1, :]
            a = jnp.where(prow == i, a * r, a - mult * a[i : i + 1, :])
            m = jnp.where(prow == i, m * r, m - mult * m[i : i + 1, :])
        mm[pl.ds(base, PANEL), :] = m
        left = jnp.where(pcol >= base + PANEL, a, 0.0)
        both = jnp.concatenate([a, m], axis=1)
        a_high, a_mid, a_low = terms(left)
        b_high, b_mid, b_low = terms(both)
        deep_a = jnp.concatenate([a_high, a_high, a_mid, a_high, a_low, a_mid], axis=0)
        deep_b = jnp.concatenate([b_high, b_mid, b_high, b_low, b_high, b_mid], axis=0)
        change = lax.dot_general(
            deep_a, deep_b, (((0,), (0,)), ((), ())), preferred_element_type=F32
        )
        cm[...] -= change[:, :RANK]
        mm[...] -= change[:, RANK:]
        return carry

    lax.fori_loop(0, RANK // PANEL, panel, 0)
    return mm[...]


def body(
    scale,
    row_ids, col_ids, grads, acts, om,
    out,
    pick, pick_x, g_in, gs, xs,
    xr, gl, gr, wl, wr,
    nls, nrs, pxl, pxr, pxl2, pxr2,
    spa, spb, ra1, rb1, mid_a, mid_b, ra2, rb2, bta, btb,
    ws, wgl, wgr,
    pwl, pwr, rl1, rr1, mid_l, mid_r, turn_l, turn_r, rl2, rr2, own_rl, own_rr, rbl, rbr,
    gm, gb, cm, mm,
    ssem, rsem, gsem, selfsem, in_sem, slot_sem, left_sem, right_sem,
    line_send, line_recv, share_recv, piece_recv, half_send, half_recv,
):
    tok = lax.axis_index("tok")
    ex = lax.axis_index("exp")
    y, z = lax.div(tok, N), lax.rem(tok, N)
    x, k = lax.div(ex, 2), lax.rem(ex, 2)
    half = gl.shape[1]
    width = xr.shape[1]
    wc = width // TOK
    hc = half // TOK

    def dev(a, b, c, core):
        return (b * N + c, a * 2 + core)

    def add(a, b, n):
        return lax.rem(a + b, n)

    def remote(src, dst, s, r, where):
        return pltpu.make_async_remote_copy(
            src_ref=src, dst_ref=dst, send_sem=s, recv_sem=r, device_id=where, device_id_type=MESH
        )

    def loop(lo, hi, fn):
        lax.fori_loop(lo, hi, lambda i, c: (fn(i), c)[1], 0)

    pending = []

    def later(ref, sem, when=None):
        if when is None:
            pending.append(lambda: bytes_wait(ref, sem))
        else:
            pending.append(lambda: pl.when(when)(lambda: bytes_wait(ref, sem)))

    chunk = gs.shape[3]
    chunks = half // chunk
    pairs = pick.shape[1]

    def load(side, i):
        cols = pl.ds(pl.multiple_of(side * half + i * chunk, chunk), chunk)
        slot = lax.rem(i, 2)
        return pltpu.make_async_copy(
            grads.at[:, :, cols], g_in.at[side, slot], in_sem.at[side, slot]
        )

    x_block = pwl.shape[2]
    x_blocks = width // x_block

    def load_x(i):
        cols = pl.ds(i * x_block, x_block)
        return pltpu.make_async_copy(acts.at[:, cols], pwl.at[i], in_sem.at[2, i])

    for i in range(2):
        load(0, i).start()
        load(1, i).start()
    for i in range(x_blocks):
        load_x(i).start()

    barrier = pltpu.get_barrier_semaphore()

    def greet(where):
        pl.semaphore_signal(barrier, inc=1, device_id=where, device_id_type=MESH)

    chip = x * TOK + tok

    def same_core(d):
        c = add(chip, d, N * TOK)
        greet((lax.rem(c, TOK), lax.div(c, TOK) * 2 + k))

    loop(1, N * TOK, same_core)

    def other_core(d):
        greet(dev(add(x, d, N), y, z, 1 - k))

    loop(0, N, other_core)

    def other_core_y(d):
        greet(dev(x, add(y, d, N), z, 1 - k))
        greet(dev(x, y, add(z, d, N), 1 - k))

    loop(1, N, other_core_y)
    picks(row_ids, col_ids, pick, pick_x)
    part = pl.ds(0, ROWS - CAP)

    def sort_side(i, side, first):
        slot = lax.rem(i, 2)
        load(side, i).wait()
        if not first:
            bytes_wait(gs.at[side, slot, part, :], slot_sem.at[side, slot])
        block = g_in[side, slot].reshape(pairs, chunk)
        gs[side, slot] = dot(pick[...], block).astype(BF16)

        @pl.when(i + 2 < chunks)
        def _():
            load(side, i + 2).start()

    sort_side(0, 0, True)
    sort_side(0, 1, True)
    pl.semaphore_wait(barrier, N * TOK - 1 + N + 2 * (N - 1))

    shift_r = lax.rem(N - z, N)
    swap_l = y == 0
    swap_r = z == 0
    xl = add(x, y, N)
    xd = add(x, shift_r, N)
    own_el, own_er = xl * 2 + k, xd * 2 + k

    def left_y(at_x, to_x):
        return lax.rem(to_x - at_x + N, N)

    def right_z(at_x, to_x):
        return lax.rem(at_x - to_x + N, N)

    quarter = half // N

    def om_rows(i):
        return pl.ds(pl.multiple_of(i * quarter, quarter), quarter)

    def om_right_rows(i):
        return pl.ds(pl.multiple_of(half + i * quarter, quarter), quarter)

    def om_left():
        return remote(
            om.at[om_rows(z), :], wl.at[om_rows(z), :], ssem.at[0], rsem.at[0],
            dev(add(x, N - y, N), y, z, k),
        )

    def om_right():
        return remote(
            om.at[om_right_rows(y), :], wr.at[om_rows(y), :], ssem.at[1], rsem.at[1],
            dev(add(x, z, N), y, z, k),
        )

    @pl.when(swap_l)
    def _():
        pltpu.make_async_copy(om.at[om_rows(z), :], wl.at[om_rows(z), :], rsem.at[0]).start()

    @pl.when(jnp.logical_not(swap_l))
    def _():
        om_left().start()

    @pl.when(swap_r)
    def _():
        pltpu.make_async_copy(om.at[om_right_rows(y), :], wr.at[om_rows(y), :], rsem.at[1]).start()

    @pl.when(jnp.logical_not(swap_r))
    def _():
        om_right().start()

    later(wl.at[om_rows(0), :], ssem.at[0], jnp.logical_not(swap_l))
    later(wr.at[om_rows(0), :], ssem.at[1], jnp.logical_not(swap_r))

    el, er = y * 2 + k, z * 2 + k

    def rows_of(e):
        return pl.ds(pl.multiple_of(e * CAP, CAP), CAP)

    def send_side(i, side):
        slot = lax.rem(i, 2)
        cols = pl.ds(pl.multiple_of(i * chunk, chunk), chunk)
        dst, own, here, sems = (
            (gl, own_el, el, left_sem) if side == 0 else (gr, own_er, er, right_sem)
        )

        def send_g(d):
            e = add(own, d, EXP)
            to, core = lax.div(e, 2), lax.rem(e, 2)
            if side == 0:
                where = dev(x, left_y(x, to), z, core)
            else:
                where = dev(x, y, right_z(x, to), core)
            remote(
                gs.at[side, slot, rows_of(e), :], dst.at[rows_of(here), cols],
                slot_sem.at[side, slot], sems.at[i], where,
            ).start()

        loop(1, EXP, send_g)
        dst[rows_of(here), cols] = gs[side, slot, rows_of(own), :]

    def send_chunk(i, first):
        for side in range(2):
            sort_side(i, side, first)
            send_side(i, side)

    send_side(0, 0)
    send_side(0, 1)

    for i in range(x_blocks):
        load_x(i).wait()
        xs[:, pl.ds(i * x_block, x_block)] = dot(pick_x[...], pwl[i]).astype(BF16)

    def send_x(d):
        e = add(ex, d, EXP)
        remote(
            xs.at[rows_of(e), :], xr.at[rows_of(ex), :], ssem.at[4], rsem.at[4], (tok, e)
        ).start()

    loop(1, EXP, send_x)
    later(xr.at[part, :], ssem.at[4])
    pltpu.make_async_copy(xs.at[rows_of(ex), :], xr.at[rows_of(ex), :], rsem.at[4]).start()

    send_chunk(1, True)
    loop(2, chunks // 2, lambda i: send_chunk(i, False))
    bytes_wait(wl.at[om_rows(z), :], rsem.at[0])
    bytes_wait(wr.at[om_rows(y), :], rsem.at[1])

    def om_share(d):
        remote(
            wl.at[om_rows(z), :], wl.at[om_rows(z), :], ssem.at[18], rsem.at[18],
            dev(x, y, add(z, d, N), k),
        ).start()
        remote(
            wr.at[om_rows(y), :], wr.at[om_rows(y), :], ssem.at[19], rsem.at[19],
            dev(x, add(y, d, N), z, k),
        ).start()

    loop(1, N, om_share)
    most = pl.ds(0, 3 * quarter)
    later(wl.at[most, :], ssem.at[18])
    later(wr.at[most, :], ssem.at[19])
    loop(chunks // 2, chunks, lambda i: send_chunk(i, False))
    for slot in range(2):
        later(gs.at[0, slot, part, :], slot_sem.at[0, slot])
        later(gs.at[1, slot, part, :], slot_sem.at[1, slot])

    def piece(i):
        return pl.ds(pl.multiple_of(i * PIECE, PIECE), PIECE)

    def to_x(left, right, dl, dr, phase):
        nls[phase] = left.astype(BF16)
        nrs[phase] = right.astype(BF16)
        sl, sr = ssem.at[5 + 2 * phase], ssem.at[6 + 2 * phase]
        rl_, rr_ = rsem.at[5 + 2 * phase], rsem.at[6 + 2 * phase]

        def go_l(d):
            b = add(y, d, N)
            remote(nls.at[phase, piece(b), :], dl.at[piece(x), :], sl, rl_, dev(xl, b, z, k)).start()

        def go_r(d):
            c = add(z, d, N)
            remote(nrs.at[phase, piece(c), :], dr.at[piece(x), :], sr, rr_, dev(xd, y, c, k)).start()

        loop(1, N, go_l)
        loop(1, N, go_r)
        own_l = selfsem.at[12 + 2 * phase]
        own_r = selfsem.at[13 + 2 * phase]

        @pl.when(swap_l)
        def _():
            pltpu.make_async_copy(nls.at[phase, piece(y), :], dl.at[piece(x), :], rl_).start()

        @pl.when(jnp.logical_not(swap_l))
        def _():
            remote(
                nls.at[phase, piece(y), :], dl.at[piece(x), :], own_l, rl_, dev(xl, y, z, k)
            ).start()

        @pl.when(swap_r)
        def _():
            pltpu.make_async_copy(nrs.at[phase, piece(z), :], dr.at[piece(x), :], rr_).start()

        @pl.when(jnp.logical_not(swap_r))
        def _():
            remote(
                nrs.at[phase, piece(z), :], dr.at[piece(x), :], own_r, rr_, dev(xd, y, z, k)
            ).start()

        bytes_wait(dl, rl_)
        bytes_wait(dr, rr_)
        total = dl[...].astype(F32) + dr[...].astype(F32)
        three = nls.at[phase, pl.ds(0, 3 * PIECE), :]
        bytes_wait(three, sl)
        bytes_wait(nrs.at[phase, pl.ds(0, 3 * PIECE), :], sr)

        @pl.when(jnp.logical_not(swap_l))
        def _():
            bytes_wait(nls.at[phase, pl.ds(0, PIECE), :], own_l)

        @pl.when(jnp.logical_not(swap_r))
        def _():
            bytes_wait(nrs.at[phase, pl.ds(0, PIECE), :], own_r)

        return total

    def gram_all(s, phase):
        gm[phase] = dot_t(s, s, HIGH).astype(BF16)
        pltpu.make_async_copy(gm.at[phase], gb.at[phase, tok], gsem.at[2 * phase]).start()

        def go(d):
            t = add(tok, d, TOK)
            remote(
                gm.at[phase], gb.at[phase, tok], gsem.at[2 * phase + 1], gsem.at[2 * phase], (t, ex)
            ).start()

        loop(1, TOK, go)
        bytes_wait(gb.at[phase], gsem.at[2 * phase])
        c = lax.fori_loop(
            0, TOK, lambda i, c: c + gb[phase, i].astype(F32), jnp.zeros((RANK, RANK), F32)
        )
        bytes_wait(gb.at[phase, pl.ds(0, TOK - 1)], gsem.at[2 * phase + 1])
        return inverse_factor(c, cm, mm)

    part3 = pl.ds(0, N - 1)

    def sum_along(own, got, me, cols, rows=slice(None)):
        total = own[me, rows, cols].astype(F32)
        for i in range(1, N):
            total = total + got[add(me, i, N), rows, cols].astype(F32)
        return total

    def sum_last(own, got, me):
        def term(i, acc):
            return acc + got[add(me, i, N)].astype(F32)

        return lax.fori_loop(1, N, term, own[me].astype(F32))

    def span(i, n):
        return pl.ds(pl.multiple_of(i * n, 128), n)

    wg, hg = N * wc, N * hc

    rh = RANK // 2

    def reduce_x(p, phase):
        pt = p.T.astype(BF16)
        s, r = line_send.at[phase], line_recv.at[phase]
        ra, rb = ra1.at[phase], rb1.at[phase]
        ra_last, rb_last = ra2.at[phase], rb2.at[phase]

        def group(d):
            b = add(y, d, N)
            v = dot(pt, xr[:, span(b, wg)]).astype(BF16)
            spa[b] = v[:rh]
            for c in range(N):
                spb[c, :, span(b, wc)] = v[rh:, c * wc : (c + 1) * wc]

            @pl.when(d < N)
            def _():
                remote(spa.at[b], ra.at[y], s.at[0], r.at[0], dev(x, b, z, k)).start()

        loop(1, N + 1, group)

        def send_b(d):
            c = add(z, d, N)
            remote(spb.at[c], rb.at[z], s.at[1], r.at[1], dev(x, y, c, k)).start()

        loop(1, N, send_b)
        bytes_wait(ra.at[part3], r.at[0])

        def second_a(d):
            c = add(z, d, N)
            mid_a[c] = sum_along(spa, ra, y, span(c, wc)).astype(BF16)

            @pl.when(d < N)
            def _():
                remote(mid_a.at[c], ra_last.at[z], s.at[2], r.at[2], dev(x, y, c, k)).start()

        loop(1, N + 1, second_a)
        bytes_wait(rb.at[part3], r.at[1])

        def second_b(d):
            b = add(y, d, N)
            mid_b[b] = sum_along(spb, rb, z, span(b, wc)).astype(BF16)

            @pl.when(d < N)
            def _():
                remote(mid_b.at[b], rb_last.at[y], s.at[3], r.at[3], dev(x, b, z, k)).start()

        loop(1, N + 1, second_b)
        bytes_wait(ra_last.at[part3], r.at[2])
        top = sum_last(mid_a, ra_last, z)
        bytes_wait(rb_last.at[part3], r.at[3])
        low = sum_last(mid_b, rb_last, y)
        bytes_wait(spa.at[part3], s.at[0])
        bytes_wait(spb.at[part3], s.at[1])
        bytes_wait(mid_a.at[part3], s.at[2])
        bytes_wait(mid_b.at[part3], s.at[3])
        return jnp.concatenate([top, low], axis=0)

    bytes_wait(wl.at[most, :], rsem.at[18])
    bytes_wait(wr.at[most, :], rsem.at[19])

    def proj_chunk(i, acc):
        cols = pl.ds(pl.multiple_of(i * chunk, chunk), chunk)
        a, b = acc
        bytes_wait(gl.at[part, cols], left_sem.at[i])
        a = a + dot(gl[:, cols], wl[cols, :])
        bytes_wait(gr.at[part, cols], right_sem.at[i])
        b = b + dot(gr[:, cols], wr[cols, :])
        return a, b

    zero = jnp.zeros((ROWS, RANK), F32)
    left, right = lax.fori_loop(0, chunks, proj_chunk, (zero, zero))
    proj = to_x(left, right, pxl, pxr, 0).astype(BF16).astype(F32)
    bytes_wait(xr, rsem.at[4])

    s = reduce_x(proj, 0)
    inv = gram_all(s, 0)
    basis = jnp.dot(inv, s, precision=HIGH, preferred_element_type=F32).astype(BF16)
    bta[y, :, span(z, wc)] = basis[:rh]
    btb[z, :, span(y, wc)] = basis[rh:]
    own_a, own_b = bta.at[y, :, span(z, wc)], btb.at[z, :, span(y, wc)]
    three = pl.ds(0, (N - 1) * wc)

    def first_b(d):
        c, b = add(z, d, N), add(y, d, N)
        remote(
            own_a, own_a, line_send.at[2, 0], line_recv.at[2, 0], dev(x, y, c, k)
        ).start()
        remote(
            own_b, own_b, line_send.at[2, 1], line_recv.at[2, 1], dev(x, b, z, k)
        ).start()

    loop(1, N, first_b)
    bytes_wait(bta.at[y, :, three], line_recv.at[2, 0])

    def then_a(d):
        remote(
            bta.at[y], bta.at[y], line_send.at[2, 2], line_recv.at[2, 2], dev(x, add(y, d, N), z, k)
        ).start()

    loop(1, N, then_a)
    bytes_wait(btb.at[z, :, three], line_recv.at[2, 1])

    def then_b(d):
        remote(
            btb.at[z], btb.at[z], line_send.at[2, 3], line_recv.at[2, 3], dev(x, y, add(z, d, N), k)
        ).start()

    loop(1, N, then_b)
    later(bta.at[0, :, three], line_send.at[2, 0])
    later(btb.at[0, :, three], line_send.at[2, 1])
    later(bta.at[part3], line_send.at[2, 2])
    later(btb.at[part3], line_send.at[2, 3])
    bytes_wait(bta.at[part3], line_recv.at[2, 2])
    bytes_wait(btb.at[part3], line_recv.at[2, 3])

    def w_step(b, acc):
        low = jnp.concatenate([btb[c, :, span(b, wc)] for c in range(N)], axis=1)
        both = jnp.concatenate([bta[b], low], axis=0)
        return acc + dot_t(xr[:, span(b, wg)], both)

    weights = lax.fori_loop(0, N, w_step, jnp.zeros((ROWS, RANK), F32))
    ws[...] = weights.astype(BF16)

    def go_w(d):
        a = add(x, d, N)
        remote(
            ws.at[piece(a), :], wgl.at[piece(y), :], ssem.at[11], rsem.at[11],
            dev(a, left_y(a, x), z, k),
        ).start()
        remote(
            ws.at[piece(a), :], wgr.at[piece(z), :], ssem.at[12], rsem.at[12],
            dev(a, y, right_z(a, x), k),
        ).start()

    loop(1, N, go_w)
    later(ws.at[pl.ds(0, 3 * PIECE), :], ssem.at[11])
    later(ws.at[pl.ds(0, 3 * PIECE), :], ssem.at[12])
    later(ws.at[piece(0), :], selfsem.at[16], jnp.logical_not(swap_l))
    later(ws.at[piece(0), :], selfsem.at[17], jnp.logical_not(swap_r))

    @pl.when(swap_l)
    def _():
        pltpu.make_async_copy(ws.at[piece(x), :], wgl.at[piece(y), :], rsem.at[11]).start()

    @pl.when(jnp.logical_not(swap_l))
    def _():
        remote(
            ws.at[piece(x), :], wgl.at[piece(y), :], selfsem.at[16], rsem.at[11],
            dev(x, left_y(x, x), z, k),
        ).start()

    @pl.when(swap_r)
    def _():
        pltpu.make_async_copy(ws.at[piece(x), :], wgr.at[piece(z), :], rsem.at[12]).start()

    @pl.when(jnp.logical_not(swap_r))
    def _():
        remote(
            ws.at[piece(x), :], wgr.at[piece(z), :], selfsem.at[17], rsem.at[12],
            dev(x, y, right_z(x, x), k),
        ).start()

    bytes_wait(wgl, rsem.at[11])
    bytes_wait(wgr, rsem.at[12])

    wlt = wgl[...].astype(F32).T.astype(BF16)
    wrt = wgr[...].astype(F32).T.astype(BF16)

    rank_halves = (pl.ds(0, rh), pl.ds(rh, rh))

    def first_left(g, h):
        rows = rank_halves[h]
        remote(
            pwl.at[g, rows], rl1.at[z, rows], half_send.at[0, h], half_recv.at[0, h],
            dev(x, y, g, k),
        ).start()

    def first_right(g, h):
        rows = rank_halves[h]
        remote(
            pwr.at[g, rows], rr1.at[y, rows], half_send.at[1, h], half_recv.at[1, h],
            dev(x, g, z, k),
        ).start()

    def power_group(d):
        g, g2 = add(z, d, N), add(y, d, N)
        pwl[g] = dot(wlt, gl[:, span(g, hg)]).astype(BF16)

        @pl.when(d < N)
        def _():
            first_left(g, 0)

        pwr[g2] = dot(wrt, gr[:, span(g2, hg)]).astype(BF16)

        @pl.when(d < N)
        def _():
            first_right(g2, 0)

    loop(1, N + 1, power_group)

    def other_half(d):
        first_left(add(z, d, N), 1)
        first_right(add(y, d, N), 1)

    loop(1, N, other_half)

    for h in range(2):
        rows = rank_halves[h]
        s_h = [half_send.at[i, h] for i in range(6)]
        r_h = [half_recv.at[i, h] for i in range(6)]
        later(rl1.at[part3, rows], s_h[0])
        later(rr1.at[part3, rows], s_h[1])

        def stage2_left(i):
            b = add(y, i, N)
            mid_l[b, rows] = sum_along(pwl, rl1, z, span(b, hc), rows).astype(BF16)

            @pl.when(i < N)
            def _():
                remote(
                    mid_l.at[b, rows], turn_l.at[y, rows], s_h[2], r_h[2], dev(x, b, z, k)
                ).start()

        def stage2_right(i):
            c = add(z, i, N)
            mid_r[c, rows] = sum_along(pwr, rr1, y, span(c, hc), rows).astype(BF16)

            @pl.when(i < N)
            def _():
                remote(
                    mid_r.at[c, rows], turn_r.at[z, rows], s_h[3], r_h[3], dev(x, y, c, k)
                ).start()

        bytes_wait(rl1.at[part3, rows], r_h[0])
        loop(1, N + 1, stage2_left)
        turn_l[y, rows] = mid_l[y, rows]
        bytes_wait(rr1.at[part3, rows], r_h[1])
        loop(1, N + 1, stage2_right)
        turn_r[z, rows] = mid_r[z, rows]

        def along_x_left(i):
            remote(
                turn_l.at[i, rows], rl2.at[x, rows], s_h[4], r_h[4], dev(add(x, i, N), y, z, k)
            ).start()

        def along_x_right(i):
            remote(
                turn_r.at[i, rows], rr2.at[x, rows], s_h[5], r_h[5], dev(add(x, N - i, N), y, z, k)
            ).start()

        bytes_wait(turn_l.at[part3, rows], r_h[2])
        loop(1, N, along_x_left)
        rl2[x, rows] = turn_l[0, rows]
        bytes_wait(turn_r.at[part3, rows], r_h[3])
        loop(1, N, along_x_right)
        rr2[x, rows] = turn_r[0, rows]
        later(mid_l.at[part3, rows], s_h[2])
        later(mid_r.at[part3, rows], s_h[3])
        later(rl2.at[part3, rows], s_h[4])
        later(rr2.at[part3, rows], s_h[5])

    for h in range(2):
        rows = rank_halves[h]
        bytes_wait(rl2.at[part3, rows], half_recv.at[4, h])
        bytes_wait(rr2.at[part3, rows], half_recv.at[5, h])

    zero = jnp.zeros((RANK, hc), F32)
    sl = lax.fori_loop(0, N, lambda i, c: c + rl2[i].astype(F32), zero)
    sr = lax.fori_loop(0, N, lambda i, c: c + rr2[i].astype(F32), zero)
    s2 = jnp.concatenate([sl, sr], axis=1)
    inv = gram_all(s2, 1)
    right_basis = jnp.dot(inv, s2, precision=HIGH, preferred_element_type=F32).astype(BF16)

    own_rl[...] = right_basis[:, :hc]
    own_rr[...] = right_basis[:, hc:]

    def send_half(h):
        rows = rank_halves[h]
        from_l, from_r = own_rl.at[rows], own_rr.at[rows]
        at_l, at_r = rbl.at[z, rows, span(y, hc)], rbr.at[y, rows, span(z, hc)]
        here_l, here_r = piece_recv.at[0, h, y], piece_recv.at[1, h, z]

        def send_r(d):
            a = add(x, d, N)
            remote(from_l, at_l, ssem.at[15], here_l, dev(a, left_y(a, x), z, k)).start()
            remote(from_r, at_r, ssem.at[16], here_r, dev(a, y, right_z(a, x), k)).start()

        loop(1, N, send_r)

        @pl.when(swap_l)
        def _():
            pltpu.make_async_copy(from_l, at_l, here_l).start()

        @pl.when(jnp.logical_not(swap_l))
        def _():
            remote(from_l, at_l, selfsem.at[10], here_l, dev(x, 0, z, k)).start()

        @pl.when(swap_r)
        def _():
            pltpu.make_async_copy(from_r, at_r, here_r).start()

        @pl.when(jnp.logical_not(swap_r))
        def _():
            remote(from_r, at_r, selfsem.at[11], here_r, dev(x, y, 0, k)).start()

    send_half(0)
    send_half(1)
    later(rl2.at[part3], ssem.at[15])
    later(rr2.at[part3], ssem.at[16])
    later(own_rl, selfsem.at[10], jnp.logical_not(swap_l))
    later(own_rr, selfsem.at[11], jnp.logical_not(swap_r))

    def forward_half(h):
        rows = rank_halves[h]

        def forward(i):
            b, c = add(y, i, N), add(z, i, N)
            left_piece = rbl.at[z, rows, span(b, hc)]
            right_piece = rbr.at[y, rows, span(c, hc)]
            bytes_wait(left_piece, piece_recv.at[0, h, b])

            def share_l(d):
                remote(
                    left_piece, left_piece, ssem.at[22], share_recv.at[0, d],
                    dev(x, y, add(z, d, N), k),
                ).start()

            loop(1, N, share_l)
            bytes_wait(right_piece, piece_recv.at[1, h, c])

            def share_r(d):
                remote(
                    right_piece, right_piece, ssem.at[23], share_recv.at[1, d],
                    dev(x, add(y, d, N), z, k),
                ).start()

            loop(1, N, share_r)

        loop(0, N, forward)

    forward_half(0)
    forward_half(1)
    later(rbl.at[part3], ssem.at[22])
    later(rbr.at[part3], ssem.at[23])

    def left_group(g, acc):
        return acc + dot_t(gl[:, span(g, hg)], rbl[g])

    def right_group(g, acc):
        return acc + dot_t(gr[:, span(g, hg)], rbr[g])

    zero = jnp.zeros((ROWS, RANK), F32)
    left = left_group(z, zero)
    right = right_group(y, zero)

    def next_groups(d, acc):
        a, b = acc
        g = add(z, N - d, N)
        bytes_wait(rbl.at[g], share_recv.at[0, d])
        a = left_group(g, a)
        g = add(y, N - d, N)
        bytes_wait(rbr.at[g], share_recv.at[1, d])
        b = right_group(g, b)
        return a, b

    left, right = lax.fori_loop(1, N, next_groups, (left, right))
    second = to_x(left, right, pxl2, pxr2, 1).astype(BF16).astype(F32)

    s3 = reduce_x(second, 1)
    inv = gram_all(s3, 2)
    last = jnp.dot(inv, s3, precision=HIGH, preferred_element_type=F32)
    out[0] = last.T * scale

    for drain in pending:
        drain()


def owners(row_ids, col_ids, grads, acts, om):
    toks, top, hidden = grads.shape
    width = acts.shape[1]
    half = hidden // 2
    wc, hc = width // TOK, half // TOK
    chunk = half // 8
    rh = RANK // 2

    def vm(*shape, dtype=BF16):
        return pltpu.VMEM(shape, dtype)

    any_spec = pl.BlockSpec(memory_space=pl.ANY)
    return pl.pallas_call(
        functools.partial(body, float(width) ** 0.5),
        out_shape=jax.ShapeDtypeStruct((1, wc, RANK), F32),
        in_specs=[pl.BlockSpec(memory_space=pltpu.VMEM)] * 2 + [any_spec] * 3,
        out_specs=pl.BlockSpec(memory_space=pltpu.VMEM),
        scratch_shapes=[
            vm(ROWS, toks * top), vm(ROWS, toks), vm(2, 2, toks, top, chunk),
            vm(2, 2, ROWS, chunk), vm(ROWS, width),
            vm(ROWS, width), vm(ROWS, half), vm(ROWS, half), vm(half, RANK), vm(half, RANK),
            vm(2, ROWS, RANK), vm(2, ROWS, RANK),
            vm(ROWS, RANK), vm(ROWS, RANK), vm(ROWS, RANK), vm(ROWS, RANK),
            vm(N, rh, N * wc), vm(N, rh, N * wc), vm(2, N, rh, N * wc), vm(2, N, rh, N * wc),
            vm(N, rh, wc), vm(N, rh, wc), vm(2, N, rh, wc), vm(2, N, rh, wc),
            vm(N, rh, N * wc), vm(N, rh, N * wc),
            vm(ROWS, RANK), vm(ROWS, RANK), vm(ROWS, RANK),
            vm(N, RANK, N * hc), vm(N, RANK, N * hc), vm(N, RANK, N * hc), vm(N, RANK, N * hc),
            vm(N, RANK, hc), vm(N, RANK, hc), vm(N, RANK, hc), vm(N, RANK, hc),
            vm(N, RANK, hc), vm(N, RANK, hc),
            vm(RANK, hc), vm(RANK, hc), vm(N, RANK, N * hc), vm(N, RANK, N * hc),
            vm(3, RANK, RANK), vm(3, TOK, RANK, RANK),
            vm(RANK, RANK, dtype=F32), vm(RANK, RANK, dtype=F32),
            pltpu.SemaphoreType.DMA((24,)),
            pltpu.SemaphoreType.DMA((26,)),
            pltpu.SemaphoreType.DMA((6,)),
            pltpu.SemaphoreType.DMA((18,)),
            pltpu.SemaphoreType.DMA((3, N)),
            pltpu.SemaphoreType.DMA((2, 2)),
            pltpu.SemaphoreType.DMA((8,)),
            pltpu.SemaphoreType.DMA((8,)),
            pltpu.SemaphoreType.DMA((3, 4)),
            pltpu.SemaphoreType.DMA((3, 4)),
            pltpu.SemaphoreType.DMA((2, N)),
            pltpu.SemaphoreType.DMA((2, 2, N)),
            pltpu.SemaphoreType.DMA((6, 2)),
            pltpu.SemaphoreType.DMA((6, 2)),
        ],
        compiler_params=pltpu.CompilerParams(
            collective_id=0, has_side_effects=True, vmem_limit_bytes=60 * 1024 * 1024
        ),
        name="owners",
    )(row_ids, col_ids, grads, acts, om)


def shards(activations, expert_ids, out_grads, sketch_matrix):
    ids = expert_ids.reshape(1, -1)
    om = sketch_matrix.reshape(sketch_matrix.shape[1:])
    return owners(ids, ids.reshape(-1, 1), out_grads, activations, om)


def solution(mesh):
    return jax.shard_map(
        shards,
        mesh=mesh,
        in_specs=(
            P(("tok", "exp"), None),
            P(("tok", "exp"), None),
            P(("tok", "exp"), None, None),
            P("exp", None, None),
        ),
        out_specs=P("exp", "tok", None),
        check_vma=False,
    )
```

```python
import functools

import jax
import jax.numpy as jnp
from jax import lax
from jax.experimental import pallas as pl
from jax.experimental.pallas import tpu as pltpu
from jax.sharding import PartitionSpec as P

MESH = pl.DeviceIdType.MESH
HIGH = lax.Precision.HIGHEST
F32 = jnp.float32
BF16 = jnp.bfloat16

N = 4
TOK = N * N
EXP = 2 * N
CAP = 48
ROWS = EXP * CAP
PIECE = 2 * CAP
RANK = 128
PANEL = 16


def dot(a, b):
    return jnp.dot(a, b, preferred_element_type=F32)


def dot_t(a, b, precision=None):
    return lax.dot_general(
        a, b, (((1,), (1,)), ((), ())), precision=precision, preferred_element_type=F32
    )


def picks(ids_ref, pick, pick_x):
    toks = pick_x.shape[1]
    top = pick.shape[1] // toks
    ids = ids_ref[...].astype(F32)
    q = lax.broadcasted_iota(jnp.int32, (toks, toks), 0)
    p = lax.broadcasted_iota(jnp.int32, (toks, toks), 1)
    slot_row = lax.broadcasted_iota(jnp.int32, (ROWS, toks), 0).astype(F32)
    token = lax.broadcasted_iota(jnp.int32, (toks, top * toks), 0) * top
    pair = lax.broadcasted_iota(jnp.int32, (toks, top * toks), 1)
    along = [jnp.broadcast_to(ids[i : i + 1, :], (toks, toks)) for i in range(top)]
    down = [v.T for v in along]
    placed = jnp.zeros(pick.shape, F32)
    by_token = jnp.zeros(pick_x.shape, F32)
    for i in range(top):
        ahead = ((down[i] == along[i]) & (q < p)).astype(F32)
        for j in range(i):
            ahead = ahead + (down[j] == along[i]).astype(F32)
        slot = ids[i : i + 1, :] * CAP + jnp.sum(ahead, axis=0, keepdims=True)
        hot = (slot_row == slot).astype(F32)
        by_token = by_token + hot
        spread = (pair == token + i).astype(F32).astype(BF16)
        placed = placed + dot(hot.astype(BF16), spread)
    pick[...] = placed.astype(BF16)
    pick_x[...] = by_token.astype(BF16)


def bytes_wait(ref, sem):
    pltpu.make_async_copy(ref, ref, sem).wait()


def terms(v):
    high = v.astype(BF16)
    rest = v - high.astype(F32)
    mid = rest.astype(BF16)
    return high, mid, (rest - mid.astype(F32)).astype(BF16)


def inverse_factor(c, cm, mm):
    cm[...] = c
    rows = lax.broadcasted_iota(jnp.int32, (RANK, RANK), 0)
    cols = lax.broadcasted_iota(jnp.int32, (RANK, RANK), 1)
    mm[...] = (rows == cols).astype(F32)
    prow = lax.broadcasted_iota(jnp.int32, (PANEL, RANK), 0)
    pcol = lax.broadcasted_iota(jnp.int32, (PANEL, RANK), 1)

    def panel(p, carry):
        base = pl.multiple_of(p * PANEL, PANEL)
        a = cm[pl.ds(base, PANEL), :]
        m = mm[pl.ds(base, PANEL), :]
        near = pltpu.roll(a, lax.rem(RANK - base, RANK), 1)
        block = [jnp.broadcast_to(near[:, i : i + 1], (PANEL, RANK)) for i in range(PANEL)]
        for i in range(PANEL):
            r = lax.rsqrt(block[i][i : i + 1, :])
            mult = jnp.where(prow > i, block[i] * (r * r), 0.0)
            for j in range(i + 1, PANEL):
                block[j] = block[j] - mult * block[j][i : i + 1, :]
            a = jnp.where(prow == i, a * r, a - mult * a[i : i + 1, :])
            m = jnp.where(prow == i, m * r, m - mult * m[i : i + 1, :])
        mm[pl.ds(base, PANEL), :] = m
        left = jnp.where(pcol >= base + PANEL, a, 0.0)
        both = jnp.concatenate([a, m], axis=1)
        a_high, a_mid, a_low = terms(left)
        b_high, b_mid, b_low = terms(both)
        deep_a = jnp.concatenate([a_high, a_high, a_mid, a_high, a_low, a_mid], axis=0)
        deep_b = jnp.concatenate([b_high, b_mid, b_high, b_low, b_high, b_mid], axis=0)
        change = lax.dot_general(
            deep_a, deep_b, (((0,), (0,)), ((), ())), preferred_element_type=F32
        )
        cm[...] -= change[:, :RANK]
        mm[...] -= change[:, RANK:]
        return carry

    lax.fori_loop(0, RANK // PANEL, panel, 0)
    return mm[...]


def body(
    scale,
    ids_ref, grads, acts, om,
    out,
    pick, pick_x, g_in, gs, xs,
    xr, gl, gr, wl, wr,
    nls, nrs, pxl, pxr, pxl2, pxr2,
    spa, spb, ra1, rb1, mid_a, mid_b, ra2, rb2, bta, btb,
    ws, wgl, wgr,
    pwl, pwr, rl1, rr1, mid_l, mid_r, turn_l, turn_r, rl2, rr2, own_rl, own_rr, rbl, rbr,
    gm, gb, cm, mm,
    ssem, rsem, gsem, selfsem, in_sem, slot_sem, left_sem, right_sem,
    line_send, line_recv, share_recv, piece_recv, half_send, half_recv,
):
    tok = lax.axis_index("tok")
    ex = lax.axis_index("exp")
    y, z = lax.div(tok, N), lax.rem(tok, N)
    x, k = lax.div(ex, 2), lax.rem(ex, 2)
    half = gl.shape[1]
    width = xr.shape[1]
    wc = width // TOK
    hc = half // TOK

    def dev(a, b, c, core):
        return (b * N + c, a * 2 + core)

    def add(a, b, n):
        return lax.rem(a + b, n)

    def remote(src, dst, s, r, where):
        return pltpu.make_async_remote_copy(
            src_ref=src, dst_ref=dst, send_sem=s, recv_sem=r, device_id=where, device_id_type=MESH
        )

    def loop(lo, hi, fn):
        lax.fori_loop(lo, hi, lambda i, c: (fn(i), c)[1], 0)

    pending = []

    def later(ref, sem, when=None):
        if when is None:
            pending.append(lambda: bytes_wait(ref, sem))
        else:
            pending.append(lambda: pl.when(when)(lambda: bytes_wait(ref, sem)))

    chunk = gs.shape[3]
    chunks = half // chunk
    pairs = pick.shape[1]

    def load(side, i):
        cols = pl.ds(pl.multiple_of(side * half + i * chunk, chunk), chunk)
        slot = lax.rem(i, 2)
        return pltpu.make_async_copy(
            grads.at[:, :, cols], g_in.at[side, slot], in_sem.at[side, slot]
        )

    x_block = pwl.shape[2]
    x_blocks = width // x_block

    def load_x(i):
        cols = pl.ds(i * x_block, x_block)
        return pltpu.make_async_copy(acts.at[:, cols], pwl.at[i], in_sem.at[2, i])

    for i in range(2):
        load(0, i).start()
        load(1, i).start()
    for i in range(x_blocks):
        load_x(i).start()

    barrier = pltpu.get_barrier_semaphore()

    def greet(where):
        pl.semaphore_signal(barrier, inc=1, device_id=where, device_id_type=MESH)

    chip = x * TOK + tok

    def same_core(d):
        c = add(chip, d, N * TOK)
        greet((lax.rem(c, TOK), lax.div(c, TOK) * 2 + k))

    loop(1, N * TOK, same_core)

    def other_core(d):
        greet(dev(add(x, d, N), y, z, 1 - k))

    loop(0, N, other_core)

    def other_core_y(d):
        greet(dev(x, add(y, d, N), z, 1 - k))
        greet(dev(x, y, add(z, d, N), 1 - k))

    loop(1, N, other_core_y)
    picks(ids_ref, pick, pick_x)
    part = pl.ds(0, ROWS - CAP)

    def sort_side(i, side, first):
        slot = lax.rem(i, 2)
        load(side, i).wait()
        if not first:
            bytes_wait(gs.at[side, slot, part, :], slot_sem.at[side, slot])
        block = g_in[side, slot].reshape(pairs, chunk)
        gs[side, slot] = dot(pick[...], block).astype(BF16)

        @pl.when(i + 2 < chunks)
        def _():
            load(side, i + 2).start()

    sort_side(0, 0, True)
    sort_side(0, 1, True)
    pl.semaphore_wait(barrier, N * TOK - 1 + N + 2 * (N - 1))

    shift_r = lax.rem(N - z, N)
    swap_l = y == 0
    swap_r = z == 0
    xl = add(x, y, N)
    xd = add(x, shift_r, N)
    own_el, own_er = xl * 2 + k, xd * 2 + k

    def left_y(at_x, to_x):
        return lax.rem(to_x - at_x + N, N)

    def right_z(at_x, to_x):
        return lax.rem(at_x - to_x + N, N)

    quarter = half // N

    def om_rows(i):
        return pl.ds(pl.multiple_of(i * quarter, quarter), quarter)

    def om_right_rows(i):
        return pl.ds(pl.multiple_of(half + i * quarter, quarter), quarter)

    def om_left():
        return remote(
            om.at[om_rows(z), :], wl.at[om_rows(z), :], ssem.at[0], rsem.at[0],
            dev(add(x, N - y, N), y, z, k),
        )

    def om_right():
        return remote(
            om.at[om_right_rows(y), :], wr.at[om_rows(y), :], ssem.at[1], rsem.at[1],
            dev(add(x, z, N), y, z, k),
        )

    @pl.when(swap_l)
    def _():
        pltpu.make_async_copy(om.at[om_rows(z), :], wl.at[om_rows(z), :], rsem.at[0]).start()

    @pl.when(jnp.logical_not(swap_l))
    def _():
        om_left().start()

    @pl.when(swap_r)
    def _():
        pltpu.make_async_copy(om.at[om_right_rows(y), :], wr.at[om_rows(y), :], rsem.at[1]).start()

    @pl.when(jnp.logical_not(swap_r))
    def _():
        om_right().start()

    later(wl.at[om_rows(0), :], ssem.at[0], jnp.logical_not(swap_l))
    later(wr.at[om_rows(0), :], ssem.at[1], jnp.logical_not(swap_r))

    el, er = y * 2 + k, z * 2 + k

    def rows_of(e):
        return pl.ds(pl.multiple_of(e * CAP, CAP), CAP)

    def send_side(i, side):
        slot = lax.rem(i, 2)
        cols = pl.ds(pl.multiple_of(i * chunk, chunk), chunk)
        dst, own, here, sems = (
            (gl, own_el, el, left_sem) if side == 0 else (gr, own_er, er, right_sem)
        )

        def send_g(d):
            e = add(own, d, EXP)
            to, core = lax.div(e, 2), lax.rem(e, 2)
            if side == 0:
                where = dev(x, left_y(x, to), z, core)
            else:
                where = dev(x, y, right_z(x, to), core)
            remote(
                gs.at[side, slot, rows_of(e), :], dst.at[rows_of(here), cols],
                slot_sem.at[side, slot], sems.at[i], where,
            ).start()

        loop(1, EXP, send_g)
        dst[rows_of(here), cols] = gs[side, slot, rows_of(own), :]

    def send_chunk(i, first):
        for side in range(2):
            sort_side(i, side, first)
            send_side(i, side)

    send_side(0, 0)
    send_side(0, 1)

    for i in range(x_blocks):
        load_x(i).wait()
        xs[:, pl.ds(i * x_block, x_block)] = dot(pick_x[...], pwl[i]).astype(BF16)

    def send_x(d):
        e = add(ex, d, EXP)
        remote(
            xs.at[rows_of(e), :], xr.at[rows_of(ex), :], ssem.at[4], rsem.at[4], (tok, e)
        ).start()

    loop(1, EXP, send_x)
    later(xr.at[part, :], ssem.at[4])
    pltpu.make_async_copy(xs.at[rows_of(ex), :], xr.at[rows_of(ex), :], rsem.at[4]).start()

    send_chunk(1, True)
    loop(2, chunks // 2, lambda i: send_chunk(i, False))
    bytes_wait(wl.at[om_rows(z), :], rsem.at[0])
    bytes_wait(wr.at[om_rows(y), :], rsem.at[1])

    def om_share(d):
        remote(
            wl.at[om_rows(z), :], wl.at[om_rows(z), :], ssem.at[18], rsem.at[18],
            dev(x, y, add(z, d, N), k),
        ).start()
        remote(
            wr.at[om_rows(y), :], wr.at[om_rows(y), :], ssem.at[19], rsem.at[19],
            dev(x, add(y, d, N), z, k),
        ).start()

    loop(1, N, om_share)
    most = pl.ds(0, 3 * quarter)
    later(wl.at[most, :], ssem.at[18])
    later(wr.at[most, :], ssem.at[19])
    loop(chunks // 2, chunks, lambda i: send_chunk(i, False))
    for slot in range(2):
        later(gs.at[0, slot, part, :], slot_sem.at[0, slot])
        later(gs.at[1, slot, part, :], slot_sem.at[1, slot])

    def piece(i):
        return pl.ds(pl.multiple_of(i * PIECE, PIECE), PIECE)

    def to_x(left, right, dl, dr, phase):
        nls[phase] = left.astype(BF16)
        nrs[phase] = right.astype(BF16)
        sl, sr = ssem.at[5 + 2 * phase], ssem.at[6 + 2 * phase]
        rl_, rr_ = rsem.at[5 + 2 * phase], rsem.at[6 + 2 * phase]

        def go_l(d):
            b = add(y, d, N)
            remote(nls.at[phase, piece(b), :], dl.at[piece(x), :], sl, rl_, dev(xl, b, z, k)).start()

        def go_r(d):
            c = add(z, d, N)
            remote(nrs.at[phase, piece(c), :], dr.at[piece(x), :], sr, rr_, dev(xd, y, c, k)).start()

        loop(1, N, go_l)
        loop(1, N, go_r)
        own_l = selfsem.at[12 + 2 * phase]
        own_r = selfsem.at[13 + 2 * phase]

        @pl.when(swap_l)
        def _():
            pltpu.make_async_copy(nls.at[phase, piece(y), :], dl.at[piece(x), :], rl_).start()

        @pl.when(jnp.logical_not(swap_l))
        def _():
            remote(
                nls.at[phase, piece(y), :], dl.at[piece(x), :], own_l, rl_, dev(xl, y, z, k)
            ).start()

        @pl.when(swap_r)
        def _():
            pltpu.make_async_copy(nrs.at[phase, piece(z), :], dr.at[piece(x), :], rr_).start()

        @pl.when(jnp.logical_not(swap_r))
        def _():
            remote(
                nrs.at[phase, piece(z), :], dr.at[piece(x), :], own_r, rr_, dev(xd, y, z, k)
            ).start()

        bytes_wait(dl, rl_)
        bytes_wait(dr, rr_)
        total = dl[...].astype(F32) + dr[...].astype(F32)
        three = nls.at[phase, pl.ds(0, 3 * PIECE), :]
        bytes_wait(three, sl)
        bytes_wait(nrs.at[phase, pl.ds(0, 3 * PIECE), :], sr)

        @pl.when(jnp.logical_not(swap_l))
        def _():
            bytes_wait(nls.at[phase, pl.ds(0, PIECE), :], own_l)

        @pl.when(jnp.logical_not(swap_r))
        def _():
            bytes_wait(nrs.at[phase, pl.ds(0, PIECE), :], own_r)

        return total

    rh = RANK // 2
    gram_lane = lax.broadcasted_iota(jnp.int32, (rh // 2, RANK), 1)

    def gram_all(s, phase):
        gram = dot_t(s, s, HIGH)
        fold = pltpu.roll(gram[rh : rh + rh // 2], rh, 1)
        low = jnp.where(gram_lane < rh, fold, gram[rh + rh // 2 :])
        gm[phase] = jnp.concatenate([gram[:rh], low], axis=0).astype(BF16)
        pltpu.make_async_copy(gm.at[phase], gb.at[phase, tok], gsem.at[2 * phase]).start()

        def go(d):
            t = add(tok, d, TOK)
            remote(
                gm.at[phase], gb.at[phase, tok], gsem.at[2 * phase + 1], gsem.at[2 * phase], (t, ex)
            ).start()

        loop(1, TOK, go)
        bytes_wait(gb.at[phase], gsem.at[2 * phase])
        c = lax.fori_loop(
            0, TOK, lambda i, c: c + gb[phase, i].astype(F32), jnp.zeros((RANK - rh // 2, RANK), F32)
        )
        bytes_wait(gb.at[phase, pl.ds(0, TOK - 1)], gsem.at[2 * phase + 1])
        low = c[rh:]
        upper = jnp.where(gram_lane < rh, 0.0, pltpu.roll(low, rh, 1))
        lower = jnp.where(gram_lane < rh, 0.0, low)
        return inverse_factor(jnp.concatenate([c[:rh], upper, lower], axis=0), cm, mm)

    part3 = pl.ds(0, N - 1)

    def sum_along(own, got, me, cols, rows=slice(None)):
        total = own[me, rows, cols].astype(F32)
        for i in range(1, N):
            total = total + got[add(me, i, N), rows, cols].astype(F32)
        return total

    def sum_last(own, got, me):
        def term(i, acc):
            return acc + got[add(me, i, N)].astype(F32)

        return lax.fori_loop(1, N, term, own[me].astype(F32))

    def span(i, n):
        return pl.ds(pl.multiple_of(i * n, 128), n)

    wg, hg = N * wc, N * hc

    def reduce_x(p, phase):
        pt = p.T.astype(BF16)
        s, r = line_send.at[phase], line_recv.at[phase]
        ra, rb = ra1.at[phase], rb1.at[phase]
        ra_last, rb_last = ra2.at[phase], rb2.at[phase]

        def group(d):
            b = add(y, d, N)
            v = dot(pt, xr[:, span(b, wg)]).astype(BF16)
            spa[b] = v[:rh]
            for c in range(N):
                spb[c, :, span(b, wc)] = v[rh:, c * wc : (c + 1) * wc]

            @pl.when(d < N)
            def _():
                remote(spa.at[b], ra.at[y], s.at[0], r.at[0], dev(x, b, z, k)).start()

        loop(1, N + 1, group)

        def send_b(d):
            c = add(z, d, N)
            remote(spb.at[c], rb.at[z], s.at[1], r.at[1], dev(x, y, c, k)).start()

        loop(1, N, send_b)
        bytes_wait(ra.at[part3], r.at[0])

        def second_a(d):
            c = add(z, d, N)
            mid_a[c] = sum_along(spa, ra, y, span(c, wc)).astype(BF16)

            @pl.when(d < N)
            def _():
                remote(mid_a.at[c], ra_last.at[z], s.at[2], r.at[2], dev(x, y, c, k)).start()

        loop(1, N + 1, second_a)
        bytes_wait(rb.at[part3], r.at[1])

        def second_b(d):
            b = add(y, d, N)
            mid_b[b] = sum_along(spb, rb, z, span(b, wc)).astype(BF16)

            @pl.when(d < N)
            def _():
                remote(mid_b.at[b], rb_last.at[y], s.at[3], r.at[3], dev(x, b, z, k)).start()

        loop(1, N + 1, second_b)
        bytes_wait(ra_last.at[part3], r.at[2])
        top = sum_last(mid_a, ra_last, z)
        bytes_wait(rb_last.at[part3], r.at[3])
        low = sum_last(mid_b, rb_last, y)
        bytes_wait(spa.at[part3], s.at[0])
        bytes_wait(spb.at[part3], s.at[1])
        bytes_wait(mid_a.at[part3], s.at[2])
        bytes_wait(mid_b.at[part3], s.at[3])
        return jnp.concatenate([top, low], axis=0)

    bytes_wait(wl.at[most, :], rsem.at[18])
    bytes_wait(wr.at[most, :], rsem.at[19])

    def proj_chunk(i, acc):
        cols = pl.ds(pl.multiple_of(i * chunk, chunk), chunk)
        a, b = acc
        bytes_wait(gl.at[part, cols], left_sem.at[i])
        a = a + dot(gl[:, cols], wl[cols, :])
        bytes_wait(gr.at[part, cols], right_sem.at[i])
        b = b + dot(gr[:, cols], wr[cols, :])
        return a, b

    zero = jnp.zeros((ROWS, RANK), F32)
    left, right = lax.fori_loop(0, chunks, proj_chunk, (zero, zero))
    proj = to_x(left, right, pxl, pxr, 0).astype(BF16).astype(F32)
    bytes_wait(xr, rsem.at[4])

    s = reduce_x(proj, 0)
    inv = gram_all(s, 0)
    basis = jnp.dot(inv, s, precision=HIGH, preferred_element_type=F32).astype(BF16)
    bta[y, :, span(z, wc)] = basis[:rh]
    btb[z, :, span(y, wc)] = basis[rh:]
    own_a, own_b = bta.at[y, :, span(z, wc)], btb.at[z, :, span(y, wc)]
    three = pl.ds(0, (N - 1) * wc)

    def first_b(d):
        c, b = add(z, d, N), add(y, d, N)
        remote(
            own_a, own_a, line_send.at[2, 0], line_recv.at[2, 0], dev(x, y, c, k)
        ).start()
        remote(
            own_b, own_b, line_send.at[2, 1], line_recv.at[2, 1], dev(x, b, z, k)
        ).start()

    loop(1, N, first_b)
    bytes_wait(bta.at[y, :, three], line_recv.at[2, 0])

    def then_a(d):
        remote(
            bta.at[y], bta.at[y], line_send.at[2, 2], line_recv.at[2, 2], dev(x, add(y, d, N), z, k)
        ).start()

    loop(1, N, then_a)
    bytes_wait(btb.at[z, :, three], line_recv.at[2, 1])

    def then_b(d):
        remote(
            btb.at[z], btb.at[z], line_send.at[2, 3], line_recv.at[2, 3], dev(x, y, add(z, d, N), k)
        ).start()

    loop(1, N, then_b)
    later(bta.at[0, :, three], line_send.at[2, 0])
    later(btb.at[0, :, three], line_send.at[2, 1])
    later(bta.at[part3], line_send.at[2, 2])
    later(btb.at[part3], line_send.at[2, 3])
    bytes_wait(bta.at[part3], line_recv.at[2, 2])
    bytes_wait(btb.at[part3], line_recv.at[2, 3])

    def w_step(b, acc):
        low = jnp.concatenate([btb[c, :, span(b, wc)] for c in range(N)], axis=1)
        both = jnp.concatenate([bta[b], low], axis=0)
        return acc + dot_t(xr[:, span(b, wg)], both)

    weights = lax.fori_loop(0, N, w_step, jnp.zeros((ROWS, RANK), F32))
    ws[...] = weights.astype(BF16)

    def go_w(d):
        a = add(x, d, N)
        remote(
            ws.at[piece(a), :], wgl.at[piece(y), :], ssem.at[11], rsem.at[11],
            dev(a, left_y(a, x), z, k),
        ).start()
        remote(
            ws.at[piece(a), :], wgr.at[piece(z), :], ssem.at[12], rsem.at[12],
            dev(a, y, right_z(a, x), k),
        ).start()

    loop(1, N, go_w)
    later(ws.at[pl.ds(0, 3 * PIECE), :], ssem.at[11])
    later(ws.at[pl.ds(0, 3 * PIECE), :], ssem.at[12])
    later(ws.at[piece(0), :], selfsem.at[16], jnp.logical_not(swap_l))
    later(ws.at[piece(0), :], selfsem.at[17], jnp.logical_not(swap_r))

    @pl.when(swap_l)
    def _():
        pltpu.make_async_copy(ws.at[piece(x), :], wgl.at[piece(y), :], rsem.at[11]).start()

    @pl.when(jnp.logical_not(swap_l))
    def _():
        remote(
            ws.at[piece(x), :], wgl.at[piece(y), :], selfsem.at[16], rsem.at[11],
            dev(x, left_y(x, x), z, k),
        ).start()

    @pl.when(swap_r)
    def _():
        pltpu.make_async_copy(ws.at[piece(x), :], wgr.at[piece(z), :], rsem.at[12]).start()

    @pl.when(jnp.logical_not(swap_r))
    def _():
        remote(
            ws.at[piece(x), :], wgr.at[piece(z), :], selfsem.at[17], rsem.at[12],
            dev(x, y, right_z(x, x), k),
        ).start()

    bytes_wait(wgl, rsem.at[11])
    bytes_wait(wgr, rsem.at[12])

    wlt = wgl[...].astype(F32).T.astype(BF16)
    wrt = wgr[...].astype(F32).T.astype(BF16)

    rank_halves = (pl.ds(0, rh), pl.ds(rh, rh))

    def first_left(g, h):
        rows = rank_halves[h]
        remote(
            pwl.at[g, rows], rl1.at[z, rows], half_send.at[0, h], half_recv.at[0, h],
            dev(x, y, g, k),
        ).start()

    def first_right(g, h):
        rows = rank_halves[h]
        remote(
            pwr.at[g, rows], rr1.at[y, rows], half_send.at[1, h], half_recv.at[1, h],
            dev(x, g, z, k),
        ).start()

    def power_group(d):
        g, g2 = add(z, d, N), add(y, d, N)
        pwl[g] = dot(wlt, gl[:, span(g, hg)]).astype(BF16)

        @pl.when(d < N)
        def _():
            first_left(g, 0)

        pwr[g2] = dot(wrt, gr[:, span(g2, hg)]).astype(BF16)

        @pl.when(d < N)
        def _():
            first_right(g2, 0)

    loop(1, N + 1, power_group)

    def other_half(d):
        first_left(add(z, d, N), 1)
        first_right(add(y, d, N), 1)

    loop(1, N, other_half)

    for h in range(2):
        rows = rank_halves[h]
        s_h = [half_send.at[i, h] for i in range(6)]
        r_h = [half_recv.at[i, h] for i in range(6)]
        later(rl1.at[part3, rows], s_h[0])
        later(rr1.at[part3, rows], s_h[1])

        def stage2_left(i):
            b = add(y, i, N)
            mid_l[b, rows] = sum_along(pwl, rl1, z, span(b, hc), rows).astype(BF16)

            @pl.when(i < N)
            def _():
                remote(
                    mid_l.at[b, rows], turn_l.at[y, rows], s_h[2], r_h[2], dev(x, b, z, k)
                ).start()

        def stage2_right(i):
            c = add(z, i, N)
            mid_r[c, rows] = sum_along(pwr, rr1, y, span(c, hc), rows).astype(BF16)

            @pl.when(i < N)
            def _():
                remote(
                    mid_r.at[c, rows], turn_r.at[z, rows], s_h[3], r_h[3], dev(x, y, c, k)
                ).start()

        bytes_wait(rl1.at[part3, rows], r_h[0])
        loop(1, N + 1, stage2_left)
        turn_l[y, rows] = mid_l[y, rows]
        bytes_wait(rr1.at[part3, rows], r_h[1])
        loop(1, N + 1, stage2_right)
        turn_r[z, rows] = mid_r[z, rows]

        def along_x_left(i):
            remote(
                turn_l.at[i, rows], rl2.at[x, rows], s_h[4], r_h[4], dev(add(x, i, N), y, z, k)
            ).start()

        def along_x_right(i):
            remote(
                turn_r.at[i, rows], rr2.at[x, rows], s_h[5], r_h[5], dev(add(x, N - i, N), y, z, k)
            ).start()

        bytes_wait(turn_l.at[part3, rows], r_h[2])
        loop(1, N, along_x_left)
        rl2[x, rows] = turn_l[0, rows]
        bytes_wait(turn_r.at[part3, rows], r_h[3])
        loop(1, N, along_x_right)
        rr2[x, rows] = turn_r[0, rows]
        later(mid_l.at[part3, rows], s_h[2])
        later(mid_r.at[part3, rows], s_h[3])
        later(rl2.at[part3, rows], s_h[4])
        later(rr2.at[part3, rows], s_h[5])

    for h in range(2):
        rows = rank_halves[h]
        bytes_wait(rl2.at[part3, rows], half_recv.at[4, h])
        bytes_wait(rr2.at[part3, rows], half_recv.at[5, h])

    zero = jnp.zeros((RANK, hc), F32)
    sl = lax.fori_loop(0, N, lambda i, c: c + rl2[i].astype(F32), zero)
    sr = lax.fori_loop(0, N, lambda i, c: c + rr2[i].astype(F32), zero)
    s2 = jnp.concatenate([sl, sr], axis=1)
    inv = gram_all(s2, 1)
    right_basis = jnp.dot(inv, s2, precision=HIGH, preferred_element_type=F32).astype(BF16)

    own_rl[...] = right_basis[:, :hc]
    own_rr[...] = right_basis[:, hc:]

    def send_half(h):
        rows = rank_halves[h]
        from_l, from_r = own_rl.at[rows], own_rr.at[rows]
        at_l, at_r = rbl.at[z, rows, span(y, hc)], rbr.at[y, rows, span(z, hc)]
        here_l, here_r = piece_recv.at[0, h, y], piece_recv.at[1, h, z]

        def send_r(d):
            a = add(x, d, N)
            remote(from_l, at_l, ssem.at[15], here_l, dev(a, left_y(a, x), z, k)).start()
            remote(from_r, at_r, ssem.at[16], here_r, dev(a, y, right_z(a, x), k)).start()

        loop(1, N, send_r)

        @pl.when(swap_l)
        def _():
            pltpu.make_async_copy(from_l, at_l, here_l).start()

        @pl.when(jnp.logical_not(swap_l))
        def _():
            remote(from_l, at_l, selfsem.at[10], here_l, dev(x, 0, z, k)).start()

        @pl.when(swap_r)
        def _():
            pltpu.make_async_copy(from_r, at_r, here_r).start()

        @pl.when(jnp.logical_not(swap_r))
        def _():
            remote(from_r, at_r, selfsem.at[11], here_r, dev(x, y, 0, k)).start()

    send_half(0)
    send_half(1)
    later(rl2.at[part3], ssem.at[15])
    later(rr2.at[part3], ssem.at[16])
    later(own_rl, selfsem.at[10], jnp.logical_not(swap_l))
    later(own_rr, selfsem.at[11], jnp.logical_not(swap_r))

    def forward_half(h):
        rows = rank_halves[h]

        def forward(i):
            b, c = add(y, i, N), add(z, i, N)
            left_piece = rbl.at[z, rows, span(b, hc)]
            right_piece = rbr.at[y, rows, span(c, hc)]
            bytes_wait(left_piece, piece_recv.at[0, h, b])

            def share_l(d):
                remote(
                    left_piece, left_piece, ssem.at[22], share_recv.at[0, d],
                    dev(x, y, add(z, d, N), k),
                ).start()

            loop(1, N, share_l)
            bytes_wait(right_piece, piece_recv.at[1, h, c])

            def share_r(d):
                remote(
                    right_piece, right_piece, ssem.at[23], share_recv.at[1, d],
                    dev(x, add(y, d, N), z, k),
                ).start()

            loop(1, N, share_r)

        loop(0, N, forward)

    forward_half(0)
    forward_half(1)
    later(rbl.at[part3], ssem.at[22])
    later(rbr.at[part3], ssem.at[23])

    def left_group(g, acc):
        return acc + dot_t(gl[:, span(g, hg)], rbl[g])

    def right_group(g, acc):
        return acc + dot_t(gr[:, span(g, hg)], rbr[g])

    zero = jnp.zeros((ROWS, RANK), F32)
    left = left_group(z, zero)
    right = right_group(y, zero)

    def next_groups(d, acc):
        a, b = acc
        g = add(z, N - d, N)
        bytes_wait(rbl.at[g], share_recv.at[0, d])
        a = left_group(g, a)
        g = add(y, N - d, N)
        bytes_wait(rbr.at[g], share_recv.at[1, d])
        b = right_group(g, b)
        return a, b

    left, right = lax.fori_loop(1, N, next_groups, (left, right))
    second = to_x(left, right, pxl2, pxr2, 1).astype(BF16).astype(F32)

    s3 = reduce_x(second, 1)
    inv = gram_all(s3, 2)
    last = jnp.dot(inv, s3, precision=HIGH, preferred_element_type=F32)
    out[0] = last.T * scale

    for drain in pending:
        drain()


def owners(ids, grads, acts, om):
    toks, top, hidden = grads.shape
    width = acts.shape[1]
    half = hidden // 2
    wc, hc = width // TOK, half // TOK
    chunk = half // 8
    rh = RANK // 2

    def vm(*shape, dtype=BF16):
        return pltpu.VMEM(shape, dtype)

    any_spec = pl.BlockSpec(memory_space=pl.ANY)
    return pl.pallas_call(
        functools.partial(body, float(width) ** 0.5),
        out_shape=jax.ShapeDtypeStruct((1, wc, RANK), F32),
        in_specs=[pl.BlockSpec(memory_space=pltpu.VMEM)] + [any_spec] * 3,
        out_specs=pl.BlockSpec(memory_space=pltpu.VMEM),
        scratch_shapes=[
            vm(ROWS, toks * top), vm(ROWS, toks), vm(2, 2, toks, top, chunk),
            vm(2, 2, ROWS, chunk), vm(ROWS, width),
            vm(ROWS, width), vm(ROWS, half), vm(ROWS, half), vm(half, RANK), vm(half, RANK),
            vm(2, ROWS, RANK), vm(2, ROWS, RANK),
            vm(ROWS, RANK), vm(ROWS, RANK), vm(ROWS, RANK), vm(ROWS, RANK),
            vm(N, rh, N * wc), vm(N, rh, N * wc), vm(2, N, rh, N * wc), vm(2, N, rh, N * wc),
            vm(N, rh, wc), vm(N, rh, wc), vm(2, N, rh, wc), vm(2, N, rh, wc),
            vm(N, rh, N * wc), vm(N, rh, N * wc),
            vm(ROWS, RANK), vm(ROWS, RANK), vm(ROWS, RANK),
            vm(N, RANK, N * hc), vm(N, RANK, N * hc), vm(N, RANK, N * hc), vm(N, RANK, N * hc),
            vm(N, RANK, hc), vm(N, RANK, hc), vm(N, RANK, hc), vm(N, RANK, hc),
            vm(N, RANK, hc), vm(N, RANK, hc),
            vm(RANK, hc), vm(RANK, hc), vm(N, RANK, N * hc), vm(N, RANK, N * hc),
            vm(3, RANK - rh // 2, RANK), vm(3, TOK, RANK - rh // 2, RANK),
            vm(RANK, RANK, dtype=F32), vm(RANK, RANK, dtype=F32),
            pltpu.SemaphoreType.DMA((24,)),
            pltpu.SemaphoreType.DMA((26,)),
            pltpu.SemaphoreType.DMA((6,)),
            pltpu.SemaphoreType.DMA((18,)),
            pltpu.SemaphoreType.DMA((3, N)),
            pltpu.SemaphoreType.DMA((2, 2)),
            pltpu.SemaphoreType.DMA((8,)),
            pltpu.SemaphoreType.DMA((8,)),
            pltpu.SemaphoreType.DMA((3, 4)),
            pltpu.SemaphoreType.DMA((3, 4)),
            pltpu.SemaphoreType.DMA((2, N)),
            pltpu.SemaphoreType.DMA((2, 2, N)),
            pltpu.SemaphoreType.DMA((6, 2)),
            pltpu.SemaphoreType.DMA((6, 2)),
        ],
        compiler_params=pltpu.CompilerParams(
            collective_id=0, has_side_effects=True, vmem_limit_bytes=60 * 1024 * 1024
        ),
        name="owners",
    )(ids, grads, acts, om)


def shards(activations, expert_ids, out_grads, sketch_matrix):
    om = sketch_matrix.reshape(sketch_matrix.shape[1:])
    return owners(expert_ids.T, out_grads, activations, om)


def solution(mesh):
    return jax.shard_map(
        shards,
        mesh=mesh,
        in_specs=(
            P(("tok", "exp"), None),
            P(("tok", "exp"), None),
            P(("tok", "exp"), None, None),
            P("exp", None, None),
        ),
        out_specs=P("exp", "tok", None),
        check_vma=False,
    )
```

```python
import functools

import jax
import jax.numpy as jnp
from jax import lax
from jax.experimental import pallas as pl
from jax.experimental.pallas import tpu as pltpu
from jax.sharding import PartitionSpec as P

MESH = pl.DeviceIdType.MESH
HIGH = lax.Precision.HIGHEST
F32 = jnp.float32
BF16 = jnp.bfloat16

N = 4
TOK = N * N
EXP = 2 * N
CAP = 48
ROWS = EXP * CAP
PIECE = 2 * CAP
RANK = 128
PANEL = 16


def dot(a, b):
    return jnp.dot(a, b, preferred_element_type=F32)


def dot_t(a, b, precision=None):
    return lax.dot_general(
        a, b, (((1,), (1,)), ((), ())), precision=precision, preferred_element_type=F32
    )


def picks(ids_ref, pick, pick_x):
    toks = pick_x.shape[1]
    top = pick.shape[1] // toks
    ids = ids_ref[...].astype(F32)
    q = lax.broadcasted_iota(jnp.int32, (toks, toks), 0)
    p = lax.broadcasted_iota(jnp.int32, (toks, toks), 1)
    slot_row = lax.broadcasted_iota(jnp.int32, (ROWS, toks), 0).astype(F32)
    token = lax.broadcasted_iota(jnp.int32, (toks, top * toks), 0) * top
    pair = lax.broadcasted_iota(jnp.int32, (toks, top * toks), 1)
    along = [jnp.broadcast_to(ids[i : i + 1, :], (toks, toks)) for i in range(top)]
    down = [v.T for v in along]
    placed = jnp.zeros(pick.shape, F32)
    by_token = jnp.zeros(pick_x.shape, F32)
    for i in range(top):
        ahead = ((down[i] == along[i]) & (q < p)).astype(F32)
        for j in range(i):
            ahead = ahead + (down[j] == along[i]).astype(F32)
        slot = ids[i : i + 1, :] * CAP + jnp.sum(ahead, axis=0, keepdims=True)
        hot = (slot_row == slot).astype(F32)
        by_token = by_token + hot
        spread = (pair == token + i).astype(F32).astype(BF16)
        placed = placed + dot(hot.astype(BF16), spread)
    pick[...] = placed.astype(BF16)
    pick_x[...] = by_token.astype(BF16)


def bytes_wait(ref, sem):
    pltpu.make_async_copy(ref, ref, sem).wait()


def terms(v):
    high = v.astype(BF16)
    rest = v - high.astype(F32)
    mid = rest.astype(BF16)
    return high, mid, (rest - mid.astype(F32)).astype(BF16)


def inverse_factor(c, cm, mm):
    cm[...] = c
    rows = lax.broadcasted_iota(jnp.int32, (RANK, RANK), 0)
    cols = lax.broadcasted_iota(jnp.int32, (RANK, RANK), 1)
    mm[...] = (rows == cols).astype(F32)
    prow = lax.broadcasted_iota(jnp.int32, (PANEL, RANK), 0)
    pcol = lax.broadcasted_iota(jnp.int32, (PANEL, RANK), 1)

    def panel(p, carry):
        base = pl.multiple_of(p * PANEL, PANEL)
        a = cm[pl.ds(base, PANEL), :]
        m = mm[pl.ds(base, PANEL), :]
        near = pltpu.roll(a, lax.rem(RANK - base, RANK), 1)
        block = [jnp.broadcast_to(near[:, i : i + 1], (PANEL, RANK)) for i in range(PANEL)]
        for i in range(PANEL):
            r = lax.rsqrt(block[i][i : i + 1, :])
            mult = jnp.where(prow > i, block[i] * (r * r), 0.0)
            for j in range(i + 1, PANEL):
                block[j] = block[j] - mult * block[j][i : i + 1, :]
            a = jnp.where(prow == i, a * r, a - mult * a[i : i + 1, :])
            m = jnp.where(prow == i, m * r, m - mult * m[i : i + 1, :])
        mm[pl.ds(base, PANEL), :] = m
        left = jnp.where(pcol >= base + PANEL, a, 0.0)
        both = jnp.concatenate([a, m], axis=1)
        a_high, a_mid, a_low = terms(left)
        b_high, b_mid, b_low = terms(both)
        deep_a = jnp.concatenate([a_high, a_high, a_mid, a_high, a_low, a_mid], axis=0)
        deep_b = jnp.concatenate([b_high, b_mid, b_high, b_low, b_high, b_mid], axis=0)
        change = lax.dot_general(
            deep_a, deep_b, (((0,), (0,)), ((), ())), preferred_element_type=F32
        )
        cm[...] -= change[:, :RANK]
        mm[...] -= change[:, RANK:]
        return carry

    lax.fori_loop(0, RANK // PANEL, panel, 0)
    return mm[...]


def body(
    scale,
    ids_ref, grads, acts, om,
    out,
    pick, pick_x, g_in, gs, xs,
    xr, gl, gr, wl, wr,
    nls, nrs, pxl, pxr, pxl2, pxr2,
    spa, spb, ra1, rb1, mid_a, mid_b, ra2, rb2, bta, btb,
    ws, wgl, wgr,
    pwl, pwr, rl1, rr1, turn_l, turn_r, rl2, rr2, own_rl, own_rr, rbl, rbr,
    gm, gb, cm, mm,
    ssem, rsem, gsem, selfsem, in_sem, slot_sem, left_sem, right_sem,
    line_send, line_recv, share_recv, piece_recv, half_send, half_recv, om_recv,
):
    tok = lax.axis_index("tok")
    ex = lax.axis_index("exp")
    y, z = lax.div(tok, N), lax.rem(tok, N)
    x, k = lax.div(ex, 2), lax.rem(ex, 2)
    half = gl.shape[1]
    width = xr.shape[1]
    wc = width // TOK
    hc = half // TOK

    def dev(a, b, c, core):
        return (b * N + c, a * 2 + core)

    def add(a, b, n):
        return lax.rem(a + b, n)

    def remote(src, dst, s, r, where):
        return pltpu.make_async_remote_copy(
            src_ref=src, dst_ref=dst, send_sem=s, recv_sem=r, device_id=where, device_id_type=MESH
        )

    def loop(lo, hi, fn):
        lax.fori_loop(lo, hi, lambda i, c: (fn(i), c)[1], 0)

    pending = []

    def later(ref, sem, when=None):
        if when is None:
            pending.append(lambda: bytes_wait(ref, sem))
        else:
            pending.append(lambda: pl.when(when)(lambda: bytes_wait(ref, sem)))

    chunk = gs.shape[3]
    chunks = half // chunk
    pairs = pick.shape[1]

    def load(side, i):
        cols = pl.ds(pl.multiple_of(side * half + i * chunk, chunk), chunk)
        slot = lax.rem(i, 2)
        return pltpu.make_async_copy(
            grads.at[:, :, cols], g_in.at[side, slot], in_sem.at[side, slot]
        )

    x_block = pwl.shape[2]
    x_blocks = width // x_block

    def load_x(i):
        cols = pl.ds(i * x_block, x_block)
        return pltpu.make_async_copy(acts.at[:, cols], pwl.at[i], in_sem.at[2, i])

    for i in range(2):
        load(0, i).start()
        load(1, i).start()
    for i in range(x_blocks):
        load_x(i).start()

    barrier = pltpu.get_barrier_semaphore()

    def greet(where):
        pl.semaphore_signal(barrier, inc=1, device_id=where, device_id_type=MESH)

    chip = x * TOK + tok

    def same_core(d):
        c = add(chip, d, N * TOK)
        greet((lax.rem(c, TOK), lax.div(c, TOK) * 2 + k))

    loop(1, N * TOK, same_core)

    def other_core(d):
        greet(dev(add(x, d, N), y, z, 1 - k))

    loop(0, N, other_core)

    def other_core_y(d):
        greet(dev(x, add(y, d, N), z, 1 - k))
        greet(dev(x, y, add(z, d, N), 1 - k))

    loop(1, N, other_core_y)
    picks(ids_ref, pick, pick_x)
    part = pl.ds(0, ROWS - CAP)

    def sort_side(i, side, first):
        slot = lax.rem(i, 2)
        load(side, i).wait()
        if not first:
            bytes_wait(gs.at[side, slot, part, :], slot_sem.at[side, slot])
        block = g_in[side, slot].reshape(pairs, chunk)
        gs[side, slot] = dot(pick[...], block).astype(BF16)

        @pl.when(i + 2 < chunks)
        def _():
            load(side, i + 2).start()

    sort_side(0, 0, True)
    sort_side(0, 1, True)
    pl.semaphore_wait(barrier, N * TOK - 1 + N + 2 * (N - 1))

    shift_r = lax.rem(N - z, N)
    swap_l = y == 0
    swap_r = z == 0
    xl = add(x, y, N)
    xd = add(x, shift_r, N)
    own_el, own_er = xl * 2 + k, xd * 2 + k

    def left_y(at_x, to_x):
        return lax.rem(to_x - at_x + N, N)

    def right_z(at_x, to_x):
        return lax.rem(at_x - to_x + N, N)

    quarter = half // N

    def om_rows(i):
        return pl.ds(pl.multiple_of(i * quarter, quarter), quarter)

    def om_right_rows(i):
        return pl.ds(pl.multiple_of(half + i * quarter, quarter), quarter)

    def om_left():
        return remote(
            om.at[om_rows(z), :], wl.at[om_rows(z), :], ssem.at[0], rsem.at[0],
            dev(add(x, N - y, N), y, z, k),
        )

    def om_right():
        return remote(
            om.at[om_right_rows(y), :], wr.at[om_rows(y), :], ssem.at[1], rsem.at[1],
            dev(add(x, z, N), y, z, k),
        )

    @pl.when(swap_l)
    def _():
        pltpu.make_async_copy(om.at[om_rows(z), :], wl.at[om_rows(z), :], rsem.at[0]).start()

    @pl.when(jnp.logical_not(swap_l))
    def _():
        om_left().start()

    @pl.when(swap_r)
    def _():
        pltpu.make_async_copy(om.at[om_right_rows(y), :], wr.at[om_rows(y), :], rsem.at[1]).start()

    @pl.when(jnp.logical_not(swap_r))
    def _():
        om_right().start()

    later(wl.at[om_rows(0), :], ssem.at[0], jnp.logical_not(swap_l))
    later(wr.at[om_rows(0), :], ssem.at[1], jnp.logical_not(swap_r))

    el, er = y * 2 + k, z * 2 + k

    def rows_of(e):
        return pl.ds(pl.multiple_of(e * CAP, CAP), CAP)

    def send_side(i, side):
        slot = lax.rem(i, 2)
        cols = pl.ds(pl.multiple_of(i * chunk, chunk), chunk)
        dst, own, here, sems = (
            (gl, own_el, el, left_sem) if side == 0 else (gr, own_er, er, right_sem)
        )

        def send_g(d):
            e = add(own, d, EXP)
            to, core = lax.div(e, 2), lax.rem(e, 2)
            if side == 0:
                where = dev(x, left_y(x, to), z, core)
            else:
                where = dev(x, y, right_z(x, to), core)
            remote(
                gs.at[side, slot, rows_of(e), :], dst.at[rows_of(here), cols],
                slot_sem.at[side, slot], sems.at[i], where,
            ).start()

        loop(1, EXP, send_g)
        dst[rows_of(here), cols] = gs[side, slot, rows_of(own), :]

    def send_chunk(i, first):
        for side in range(2):
            sort_side(i, side, first)
            send_side(i, side)

    send_side(0, 0)
    send_side(0, 1)

    for i in range(x_blocks):
        load_x(i).wait()
        xs[:, pl.ds(i * x_block, x_block)] = dot(pick_x[...], pwl[i]).astype(BF16)

    def send_x(d):
        e = add(ex, d, EXP)
        remote(
            xs.at[rows_of(e), :], xr.at[rows_of(ex), :], ssem.at[4], rsem.at[4], (tok, e)
        ).start()

    loop(1, EXP, send_x)
    later(xr.at[part, :], ssem.at[4])
    pltpu.make_async_copy(xs.at[rows_of(ex), :], xr.at[rows_of(ex), :], rsem.at[4]).start()

    send_chunk(1, True)
    loop(2, chunks // 2, lambda i: send_chunk(i, False))
    bytes_wait(wl.at[om_rows(z), :], rsem.at[0])
    bytes_wait(wr.at[om_rows(y), :], rsem.at[1])

    def line(side, d):
        return dev(x, y, add(z, d, N), k) if side == 0 else dev(x, add(y, d, N), z, k)

    sides = ((0, wl, z), (1, wr, y))
    for side, buf, me in sides:
        mine = buf.at[om_rows(me), :]
        remote(mine, mine, ssem.at[18 + side], om_recv.at[side, 0], line(side, 1)).start()
        remote(mine, mine, ssem.at[18 + side], om_recv.at[side, 1], line(side, N - 1)).start()
        later(buf.at[pl.ds(0, 2 * quarter), :], ssem.at[18 + side])

    loop(chunks // 2, chunks - 1, lambda i: send_chunk(i, False))
    short = quarter // 2
    for side, buf, me in sides:
        below, above = add(me, N - 1, N), add(me, 1, N)
        bytes_wait(buf.at[om_rows(below), :], om_recv.at[side, 0])
        low = buf.at[pl.ds(pl.multiple_of(below * quarter, quarter), short), :]
        remote(low, low, ssem.at[24 + side], om_recv.at[side, 2], line(side, 1)).start()
        bytes_wait(buf.at[om_rows(above), :], om_recv.at[side, 1])
        high = buf.at[pl.ds(pl.multiple_of(above * quarter + short, short), short), :]
        remote(high, high, ssem.at[24 + side], om_recv.at[side, 2], line(side, N - 1)).start()
        later(buf.at[pl.ds(0, quarter), :], ssem.at[24 + side])

    send_chunk(chunks - 1, False)
    for slot in range(2):
        later(gs.at[0, slot, part, :], slot_sem.at[0, slot])
        later(gs.at[1, slot, part, :], slot_sem.at[1, slot])

    def piece(i):
        return pl.ds(pl.multiple_of(i * PIECE, PIECE), PIECE)

    def to_x(left, right, dl, dr, phase):
        nls[phase] = left.astype(BF16)
        nrs[phase] = right.astype(BF16)
        sl, sr = ssem.at[5 + 2 * phase], ssem.at[6 + 2 * phase]
        rl_, rr_ = rsem.at[5 + 2 * phase], rsem.at[6 + 2 * phase]

        def go_l(d):
            b = add(y, d, N)
            remote(nls.at[phase, piece(b), :], dl.at[piece(x), :], sl, rl_, dev(xl, b, z, k)).start()

        def go_r(d):
            c = add(z, d, N)
            remote(nrs.at[phase, piece(c), :], dr.at[piece(x), :], sr, rr_, dev(xd, y, c, k)).start()

        loop(1, N, go_l)
        loop(1, N, go_r)
        own_l = selfsem.at[12 + 2 * phase]
        own_r = selfsem.at[13 + 2 * phase]

        @pl.when(swap_l)
        def _():
            pltpu.make_async_copy(nls.at[phase, piece(y), :], dl.at[piece(x), :], rl_).start()

        @pl.when(jnp.logical_not(swap_l))
        def _():
            remote(
                nls.at[phase, piece(y), :], dl.at[piece(x), :], own_l, rl_, dev(xl, y, z, k)
            ).start()

        @pl.when(swap_r)
        def _():
            pltpu.make_async_copy(nrs.at[phase, piece(z), :], dr.at[piece(x), :], rr_).start()

        @pl.when(jnp.logical_not(swap_r))
        def _():
            remote(
                nrs.at[phase, piece(z), :], dr.at[piece(x), :], own_r, rr_, dev(xd, y, z, k)
            ).start()

        bytes_wait(dl, rl_)
        bytes_wait(dr, rr_)
        total = dl[...].astype(F32) + dr[...].astype(F32)
        three = nls.at[phase, pl.ds(0, 3 * PIECE), :]
        bytes_wait(three, sl)
        bytes_wait(nrs.at[phase, pl.ds(0, 3 * PIECE), :], sr)

        @pl.when(jnp.logical_not(swap_l))
        def _():
            bytes_wait(nls.at[phase, pl.ds(0, PIECE), :], own_l)

        @pl.when(jnp.logical_not(swap_r))
        def _():
            bytes_wait(nrs.at[phase, pl.ds(0, PIECE), :], own_r)

        return total

    rh = RANK // 2
    gram_lane = lax.broadcasted_iota(jnp.int32, (rh // 2, RANK), 1)

    def gram_all(s, phase):
        gram = dot_t(s, s, HIGH)
        fold = pltpu.roll(gram[rh : rh + rh // 2], rh, 1)
        low = jnp.where(gram_lane < rh, fold, gram[rh + rh // 2 :])
        gm[phase] = jnp.concatenate([gram[:rh], low], axis=0).astype(BF16)
        pltpu.make_async_copy(gm.at[phase], gb.at[phase, tok], gsem.at[2 * phase]).start()

        def go(d):
            t = add(tok, d, TOK)
            remote(
                gm.at[phase], gb.at[phase, tok], gsem.at[2 * phase + 1], gsem.at[2 * phase], (t, ex)
            ).start()

        loop(1, TOK, go)
        bytes_wait(gb.at[phase], gsem.at[2 * phase])
        c = lax.fori_loop(
            0, TOK, lambda i, c: c + gb[phase, i].astype(F32), jnp.zeros((RANK - rh // 2, RANK), F32)
        )
        bytes_wait(gb.at[phase, pl.ds(0, TOK - 1)], gsem.at[2 * phase + 1])
        low = c[rh:]
        upper = jnp.where(gram_lane < rh, 0.0, pltpu.roll(low, rh, 1))
        lower = jnp.where(gram_lane < rh, 0.0, low)
        return inverse_factor(jnp.concatenate([c[:rh], upper, lower], axis=0), cm, mm)

    part3 = pl.ds(0, N - 1)

    def sum_along(own, got, me, cols, rows=slice(None)):
        total = own[me, rows, cols].astype(F32)
        for i in range(1, N):
            total = total + got[add(me, i, N), rows, cols].astype(F32)
        return total

    def sum_last(own, got, me):
        def term(i, acc):
            return acc + got[add(me, i, N)].astype(F32)

        return lax.fori_loop(1, N, term, own[me].astype(F32))

    def span(i, n):
        return pl.ds(pl.multiple_of(i * n, 128), n)

    wg, hg = N * wc, N * hc

    def reduce_x(p, phase):
        pt = p.T.astype(BF16)
        s, r = line_send.at[phase], line_recv.at[phase]
        ra, rb = ra1.at[phase], rb1.at[phase]
        ra_last, rb_last = ra2.at[phase], rb2.at[phase]

        def group(d):
            b = add(y, d, N)
            v = dot(pt, xr[:, span(b, wg)]).astype(BF16)
            spa[b] = v[:rh]
            for c in range(N):
                spb[c, :, span(b, wc)] = v[rh:, c * wc : (c + 1) * wc]

            @pl.when(d < N)
            def _():
                remote(spa.at[b], ra.at[y], s.at[0], r.at[0], dev(x, b, z, k)).start()

        loop(1, N + 1, group)

        def send_b(d):
            c = add(z, d, N)
            remote(spb.at[c], rb.at[z], s.at[1], r.at[1], dev(x, y, c, k)).start()

        loop(1, N, send_b)
        bytes_wait(ra.at[part3], r.at[0])

        def second_a(d):
            c = add(z, d, N)
            mid_a[c] = sum_along(spa, ra, y, span(c, wc)).astype(BF16)

            @pl.when(d < N)
            def _():
                remote(mid_a.at[c], ra_last.at[z], s.at[2], r.at[2], dev(x, y, c, k)).start()

        loop(1, N + 1, second_a)
        bytes_wait(rb.at[part3], r.at[1])

        def second_b(d):
            b = add(y, d, N)
            mid_b[b] = sum_along(spb, rb, z, span(b, wc)).astype(BF16)

            @pl.when(d < N)
            def _():
                remote(mid_b.at[b], rb_last.at[y], s.at[3], r.at[3], dev(x, b, z, k)).start()

        loop(1, N + 1, second_b)
        bytes_wait(ra_last.at[part3], r.at[2])
        top = sum_last(mid_a, ra_last, z)
        bytes_wait(rb_last.at[part3], r.at[3])
        low = sum_last(mid_b, rb_last, y)
        bytes_wait(spa.at[part3], s.at[0])
        bytes_wait(spb.at[part3], s.at[1])
        bytes_wait(mid_a.at[part3], s.at[2])
        bytes_wait(mid_b.at[part3], s.at[3])
        return jnp.concatenate([top, low], axis=0)

    for side, buf, me in sides:
        bytes_wait(buf.at[om_rows(add(me, 2, N)), :], om_recv.at[side, 2])


    def proj_chunk(i, acc):
        cols = pl.ds(pl.multiple_of(i * chunk, chunk), chunk)
        a, b = acc
        bytes_wait(gl.at[part, cols], left_sem.at[i])
        a = a + dot(gl[:, cols], wl[cols, :])
        bytes_wait(gr.at[part, cols], right_sem.at[i])
        b = b + dot(gr[:, cols], wr[cols, :])
        return a, b

    zero = jnp.zeros((ROWS, RANK), F32)
    left, right = lax.fori_loop(0, chunks, proj_chunk, (zero, zero))
    proj = to_x(left, right, pxl, pxr, 0).astype(BF16).astype(F32)
    bytes_wait(xr, rsem.at[4])

    s = reduce_x(proj, 0)
    inv = gram_all(s, 0)
    basis = jnp.dot(inv, s, precision=HIGH, preferred_element_type=F32).astype(BF16)
    bta[y, :, span(z, wc)] = basis[:rh]
    btb[z, :, span(y, wc)] = basis[rh:]
    own_a, own_b = bta.at[y, :, span(z, wc)], btb.at[z, :, span(y, wc)]
    three = pl.ds(0, (N - 1) * wc)

    def first_b(d):
        c, b = add(z, d, N), add(y, d, N)
        remote(
            own_a, own_a, line_send.at[2, 0], line_recv.at[2, 0], dev(x, y, c, k)
        ).start()
        remote(
            own_b, own_b, line_send.at[2, 1], line_recv.at[2, 1], dev(x, b, z, k)
        ).start()

    loop(1, N, first_b)
    bytes_wait(bta.at[y, :, three], line_recv.at[2, 0])

    def then_a(d):
        remote(
            bta.at[y], bta.at[y], line_send.at[2, 2], line_recv.at[2, 2], dev(x, add(y, d, N), z, k)
        ).start()

    loop(1, N, then_a)
    bytes_wait(btb.at[z, :, three], line_recv.at[2, 1])

    def then_b(d):
        remote(
            btb.at[z], btb.at[z], line_send.at[2, 3], line_recv.at[2, 3], dev(x, y, add(z, d, N), k)
        ).start()

    loop(1, N, then_b)
    later(bta.at[0, :, three], line_send.at[2, 0])
    later(btb.at[0, :, three], line_send.at[2, 1])
    later(bta.at[part3], line_send.at[2, 2])
    later(btb.at[part3], line_send.at[2, 3])
    bytes_wait(bta.at[part3], line_recv.at[2, 2])
    bytes_wait(btb.at[part3], line_recv.at[2, 3])

    def w_step(b, acc):
        low = jnp.concatenate([btb[c, :, span(b, wc)] for c in range(N)], axis=1)
        both = jnp.concatenate([bta[b], low], axis=0)
        return acc + dot_t(xr[:, span(b, wg)], both)

    weights = lax.fori_loop(0, N, w_step, jnp.zeros((ROWS, RANK), F32))
    ws[...] = weights.astype(BF16)

    def go_w(d):
        a = add(x, d, N)
        remote(
            ws.at[piece(a), :], wgl.at[piece(y), :], ssem.at[11], rsem.at[11],
            dev(a, left_y(a, x), z, k),
        ).start()
        remote(
            ws.at[piece(a), :], wgr.at[piece(z), :], ssem.at[12], rsem.at[12],
            dev(a, y, right_z(a, x), k),
        ).start()

    loop(1, N, go_w)
    later(ws.at[pl.ds(0, 3 * PIECE), :], ssem.at[11])
    later(ws.at[pl.ds(0, 3 * PIECE), :], ssem.at[12])
    later(ws.at[piece(0), :], selfsem.at[16], jnp.logical_not(swap_l))
    later(ws.at[piece(0), :], selfsem.at[17], jnp.logical_not(swap_r))

    @pl.when(swap_l)
    def _():
        pltpu.make_async_copy(ws.at[piece(x), :], wgl.at[piece(y), :], rsem.at[11]).start()

    @pl.when(jnp.logical_not(swap_l))
    def _():
        remote(
            ws.at[piece(x), :], wgl.at[piece(y), :], selfsem.at[16], rsem.at[11],
            dev(x, left_y(x, x), z, k),
        ).start()

    @pl.when(swap_r)
    def _():
        pltpu.make_async_copy(ws.at[piece(x), :], wgr.at[piece(z), :], rsem.at[12]).start()

    @pl.when(jnp.logical_not(swap_r))
    def _():
        remote(
            ws.at[piece(x), :], wgr.at[piece(z), :], selfsem.at[17], rsem.at[12],
            dev(x, y, right_z(x, x), k),
        ).start()

    bytes_wait(wgl, rsem.at[11])
    bytes_wait(wgr, rsem.at[12])

    wlt = wgl[...].astype(F32).T.astype(BF16)
    wrt = wgr[...].astype(F32).T.astype(BF16)

    rank_halves = (pl.ds(0, rh), pl.ds(rh, rh))

    def first_left(g, h):
        rows = rank_halves[h]
        remote(
            pwl.at[g, rows], rl1.at[z, rows], half_send.at[0, h], half_recv.at[0, h],
            dev(x, y, g, k),
        ).start()

    def first_right(g, h):
        rows = rank_halves[h]
        remote(
            pwr.at[g, rows], rr1.at[y, rows], half_send.at[1, h], half_recv.at[1, h],
            dev(x, g, z, k),
        ).start()

    def power_group(d):
        g, g2 = add(z, d, N), add(y, d, N)
        pwl[g] = dot(wlt, gl[:, span(g, hg)]).astype(BF16)

        @pl.when(d < N)
        def _():
            first_left(g, 0)

        pwr[g2] = dot(wrt, gr[:, span(g2, hg)]).astype(BF16)

        @pl.when(d < N)
        def _():
            first_right(g2, 0)

    loop(1, N + 1, power_group)

    def other_half(d):
        first_left(add(z, d, N), 1)
        first_right(add(y, d, N), 1)

    loop(1, N, other_half)

    for h in range(2):
        rows = rank_halves[h]
        s_h = [half_send.at[i, h] for i in range(6)]
        r_h = [half_recv.at[i, h] for i in range(6)]
        later(rl1.at[part3, rows], s_h[0])
        later(rr1.at[part3, rows], s_h[1])

        def stage2_left(i):
            b = add(y, i, N)
            pwl[z, rows, span(b, hc)] = sum_along(pwl, rl1, z, span(b, hc), rows).astype(BF16)

            @pl.when(i < N)
            def _():
                remote(
                    pwl.at[z, rows, span(b, hc)], turn_l.at[y, rows], s_h[2], r_h[2],
                    dev(x, b, z, k),
                ).start()

        def stage2_right(i):
            c = add(z, i, N)
            pwr[y, rows, span(c, hc)] = sum_along(pwr, rr1, y, span(c, hc), rows).astype(BF16)

            @pl.when(i < N)
            def _():
                remote(
                    pwr.at[y, rows, span(c, hc)], turn_r.at[z, rows], s_h[3], r_h[3],
                    dev(x, y, c, k),
                ).start()

        bytes_wait(rl1.at[part3, rows], r_h[0])
        loop(1, N + 1, stage2_left)
        turn_l[y, rows] = pwl[z, rows, span(y, hc)]
        bytes_wait(rr1.at[part3, rows], r_h[1])
        loop(1, N + 1, stage2_right)
        turn_r[z, rows] = pwr[y, rows, span(z, hc)]

        def along_x_left(i):
            remote(
                turn_l.at[i, rows], rl2.at[x, rows], s_h[4], r_h[4], dev(add(x, i, N), y, z, k)
            ).start()

        def along_x_right(i):
            remote(
                turn_r.at[i, rows], rr2.at[x, rows], s_h[5], r_h[5], dev(add(x, N - i, N), y, z, k)
            ).start()

        bytes_wait(turn_l.at[part3, rows], r_h[2])
        loop(1, N, along_x_left)
        rl2[x, rows] = turn_l[0, rows]
        bytes_wait(turn_r.at[part3, rows], r_h[3])
        loop(1, N, along_x_right)
        rr2[x, rows] = turn_r[0, rows]
        later(turn_l.at[part3, rows], s_h[2])
        later(turn_r.at[part3, rows], s_h[3])
        later(rl2.at[part3, rows], s_h[4])
        later(rr2.at[part3, rows], s_h[5])

    for h in range(2):
        rows = rank_halves[h]
        bytes_wait(rl2.at[part3, rows], half_recv.at[4, h])
        bytes_wait(rr2.at[part3, rows], half_recv.at[5, h])

    zero = jnp.zeros((RANK, hc), F32)
    sl = lax.fori_loop(0, N, lambda i, c: c + rl2[i].astype(F32), zero)
    sr = lax.fori_loop(0, N, lambda i, c: c + rr2[i].astype(F32), zero)
    s2 = jnp.concatenate([sl, sr], axis=1)
    inv = gram_all(s2, 1)
    right_basis = jnp.dot(inv, s2, precision=HIGH, preferred_element_type=F32).astype(BF16)

    own_rl[...] = right_basis[:, :hc]
    own_rr[...] = right_basis[:, hc:]

    def send_half(h):
        rows = rank_halves[h]
        from_l, from_r = own_rl.at[rows], own_rr.at[rows]
        at_l, at_r = rbl.at[z, rows, span(y, hc)], rbr.at[y, rows, span(z, hc)]
        here_l, here_r = piece_recv.at[0, h, y], piece_recv.at[1, h, z]

        def send_r(d):
            a = add(x, d, N)
            remote(from_l, at_l, ssem.at[15], here_l, dev(a, left_y(a, x), z, k)).start()
            remote(from_r, at_r, ssem.at[16], here_r, dev(a, y, right_z(a, x), k)).start()

        loop(1, N, send_r)

        @pl.when(swap_l)
        def _():
            pltpu.make_async_copy(from_l, at_l, here_l).start()

        @pl.when(jnp.logical_not(swap_l))
        def _():
            remote(from_l, at_l, selfsem.at[10], here_l, dev(x, 0, z, k)).start()

        @pl.when(swap_r)
        def _():
            pltpu.make_async_copy(from_r, at_r, here_r).start()

        @pl.when(jnp.logical_not(swap_r))
        def _():
            remote(from_r, at_r, selfsem.at[11], here_r, dev(x, y, 0, k)).start()

    send_half(0)
    send_half(1)
    later(rl2.at[part3], ssem.at[15])
    later(rr2.at[part3], ssem.at[16])
    later(own_rl, selfsem.at[10], jnp.logical_not(swap_l))
    later(own_rr, selfsem.at[11], jnp.logical_not(swap_r))

    def forward_half(h):
        rows = rank_halves[h]

        def forward(i):
            b, c = add(y, i, N), add(z, i, N)
            left_piece = rbl.at[z, rows, span(b, hc)]
            right_piece = rbr.at[y, rows, span(c, hc)]
            bytes_wait(left_piece, piece_recv.at[0, h, b])

            for turn, d in enumerate((1, N - 1)):
                remote(
                    left_piece, left_piece, ssem.at[22], share_recv.at[0, turn, h], line(0, d)
                ).start()

            bytes_wait(right_piece, piece_recv.at[1, h, c])

            for turn, d in enumerate((1, N - 1)):
                remote(
                    right_piece, right_piece, ssem.at[23], share_recv.at[1, turn, h], line(1, d)
                ).start()

        loop(0, N, forward)

    forward_half(0)
    forward_half(1)
    pair2 = pl.ds(0, 2)
    later(rbl.at[pair2], ssem.at[22])
    later(rbr.at[pair2], ssem.at[23])

    groups = ((0, rbl, z), (1, rbr, y))
    for h, turn, back, d in ((0, 0, N - 1, 1), (1, 1, 1, N - 1)):
        for side, buf, me in groups:
            rows_h = buf.at[add(me, back, N), rank_halves[h]]
            bytes_wait(rows_h, share_recv.at[side, turn, h])
            remote(
                rows_h, rows_h, ssem.at[26 + side], share_recv.at[side, 2, h], line(side, d)
            ).start()

    later(rbl.at[0], ssem.at[26])
    later(rbr.at[0], ssem.at[27])

    def left_group(g, acc):
        return acc + dot_t(gl[:, span(g, hg)], rbl[g])

    def right_group(g, acc):
        return acc + dot_t(gr[:, span(g, hg)], rbr[g])

    zero = jnp.zeros((ROWS, RANK), F32)
    left = left_group(z, zero)
    right = right_group(y, zero)

    for turn, back in ((0, N - 1), (1, 1)):
        g, g2 = add(z, back, N), add(y, back, N)
        bytes_wait(rbl.at[g, rank_halves[1 - turn]], share_recv.at[0, turn, 1 - turn])
        left = left_group(g, left)
        bytes_wait(rbr.at[g2, rank_halves[1 - turn]], share_recv.at[1, turn, 1 - turn])
        right = right_group(g2, right)

    g, g2 = add(z, 2, N), add(y, 2, N)
    for h in range(2):
        bytes_wait(rbl.at[g, rank_halves[h]], share_recv.at[0, 2, h])
        bytes_wait(rbr.at[g2, rank_halves[h]], share_recv.at[1, 2, h])
    left = left_group(g, left)
    right = right_group(g2, right)
    second = to_x(left, right, pxl2, pxr2, 1).astype(BF16).astype(F32)

    s3 = reduce_x(second, 1)
    inv = gram_all(s3, 2)
    last = jnp.dot(inv, s3, precision=HIGH, preferred_element_type=F32)
    out[0] = last.T * scale

    for drain in pending:
        drain()


def owners(ids, grads, acts, om):
    toks, top, hidden = grads.shape
    width = acts.shape[1]
    half = hidden // 2
    wc, hc = width // TOK, half // TOK
    chunk = half // 8
    rh = RANK // 2

    def vm(*shape, dtype=BF16):
        return pltpu.VMEM(shape, dtype)

    any_spec = pl.BlockSpec(memory_space=pl.ANY)
    return pl.pallas_call(
        functools.partial(body, float(width) ** 0.5),
        out_shape=jax.ShapeDtypeStruct((1, wc, RANK), F32),
        in_specs=[pl.BlockSpec(memory_space=pltpu.VMEM)] + [any_spec] * 3,
        out_specs=pl.BlockSpec(memory_space=pltpu.VMEM),
        scratch_shapes=[
            vm(ROWS, toks * top), vm(ROWS, toks), vm(2, 2, toks, top, chunk),
            vm(2, 2, ROWS, chunk), vm(ROWS, width),
            vm(ROWS, width), vm(ROWS, half), vm(ROWS, half), vm(half, RANK), vm(half, RANK),
            vm(2, ROWS, RANK), vm(2, ROWS, RANK),
            vm(ROWS, RANK), vm(ROWS, RANK), vm(ROWS, RANK), vm(ROWS, RANK),
            vm(N, rh, N * wc), vm(N, rh, N * wc), vm(2, N, rh, N * wc), vm(2, N, rh, N * wc),
            vm(N, rh, wc), vm(N, rh, wc), vm(2, N, rh, wc), vm(2, N, rh, wc),
            vm(N, rh, N * wc), vm(N, rh, N * wc),
            vm(ROWS, RANK), vm(ROWS, RANK), vm(ROWS, RANK),
            vm(N, RANK, N * hc), vm(N, RANK, N * hc), vm(N, RANK, N * hc), vm(N, RANK, N * hc),
            vm(N, RANK, hc), vm(N, RANK, hc), vm(N, RANK, hc), vm(N, RANK, hc),
            vm(RANK, hc), vm(RANK, hc), vm(N, RANK, N * hc), vm(N, RANK, N * hc),
            vm(3, RANK - rh // 2, RANK), vm(3, TOK, RANK - rh // 2, RANK),
            vm(RANK, RANK, dtype=F32), vm(RANK, RANK, dtype=F32),
            pltpu.SemaphoreType.DMA((28,)),
            pltpu.SemaphoreType.DMA((26,)),
            pltpu.SemaphoreType.DMA((6,)),
            pltpu.SemaphoreType.DMA((18,)),
            pltpu.SemaphoreType.DMA((3, N)),
            pltpu.SemaphoreType.DMA((2, 2)),
            pltpu.SemaphoreType.DMA((8,)),
            pltpu.SemaphoreType.DMA((8,)),
            pltpu.SemaphoreType.DMA((3, 4)),
            pltpu.SemaphoreType.DMA((3, 4)),
            pltpu.SemaphoreType.DMA((2, 3, 2)),
            pltpu.SemaphoreType.DMA((2, 2, N)),
            pltpu.SemaphoreType.DMA((6, 2)),
            pltpu.SemaphoreType.DMA((6, 2)),
            pltpu.SemaphoreType.DMA((2, 3)),
        ],
        compiler_params=pltpu.CompilerParams(
            collective_id=0, has_side_effects=True, vmem_limit_bytes=60 * 1024 * 1024
        ),
        name="owners",
    )(ids, grads, acts, om)


def shards(activations, expert_ids, out_grads, sketch_matrix):
    om = sketch_matrix.reshape(sketch_matrix.shape[1:])
    return owners(expert_ids.T, out_grads, activations, om)


def solution(mesh):
    return jax.shard_map(
        shards,
        mesh=mesh,
        in_specs=(
            P(("tok", "exp"), None),
            P(("tok", "exp"), None),
            P(("tok", "exp"), None, None),
            P("exp", None, None),
        ),
        out_specs=P("exp", "tok", None),
        check_vma=False,
    )
```

```python
import functools

import jax
import jax.numpy as jnp
from jax import lax
from jax.experimental import pallas as pl
from jax.experimental.pallas import tpu as pltpu
from jax.sharding import PartitionSpec as P

MESH = pl.DeviceIdType.MESH
HIGH = lax.Precision.HIGHEST
F32 = jnp.float32
BF16 = jnp.bfloat16

N = 4
TOK = N * N
EXP = 2 * N
CAP = 48
ROWS = EXP * CAP
PIECE = 2 * CAP
RANK = 128
PANEL = 16


def dot(a, b):
    return jnp.dot(a, b, preferred_element_type=F32)


def dot_t(a, b, precision=None):
    return lax.dot_general(
        a, b, (((1,), (1,)), ((), ())), precision=precision, preferred_element_type=F32
    )


def picks(ids_ref, pick, pick_x):
    toks = pick_x.shape[1]
    top = pick.shape[1] // toks
    ids = ids_ref[...].astype(F32)
    q = lax.broadcasted_iota(jnp.int32, (toks, toks), 0)
    p = lax.broadcasted_iota(jnp.int32, (toks, toks), 1)
    slot_row = lax.broadcasted_iota(jnp.int32, (ROWS, toks), 0).astype(F32)
    token = lax.broadcasted_iota(jnp.int32, (toks, top * toks), 0) * top
    pair = lax.broadcasted_iota(jnp.int32, (toks, top * toks), 1)
    along = [jnp.broadcast_to(ids[i : i + 1, :], (toks, toks)) for i in range(top)]
    down = [v.T for v in along]
    placed = jnp.zeros(pick.shape, F32)
    by_token = jnp.zeros(pick_x.shape, F32)
    for i in range(top):
        ahead = ((down[i] == along[i]) & (q < p)).astype(F32)
        for j in range(i):
            ahead = ahead + (down[j] == along[i]).astype(F32)
        slot = ids[i : i + 1, :] * CAP + jnp.sum(ahead, axis=0, keepdims=True)
        hot = (slot_row == slot).astype(F32)
        by_token = by_token + hot
        spread = (pair == token + i).astype(F32).astype(BF16)
        placed = placed + dot(hot.astype(BF16), spread)
    pick[...] = placed.astype(BF16)
    pick_x[...] = by_token.astype(BF16)


def bytes_wait(ref, sem):
    pltpu.make_async_copy(ref, ref, sem).wait()


def terms(v):
    high = v.astype(BF16)
    rest = v - high.astype(F32)
    mid = rest.astype(BF16)
    return high, mid, (rest - mid.astype(F32)).astype(BF16)


def inverse_factor(c, cm, mm):
    cm[...] = c
    rows = lax.broadcasted_iota(jnp.int32, (RANK, RANK), 0)
    cols = lax.broadcasted_iota(jnp.int32, (RANK, RANK), 1)
    mm[...] = (rows == cols).astype(F32)
    prow = lax.broadcasted_iota(jnp.int32, (PANEL, RANK), 0)
    pcol = lax.broadcasted_iota(jnp.int32, (PANEL, RANK), 1)

    def panel(p, carry):
        base = pl.multiple_of(p * PANEL, PANEL)
        a = cm[pl.ds(base, PANEL), :]
        m = mm[pl.ds(base, PANEL), :]
        near = pltpu.roll(a, lax.rem(RANK - base, RANK), 1)
        block = [jnp.broadcast_to(near[:, i : i + 1], (PANEL, RANK)) for i in range(PANEL)]
        for i in range(PANEL):
            r = lax.rsqrt(block[i][i : i + 1, :])
            mult = jnp.where(prow > i, block[i] * (r * r), 0.0)
            for j in range(i + 1, PANEL):
                block[j] = block[j] - mult * block[j][i : i + 1, :]
            a = jnp.where(prow == i, a * r, a - mult * a[i : i + 1, :])
            m = jnp.where(prow == i, m * r, m - mult * m[i : i + 1, :])
        mm[pl.ds(base, PANEL), :] = m
        left = jnp.where(pcol >= base + PANEL, a, 0.0)
        both = jnp.concatenate([a, m], axis=1)
        a_high, a_mid, a_low = terms(left)
        b_high, b_mid, b_low = terms(both)
        deep_a = jnp.concatenate([a_high, a_high, a_mid, a_high, a_low, a_mid], axis=0)
        deep_b = jnp.concatenate([b_high, b_mid, b_high, b_low, b_high, b_mid], axis=0)
        change = lax.dot_general(
            deep_a, deep_b, (((0,), (0,)), ((), ())), preferred_element_type=F32
        )
        cm[...] -= change[:, :RANK]
        mm[...] -= change[:, RANK:]
        return carry

    lax.fori_loop(0, RANK // PANEL, panel, 0)
    return mm[...]


def body(
    scale,
    ids_ref, grads, acts, om,
    out,
    pick, pick_x, g_in, gs, xs,
    xr, gl, gr, wl, wr,
    nls, nrs, pxl, pxr, pxl2, pxr2,
    spa, spb, ra1, rb1, mid_a, mid_b, ra2, rb2, bta, btb,
    ws, wgl, wgr,
    pwl, pwr, rl1, rr1, turn_l, turn_r, rl2, rr2, own_rl, own_rr, rbl, rbr,
    gm, gb, cm, mm,
    ssem, rsem, gsem, selfsem, in_sem, slot_sem, left_sem, right_sem,
    line_send, line_recv, share_recv, piece_recv, half_send, half_recv, om_recv,
):
    tok = lax.axis_index("tok")
    ex = lax.axis_index("exp")
    y, z = lax.div(tok, N), lax.rem(tok, N)
    x, k = lax.div(ex, 2), lax.rem(ex, 2)
    half = gl.shape[1]
    width = xr.shape[1]
    wc = width // TOK
    hc = half // TOK

    def dev(a, b, c, core):
        return (b * N + c, a * 2 + core)

    def add(a, b, n):
        return lax.rem(a + b, n)

    def remote(src, dst, s, r, where):
        return pltpu.make_async_remote_copy(
            src_ref=src, dst_ref=dst, send_sem=s, recv_sem=r, device_id=where, device_id_type=MESH
        )

    def loop(lo, hi, fn):
        lax.fori_loop(lo, hi, lambda i, c: (fn(i), c)[1], 0)

    pending = []

    def later(ref, sem, when=None):
        if when is None:
            pending.append(lambda: bytes_wait(ref, sem))
        else:
            pending.append(lambda: pl.when(when)(lambda: bytes_wait(ref, sem)))

    chunk = gs.shape[3]
    chunks = half // chunk
    pairs = pick.shape[1]

    def load(side, i):
        cols = pl.ds(pl.multiple_of(side * half + i * chunk, chunk), chunk)
        slot = lax.rem(i, 2)
        return pltpu.make_async_copy(
            grads.at[:, :, cols], g_in.at[side, slot], in_sem.at[side, slot]
        )

    x_block = pwl.shape[2]
    x_blocks = width // x_block

    def load_x(i):
        cols = pl.ds(i * x_block, x_block)
        return pltpu.make_async_copy(acts.at[:, cols], pwl.at[i], in_sem.at[2, i])

    for i in range(2):
        load(0, i).start()
        load(1, i).start()
    for i in range(x_blocks):
        load_x(i).start()

    barrier = pltpu.get_barrier_semaphore()

    def greet(where):
        pl.semaphore_signal(barrier, inc=1, device_id=where, device_id_type=MESH)

    def same_experts(d):
        greet((add(tok, d, TOK), ex))

    loop(1, TOK, same_experts)

    def same_core(d):
        greet(dev(add(x, d, N), y, z, k))
        greet(dev(add(x, y, N), add(y, d, N), z, k))
        greet(dev(add(x, N - z, N), y, add(z, d, N), k))
        greet(dev(add(x + N - y, d, N), add(y, N - d, N), z, k))
        greet(dev(add(x + z, d, N), y, add(z, d, N), k))

    loop(1, N, same_core)

    def other_core(d):
        greet(dev(add(x, d, N), y, z, 1 - k))

    loop(0, N, other_core)

    def other_core_y(d):
        greet(dev(x, add(y, d, N), z, 1 - k))
        greet(dev(x, y, add(z, d, N), 1 - k))

    loop(1, N, other_core_y)
    picks(ids_ref, pick, pick_x)
    part = pl.ds(0, ROWS - CAP)

    def sort_side(i, side, first):
        slot = lax.rem(i, 2)
        load(side, i).wait()
        if not first:
            bytes_wait(gs.at[side, slot, part, :], slot_sem.at[side, slot])
        block = g_in[side, slot].reshape(pairs, chunk)
        gs[side, slot] = dot(pick[...], block).astype(BF16)

        @pl.when(i + 2 < chunks)
        def _():
            load(side, i + 2).start()

    sort_side(0, 0, True)
    sort_side(0, 1, True)
    pl.semaphore_wait(barrier, TOK - 1 + 5 * (N - 1) + N + 2 * (N - 1))

    shift_r = lax.rem(N - z, N)
    swap_l = y == 0
    swap_r = z == 0
    xl = add(x, y, N)
    xd = add(x, shift_r, N)
    own_el, own_er = xl * 2 + k, xd * 2 + k

    def left_y(at_x, to_x):
        return lax.rem(to_x - at_x + N, N)

    def right_z(at_x, to_x):
        return lax.rem(at_x - to_x + N, N)

    quarter = half // N

    def om_rows(i):
        return pl.ds(pl.multiple_of(i * quarter, quarter), quarter)

    def om_right_rows(i):
        return pl.ds(pl.multiple_of(half + i * quarter, quarter), quarter)

    def om_left():
        return remote(
            om.at[om_rows(z), :], wl.at[om_rows(z), :], ssem.at[0], rsem.at[0],
            dev(add(x, N - y, N), y, z, k),
        )

    def om_right():
        return remote(
            om.at[om_right_rows(y), :], wr.at[om_rows(y), :], ssem.at[1], rsem.at[1],
            dev(add(x, z, N), y, z, k),
        )

    @pl.when(swap_l)
    def _():
        pltpu.make_async_copy(om.at[om_rows(z), :], wl.at[om_rows(z), :], rsem.at[0]).start()

    @pl.when(jnp.logical_not(swap_l))
    def _():
        om_left().start()

    @pl.when(swap_r)
    def _():
        pltpu.make_async_copy(om.at[om_right_rows(y), :], wr.at[om_rows(y), :], rsem.at[1]).start()

    @pl.when(jnp.logical_not(swap_r))
    def _():
        om_right().start()

    later(wl.at[om_rows(0), :], ssem.at[0], jnp.logical_not(swap_l))
    later(wr.at[om_rows(0), :], ssem.at[1], jnp.logical_not(swap_r))

    el, er = y * 2 + k, z * 2 + k

    def rows_of(e):
        return pl.ds(pl.multiple_of(e * CAP, CAP), CAP)

    def send_side(i, side):
        slot = lax.rem(i, 2)
        cols = pl.ds(pl.multiple_of(i * chunk, chunk), chunk)
        dst, own, here, sems = (
            (gl, own_el, el, left_sem) if side == 0 else (gr, own_er, er, right_sem)
        )

        def send_g(d):
            e = add(own, d, EXP)
            to, core = lax.div(e, 2), lax.rem(e, 2)
            if side == 0:
                where = dev(x, left_y(x, to), z, core)
            else:
                where = dev(x, y, right_z(x, to), core)
            remote(
                gs.at[side, slot, rows_of(e), :], dst.at[rows_of(here), cols],
                slot_sem.at[side, slot], sems.at[i], where,
            ).start()

        loop(1, EXP, send_g)
        dst[rows_of(here), cols] = gs[side, slot, rows_of(own), :]

    def send_chunk(i, first):
        for side in range(2):
            sort_side(i, side, first)
            send_side(i, side)

    send_side(0, 0)
    send_side(0, 1)

    for i in range(x_blocks):
        load_x(i).wait()
        xs[:, pl.ds(i * x_block, x_block)] = dot(pick_x[...], pwl[i]).astype(BF16)

    def send_x(d):
        e = add(ex, d, EXP)
        remote(
            xs.at[rows_of(e), :], xr.at[rows_of(ex), :], ssem.at[4], rsem.at[4], (tok, e)
        ).start()

    loop(1, EXP, send_x)
    later(xr.at[part, :], ssem.at[4])
    pltpu.make_async_copy(xs.at[rows_of(ex), :], xr.at[rows_of(ex), :], rsem.at[4]).start()

    send_chunk(1, True)
    loop(2, chunks // 2, lambda i: send_chunk(i, False))
    bytes_wait(wl.at[om_rows(z), :], rsem.at[0])
    bytes_wait(wr.at[om_rows(y), :], rsem.at[1])

    def line(side, d):
        return dev(x, y, add(z, d, N), k) if side == 0 else dev(x, add(y, d, N), z, k)

    sides = ((0, wl, z), (1, wr, y))
    for side, buf, me in sides:
        mine = buf.at[om_rows(me), :]
        remote(mine, mine, ssem.at[18 + side], om_recv.at[side, 0], line(side, 1)).start()
        remote(mine, mine, ssem.at[18 + side], om_recv.at[side, 1], line(side, N - 1)).start()
        later(buf.at[pl.ds(0, 2 * quarter), :], ssem.at[18 + side])

    loop(chunks // 2, chunks - 1, lambda i: send_chunk(i, False))
    short = quarter // 2
    for side, buf, me in sides:
        below, above = add(me, N - 1, N), add(me, 1, N)
        bytes_wait(buf.at[om_rows(below), :], om_recv.at[side, 0])
        low = buf.at[pl.ds(pl.multiple_of(below * quarter, quarter), short), :]
        remote(low, low, ssem.at[24 + side], om_recv.at[side, 2], line(side, 1)).start()
        bytes_wait(buf.at[om_rows(above), :], om_recv.at[side, 1])
        high = buf.at[pl.ds(pl.multiple_of(above * quarter + short, short), short), :]
        remote(high, high, ssem.at[24 + side], om_recv.at[side, 2], line(side, N - 1)).start()
        later(buf.at[pl.ds(0, quarter), :], ssem.at[24 + side])

    send_chunk(chunks - 1, False)
    for slot in range(2):
        later(gs.at[0, slot, part, :], slot_sem.at[0, slot])
        later(gs.at[1, slot, part, :], slot_sem.at[1, slot])

    def piece(i):
        return pl.ds(pl.multiple_of(i * PIECE, PIECE), PIECE)

    def to_x(left, right, dl, dr, phase):
        nls[phase] = left.astype(BF16)
        nrs[phase] = right.astype(BF16)
        sl, sr = ssem.at[5 + 2 * phase], ssem.at[6 + 2 * phase]
        rl_, rr_ = rsem.at[5 + 2 * phase], rsem.at[6 + 2 * phase]

        def go_l(d):
            b = add(y, d, N)
            remote(nls.at[phase, piece(b), :], dl.at[piece(x), :], sl, rl_, dev(xl, b, z, k)).start()

        def go_r(d):
            c = add(z, d, N)
            remote(nrs.at[phase, piece(c), :], dr.at[piece(x), :], sr, rr_, dev(xd, y, c, k)).start()

        loop(1, N, go_l)
        loop(1, N, go_r)
        own_l = selfsem.at[12 + 2 * phase]
        own_r = selfsem.at[13 + 2 * phase]

        @pl.when(swap_l)
        def _():
            pltpu.make_async_copy(nls.at[phase, piece(y), :], dl.at[piece(x), :], rl_).start()

        @pl.when(jnp.logical_not(swap_l))
        def _():
            remote(
                nls.at[phase, piece(y), :], dl.at[piece(x), :], own_l, rl_, dev(xl, y, z, k)
            ).start()

        @pl.when(swap_r)
        def _():
            pltpu.make_async_copy(nrs.at[phase, piece(z), :], dr.at[piece(x), :], rr_).start()

        @pl.when(jnp.logical_not(swap_r))
        def _():
            remote(
                nrs.at[phase, piece(z), :], dr.at[piece(x), :], own_r, rr_, dev(xd, y, z, k)
            ).start()

        bytes_wait(dl, rl_)
        bytes_wait(dr, rr_)
        total = dl[...].astype(F32) + dr[...].astype(F32)
        three = nls.at[phase, pl.ds(0, 3 * PIECE), :]
        bytes_wait(three, sl)
        bytes_wait(nrs.at[phase, pl.ds(0, 3 * PIECE), :], sr)

        @pl.when(jnp.logical_not(swap_l))
        def _():
            bytes_wait(nls.at[phase, pl.ds(0, PIECE), :], own_l)

        @pl.when(jnp.logical_not(swap_r))
        def _():
            bytes_wait(nrs.at[phase, pl.ds(0, PIECE), :], own_r)

        return total

    rh = RANK // 2
    gram_lane = lax.broadcasted_iota(jnp.int32, (rh // 2, RANK), 1)

    def gram_all(s, phase):
        gram = dot_t(s, s, HIGH)
        fold = pltpu.roll(gram[rh : rh + rh // 2], rh, 1)
        low = jnp.where(gram_lane < rh, fold, gram[rh + rh // 2 :])
        gm[phase] = jnp.concatenate([gram[:rh], low], axis=0).astype(BF16)
        pltpu.make_async_copy(gm.at[phase], gb.at[phase, tok], gsem.at[2 * phase]).start()

        def go(d):
            t = add(tok, d, TOK)
            remote(
                gm.at[phase], gb.at[phase, tok], gsem.at[2 * phase + 1], gsem.at[2 * phase], (t, ex)
            ).start()

        loop(1, TOK, go)
        bytes_wait(gb.at[phase], gsem.at[2 * phase])
        c = lax.fori_loop(
            0, TOK, lambda i, c: c + gb[phase, i].astype(F32), jnp.zeros((RANK - rh // 2, RANK), F32)
        )
        bytes_wait(gb.at[phase, pl.ds(0, TOK - 1)], gsem.at[2 * phase + 1])
        low = c[rh:]
        upper = jnp.where(gram_lane < rh, 0.0, pltpu.roll(low, rh, 1))
        lower = jnp.where(gram_lane < rh, 0.0, low)
        return inverse_factor(jnp.concatenate([c[:rh], upper, lower], axis=0), cm, mm)

    part3 = pl.ds(0, N - 1)

    def sum_along(own, got, me, cols, rows=slice(None)):
        total = own[me, rows, cols].astype(F32)
        for i in range(1, N):
            total = total + got[add(me, i, N), rows, cols].astype(F32)
        return total

    def sum_last(own, got, me):
        def term(i, acc):
            return acc + got[add(me, i, N)].astype(F32)

        return lax.fori_loop(1, N, term, own[me].astype(F32))

    def span(i, n):
        return pl.ds(pl.multiple_of(i * n, 128), n)

    wg, hg = N * wc, N * hc

    def reduce_x(p, phase):
        pt = p.T.astype(BF16)
        s, r = line_send.at[phase], line_recv.at[phase]
        ra, rb = ra1.at[phase], rb1.at[phase]
        ra_last, rb_last = ra2.at[phase], rb2.at[phase]

        def group(d):
            b = add(y, d, N)
            v = dot(pt, xr[:, span(b, wg)]).astype(BF16)
            spa[b] = v[:rh]
            for c in range(N):
                spb[c, :, span(b, wc)] = v[rh:, c * wc : (c + 1) * wc]

            @pl.when(d < N)
            def _():
                remote(spa.at[b], ra.at[y], s.at[0], r.at[0], dev(x, b, z, k)).start()

        loop(1, N + 1, group)

        def send_b(d):
            c = add(z, d, N)
            remote(spb.at[c], rb.at[z], s.at[1], r.at[1], dev(x, y, c, k)).start()

        loop(1, N, send_b)
        bytes_wait(ra.at[part3], r.at[0])

        def second_a(d):
            c = add(z, d, N)
            mid_a[c] = sum_along(spa, ra, y, span(c, wc)).astype(BF16)

            @pl.when(d < N)
            def _():
                remote(mid_a.at[c], ra_last.at[z], s.at[2], r.at[2], dev(x, y, c, k)).start()

        loop(1, N + 1, second_a)
        bytes_wait(rb.at[part3], r.at[1])

        def second_b(d):
            b = add(y, d, N)
            mid_b[b] = sum_along(spb, rb, z, span(b, wc)).astype(BF16)

            @pl.when(d < N)
            def _():
                remote(mid_b.at[b], rb_last.at[y], s.at[3], r.at[3], dev(x, b, z, k)).start()

        loop(1, N + 1, second_b)
        bytes_wait(ra_last.at[part3], r.at[2])
        top = sum_last(mid_a, ra_last, z)
        bytes_wait(rb_last.at[part3], r.at[3])
        low = sum_last(mid_b, rb_last, y)
        bytes_wait(spa.at[part3], s.at[0])
        bytes_wait(spb.at[part3], s.at[1])
        bytes_wait(mid_a.at[part3], s.at[2])
        bytes_wait(mid_b.at[part3], s.at[3])
        return jnp.concatenate([top, low], axis=0)

    for side, buf, me in sides:
        bytes_wait(buf.at[om_rows(add(me, 2, N)), :], om_recv.at[side, 2])


    def proj_chunk(i, acc):
        cols = pl.ds(pl.multiple_of(i * chunk, chunk), chunk)
        a, b = acc
        bytes_wait(gl.at[part, cols], left_sem.at[i])
        a = a + dot(gl[:, cols], wl[cols, :])
        bytes_wait(gr.at[part, cols], right_sem.at[i])
        b = b + dot(gr[:, cols], wr[cols, :])
        return a, b

    zero = jnp.zeros((ROWS, RANK), F32)
    left, right = lax.fori_loop(0, chunks, proj_chunk, (zero, zero))
    proj = to_x(left, right, pxl, pxr, 0).astype(BF16).astype(F32)
    bytes_wait(xr, rsem.at[4])

    s = reduce_x(proj, 0)
    inv = gram_all(s, 0)
    basis = jnp.dot(inv, s, precision=HIGH, preferred_element_type=F32).astype(BF16)
    bta[y, :, span(z, wc)] = basis[:rh]
    btb[z, :, span(y, wc)] = basis[rh:]
    own_a, own_b = bta.at[y, :, span(z, wc)], btb.at[z, :, span(y, wc)]
    three = pl.ds(0, (N - 1) * wc)

    def first_b(d):
        c, b = add(z, d, N), add(y, d, N)
        remote(
            own_a, own_a, line_send.at[2, 0], line_recv.at[2, 0], dev(x, y, c, k)
        ).start()
        remote(
            own_b, own_b, line_send.at[2, 1], line_recv.at[2, 1], dev(x, b, z, k)
        ).start()

    loop(1, N, first_b)
    def then_a(i):
        piece_a = bta.at[y, :, span(add(z, i, N), wc)]

        def go(d):
            remote(
                piece_a, piece_a, line_send.at[2, 2], line_recv.at[2, 2], dev(x, add(y, d, N), z, k)
            ).start()

        loop(1, N, go)

    def then_b(i):
        piece_b = btb.at[z, :, span(add(y, i, N), wc)]

        def go(d):
            remote(
                piece_b, piece_b, line_send.at[2, 3], line_recv.at[2, 3], dev(x, y, add(z, d, N), k)
            ).start()

        loop(1, N, go)

    then_a(0)
    then_b(0)
    bytes_wait(bta.at[y, :, three], line_recv.at[2, 0])
    loop(1, N, then_a)
    bytes_wait(btb.at[z, :, three], line_recv.at[2, 1])
    loop(1, N, then_b)
    later(bta.at[0, :, three], line_send.at[2, 0])
    later(btb.at[0, :, three], line_send.at[2, 1])
    later(bta.at[part3], line_send.at[2, 2])
    later(btb.at[part3], line_send.at[2, 3])
    bytes_wait(bta.at[part3], line_recv.at[2, 2])
    bytes_wait(btb.at[part3], line_recv.at[2, 3])

    def w_step(b, acc):
        low = jnp.concatenate([btb[c, :, span(b, wc)] for c in range(N)], axis=1)
        both = jnp.concatenate([bta[b], low], axis=0)
        return acc + dot_t(xr[:, span(b, wg)], both)

    weights = lax.fori_loop(0, N, w_step, jnp.zeros((ROWS, RANK), F32))
    ws[...] = weights.astype(BF16)

    def go_w(d):
        a = add(x, d, N)
        remote(
            ws.at[piece(a), :], wgl.at[piece(y), :], ssem.at[11], rsem.at[11],
            dev(a, left_y(a, x), z, k),
        ).start()
        remote(
            ws.at[piece(a), :], wgr.at[piece(z), :], ssem.at[12], rsem.at[12],
            dev(a, y, right_z(a, x), k),
        ).start()

    loop(1, N, go_w)
    later(ws.at[pl.ds(0, 3 * PIECE), :], ssem.at[11])
    later(ws.at[pl.ds(0, 3 * PIECE), :], ssem.at[12])
    later(ws.at[piece(0), :], selfsem.at[16], jnp.logical_not(swap_l))
    later(ws.at[piece(0), :], selfsem.at[17], jnp.logical_not(swap_r))

    @pl.when(swap_l)
    def _():
        pltpu.make_async_copy(ws.at[piece(x), :], wgl.at[piece(y), :], rsem.at[11]).start()

    @pl.when(jnp.logical_not(swap_l))
    def _():
        remote(
            ws.at[piece(x), :], wgl.at[piece(y), :], selfsem.at[16], rsem.at[11],
            dev(x, left_y(x, x), z, k),
        ).start()

    @pl.when(swap_r)
    def _():
        pltpu.make_async_copy(ws.at[piece(x), :], wgr.at[piece(z), :], rsem.at[12]).start()

    @pl.when(jnp.logical_not(swap_r))
    def _():
        remote(
            ws.at[piece(x), :], wgr.at[piece(z), :], selfsem.at[17], rsem.at[12],
            dev(x, y, right_z(x, x), k),
        ).start()

    bytes_wait(wgl, rsem.at[11])
    bytes_wait(wgr, rsem.at[12])

    wlt = wgl[...].astype(F32).T.astype(BF16)
    wrt = wgr[...].astype(F32).T.astype(BF16)

    rank_halves = (pl.ds(0, rh), pl.ds(rh, rh))

    def first_left(g, h):
        rows = rank_halves[h]
        remote(
            pwl.at[g, rows], rl1.at[z, rows], half_send.at[0, h], half_recv.at[0, h],
            dev(x, y, g, k),
        ).start()

    def first_right(g, h):
        rows = rank_halves[h]
        remote(
            pwr.at[g, rows], rr1.at[y, rows], half_send.at[1, h], half_recv.at[1, h],
            dev(x, g, z, k),
        ).start()

    def power_group(d):
        g, g2 = add(z, d, N), add(y, d, N)
        pwl[g] = dot(wlt, gl[:, span(g, hg)]).astype(BF16)

        @pl.when(d < N)
        def _():
            first_left(g, 0)

        pwr[g2] = dot(wrt, gr[:, span(g2, hg)]).astype(BF16)

        @pl.when(d < N)
        def _():
            first_right(g2, 0)

    loop(1, N + 1, power_group)

    def other_half(d):
        first_left(add(z, d, N), 1)
        first_right(add(y, d, N), 1)

    loop(1, N, other_half)

    for h in range(2):
        rows = rank_halves[h]
        s_h = [half_send.at[i, h] for i in range(6)]
        r_h = [half_recv.at[i, h] for i in range(6)]
        later(rl1.at[part3, rows], s_h[0])
        later(rr1.at[part3, rows], s_h[1])

        def stage2_left(i):
            b = add(y, i, N)
            pwl[z, rows, span(b, hc)] = sum_along(pwl, rl1, z, span(b, hc), rows).astype(BF16)

            @pl.when(i < N)
            def _():
                remote(
                    pwl.at[z, rows, span(b, hc)], turn_l.at[y, rows], s_h[2], r_h[2],
                    dev(x, b, z, k),
                ).start()

        def stage2_right(i):
            c = add(z, i, N)
            pwr[y, rows, span(c, hc)] = sum_along(pwr, rr1, y, span(c, hc), rows).astype(BF16)

            @pl.when(i < N)
            def _():
                remote(
                    pwr.at[y, rows, span(c, hc)], turn_r.at[z, rows], s_h[3], r_h[3],
                    dev(x, y, c, k),
                ).start()

        bytes_wait(rl1.at[part3, rows], r_h[0])
        loop(1, N + 1, stage2_left)
        turn_l[y, rows] = pwl[z, rows, span(y, hc)]
        bytes_wait(rr1.at[part3, rows], r_h[1])
        loop(1, N + 1, stage2_right)
        turn_r[z, rows] = pwr[y, rows, span(z, hc)]

        def along_x_left(i):
            remote(
                turn_l.at[i, rows], rl2.at[x, rows], s_h[4], r_h[4], dev(add(x, i, N), y, z, k)
            ).start()

        def along_x_right(i):
            remote(
                turn_r.at[i, rows], rr2.at[x, rows], s_h[5], r_h[5], dev(add(x, N - i, N), y, z, k)
            ).start()

        bytes_wait(turn_l.at[part3, rows], r_h[2])
        loop(1, N, along_x_left)
        rl2[x, rows] = turn_l[0, rows]
        bytes_wait(turn_r.at[part3, rows], r_h[3])
        loop(1, N, along_x_right)
        rr2[x, rows] = turn_r[0, rows]
        later(turn_l.at[part3, rows], s_h[2])
        later(turn_r.at[part3, rows], s_h[3])
        later(rl2.at[part3, rows], s_h[4])
        later(rr2.at[part3, rows], s_h[5])

    for h in range(2):
        rows = rank_halves[h]
        bytes_wait(rl2.at[part3, rows], half_recv.at[4, h])
        bytes_wait(rr2.at[part3, rows], half_recv.at[5, h])

    zero = jnp.zeros((RANK, hc), F32)
    sl = lax.fori_loop(0, N, lambda i, c: c + rl2[i].astype(F32), zero)
    sr = lax.fori_loop(0, N, lambda i, c: c + rr2[i].astype(F32), zero)
    s2 = jnp.concatenate([sl, sr], axis=1)
    inv = gram_all(s2, 1)
    right_basis = jnp.dot(inv, s2, precision=HIGH, preferred_element_type=F32).astype(BF16)

    own_rl[...] = right_basis[:, :hc]
    own_rr[...] = right_basis[:, hc:]

    def send_half(h):
        rows = rank_halves[h]
        from_l, from_r = own_rl.at[rows], own_rr.at[rows]
        at_l, at_r = rbl.at[z, rows, span(y, hc)], rbr.at[y, rows, span(z, hc)]
        here_l, here_r = piece_recv.at[0, h, y], piece_recv.at[1, h, z]

        def send_r(d):
            a = add(x, d, N)
            remote(from_l, at_l, ssem.at[15], here_l, dev(a, left_y(a, x), z, k)).start()
            remote(from_r, at_r, ssem.at[16], here_r, dev(a, y, right_z(a, x), k)).start()

        loop(1, N, send_r)

        @pl.when(swap_l)
        def _():
            pltpu.make_async_copy(from_l, at_l, here_l).start()

        @pl.when(jnp.logical_not(swap_l))
        def _():
            remote(from_l, at_l, selfsem.at[10], here_l, dev(x, 0, z, k)).start()

        @pl.when(swap_r)
        def _():
            pltpu.make_async_copy(from_r, at_r, here_r).start()

        @pl.when(jnp.logical_not(swap_r))
        def _():
            remote(from_r, at_r, selfsem.at[11], here_r, dev(x, y, 0, k)).start()

    send_half(0)
    send_half(1)
    later(rl2.at[part3], ssem.at[15])
    later(rr2.at[part3], ssem.at[16])
    later(own_rl, selfsem.at[10], jnp.logical_not(swap_l))
    later(own_rr, selfsem.at[11], jnp.logical_not(swap_r))

    def forward_half(h):
        rows = rank_halves[h]

        def forward(i):
            b, c = add(y, i, N), add(z, i, N)
            left_piece = rbl.at[z, rows, span(b, hc)]
            right_piece = rbr.at[y, rows, span(c, hc)]
            bytes_wait(left_piece, piece_recv.at[0, h, b])

            for turn, d in enumerate((1, N - 1)):
                remote(
                    left_piece, left_piece, ssem.at[22], share_recv.at[0, turn, h], line(0, d)
                ).start()

            bytes_wait(right_piece, piece_recv.at[1, h, c])

            for turn, d in enumerate((1, N - 1)):
                remote(
                    right_piece, right_piece, ssem.at[23], share_recv.at[1, turn, h], line(1, d)
                ).start()

        loop(0, N, forward)

    forward_half(0)
    forward_half(1)
    pair2 = pl.ds(0, 2)
    later(rbl.at[pair2], ssem.at[22])
    later(rbr.at[pair2], ssem.at[23])

    groups = ((0, rbl, z), (1, rbr, y))
    for h, turn, back, d in ((0, 0, N - 1, 1), (1, 1, 1, N - 1)):
        for side, buf, me in groups:
            rows_h = buf.at[add(me, back, N), rank_halves[h]]
            bytes_wait(rows_h, share_recv.at[side, turn, h])
            remote(
                rows_h, rows_h, ssem.at[26 + side], share_recv.at[side, 2, h], line(side, d)
            ).start()

    later(rbl.at[0], ssem.at[26])
    later(rbr.at[0], ssem.at[27])

    def left_group(g, acc):
        return acc + dot_t(gl[:, span(g, hg)], rbl[g])

    def right_group(g, acc):
        return acc + dot_t(gr[:, span(g, hg)], rbr[g])

    zero = jnp.zeros((ROWS, RANK), F32)
    left = left_group(z, zero)
    right = right_group(y, zero)

    for turn, back in ((0, N - 1), (1, 1)):
        g, g2 = add(z, back, N), add(y, back, N)
        bytes_wait(rbl.at[g, rank_halves[1 - turn]], share_recv.at[0, turn, 1 - turn])
        left = left_group(g, left)
        bytes_wait(rbr.at[g2, rank_halves[1 - turn]], share_recv.at[1, turn, 1 - turn])
        right = right_group(g2, right)

    g, g2 = add(z, 2, N), add(y, 2, N)
    for h in range(2):
        bytes_wait(rbl.at[g, rank_halves[h]], share_recv.at[0, 2, h])
        bytes_wait(rbr.at[g2, rank_halves[h]], share_recv.at[1, 2, h])
    left = left_group(g, left)
    right = right_group(g2, right)
    second = to_x(left, right, pxl2, pxr2, 1).astype(BF16).astype(F32)

    s3 = reduce_x(second, 1)
    inv = gram_all(s3, 2)
    last = jnp.dot(inv, s3, precision=HIGH, preferred_element_type=F32)
    out[0] = last.T * scale

    for drain in pending:
        drain()


def owners(ids, grads, acts, om):
    toks, top, hidden = grads.shape
    width = acts.shape[1]
    half = hidden // 2
    wc, hc = width // TOK, half // TOK
    chunk = half // 8
    rh = RANK // 2

    def vm(*shape, dtype=BF16):
        return pltpu.VMEM(shape, dtype)

    any_spec = pl.BlockSpec(memory_space=pl.ANY)
    return pl.pallas_call(
        functools.partial(body, float(width) ** 0.5),
        out_shape=jax.ShapeDtypeStruct((1, wc, RANK), F32),
        in_specs=[pl.BlockSpec(memory_space=pltpu.VMEM)] + [any_spec] * 3,
        out_specs=pl.BlockSpec(memory_space=pltpu.VMEM),
        scratch_shapes=[
            vm(ROWS, toks * top), vm(ROWS, toks), vm(2, 2, toks, top, chunk),
            vm(2, 2, ROWS, chunk), vm(ROWS, width),
            vm(ROWS, width), vm(ROWS, half), vm(ROWS, half), vm(half, RANK), vm(half, RANK),
            vm(2, ROWS, RANK), vm(2, ROWS, RANK),
            vm(ROWS, RANK), vm(ROWS, RANK), vm(ROWS, RANK), vm(ROWS, RANK),
            vm(N, rh, N * wc), vm(N, rh, N * wc), vm(2, N, rh, N * wc), vm(2, N, rh, N * wc),
            vm(N, rh, wc), vm(N, rh, wc), vm(2, N, rh, wc), vm(2, N, rh, wc),
            vm(N, rh, N * wc), vm(N, rh, N * wc),
            vm(ROWS, RANK), vm(ROWS, RANK), vm(ROWS, RANK),
            vm(N, RANK, N * hc), vm(N, RANK, N * hc), vm(N, RANK, N * hc), vm(N, RANK, N * hc),
            vm(N, RANK, hc), vm(N, RANK, hc), vm(N, RANK, hc), vm(N, RANK, hc),
            vm(RANK, hc), vm(RANK, hc), vm(N, RANK, N * hc), vm(N, RANK, N * hc),
            vm(3, RANK - rh // 2, RANK), vm(3, TOK, RANK - rh // 2, RANK),
            vm(RANK, RANK, dtype=F32), vm(RANK, RANK, dtype=F32),
            pltpu.SemaphoreType.DMA((28,)),
            pltpu.SemaphoreType.DMA((26,)),
            pltpu.SemaphoreType.DMA((6,)),
            pltpu.SemaphoreType.DMA((18,)),
            pltpu.SemaphoreType.DMA((3, N)),
            pltpu.SemaphoreType.DMA((2, 2)),
            pltpu.SemaphoreType.DMA((8,)),
            pltpu.SemaphoreType.DMA((8,)),
            pltpu.SemaphoreType.DMA((3, 4)),
            pltpu.SemaphoreType.DMA((3, 4)),
            pltpu.SemaphoreType.DMA((2, 3, 2)),
            pltpu.SemaphoreType.DMA((2, 2, N)),
            pltpu.SemaphoreType.DMA((6, 2)),
            pltpu.SemaphoreType.DMA((6, 2)),
            pltpu.SemaphoreType.DMA((2, 3)),
        ],
        compiler_params=pltpu.CompilerParams(
            collective_id=0, has_side_effects=True, vmem_limit_bytes=60 * 1024 * 1024
        ),
        name="owners",
    )(ids, grads, acts, om)


def shards(activations, expert_ids, out_grads, sketch_matrix):
    om = sketch_matrix.reshape(sketch_matrix.shape[1:])
    return owners(expert_ids.T, out_grads, activations, om)


def solution(mesh):
    return jax.shard_map(
        shards,
        mesh=mesh,
        in_specs=(
            P(("tok", "exp"), None),
            P(("tok", "exp"), None),
            P(("tok", "exp"), None, None),
            P("exp", None, None),
        ),
        out_specs=P("exp", "tok", None),
        check_vma=False,
    )
```

```python
import functools

import jax
import jax.numpy as jnp
from jax import lax
from jax.experimental import pallas as pl
from jax.experimental.pallas import tpu as pltpu
from jax.sharding import PartitionSpec as P

MESH = pl.DeviceIdType.MESH
HIGH = lax.Precision.HIGHEST
F32 = jnp.float32
BF16 = jnp.bfloat16

N = 4
TOK = N * N
EXP = 2 * N
CAP = 48
ROWS = EXP * CAP
PIECE = 2 * CAP
RANK = 128
PANEL = 16


def dot(a, b):
    return jnp.dot(a, b, preferred_element_type=F32)


def dot_t(a, b, precision=None):
    return lax.dot_general(
        a, b, (((1,), (1,)), ((), ())), precision=precision, preferred_element_type=F32
    )


def picks(ids_ref, pick, pick_x):
    toks = pick_x.shape[1]
    top = pick.shape[1] // toks
    ids = ids_ref[...].astype(F32)
    q = lax.broadcasted_iota(jnp.int32, (toks, toks), 0)
    p = lax.broadcasted_iota(jnp.int32, (toks, toks), 1)
    slot_row = lax.broadcasted_iota(jnp.int32, (ROWS, toks), 0).astype(F32)
    token = lax.broadcasted_iota(jnp.int32, (toks, top * toks), 0) * top
    pair = lax.broadcasted_iota(jnp.int32, (toks, top * toks), 1)
    along = [jnp.broadcast_to(ids[i : i + 1, :], (toks, toks)) for i in range(top)]
    down = [v.T for v in along]
    placed = jnp.zeros(pick.shape, F32)
    by_token = jnp.zeros(pick_x.shape, F32)
    for i in range(top):
        ahead = ((down[i] == along[i]) & (q < p)).astype(F32)
        for j in range(i):
            ahead = ahead + (down[j] == along[i]).astype(F32)
        slot = ids[i : i + 1, :] * CAP + jnp.sum(ahead, axis=0, keepdims=True)
        hot = (slot_row == slot).astype(F32)
        by_token = by_token + hot
        spread = (pair == token + i).astype(F32).astype(BF16)
        placed = placed + dot(hot.astype(BF16), spread)
    pick[...] = placed.astype(BF16)
    pick_x[...] = by_token.astype(BF16)


def bytes_wait(ref, sem):
    pltpu.make_async_copy(ref, ref, sem).wait()


def terms(v):
    high = v.astype(BF16)
    rest = v - high.astype(F32)
    mid = rest.astype(BF16)
    return high, mid, (rest - mid.astype(F32)).astype(BF16)


def inverse_factor(c, cm, mm):
    cm[...] = c
    rows = lax.broadcasted_iota(jnp.int32, (RANK, RANK), 0)
    cols = lax.broadcasted_iota(jnp.int32, (RANK, RANK), 1)
    mm[...] = (rows == cols).astype(F32)
    prow = lax.broadcasted_iota(jnp.int32, (PANEL, RANK), 0)
    pcol = lax.broadcasted_iota(jnp.int32, (PANEL, RANK), 1)

    def panel(p, carry):
        base = pl.multiple_of(p * PANEL, PANEL)
        a = cm[pl.ds(base, PANEL), :]
        m = mm[pl.ds(base, PANEL), :]
        near = pltpu.roll(a, lax.rem(RANK - base, RANK), 1)
        block = [jnp.broadcast_to(near[:, i : i + 1], (PANEL, RANK)) for i in range(PANEL)]
        for i in range(PANEL):
            r = lax.rsqrt(block[i][i : i + 1, :])
            mult = jnp.where(prow > i, block[i] * (r * r), 0.0)
            for j in range(i + 1, PANEL):
                block[j] = block[j] - mult * block[j][i : i + 1, :]
            a = jnp.where(prow == i, a * r, a - mult * a[i : i + 1, :])
            m = jnp.where(prow == i, m * r, m - mult * m[i : i + 1, :])
        mm[pl.ds(base, PANEL), :] = m
        left = jnp.where(pcol >= base + PANEL, a, 0.0)
        both = jnp.concatenate([a, m], axis=1)
        a_high, a_mid, a_low = terms(left)
        b_high, b_mid, b_low = terms(both)
        deep_a = jnp.concatenate([a_high, a_high, a_mid, a_high, a_low, a_mid], axis=0)
        deep_b = jnp.concatenate([b_high, b_mid, b_high, b_low, b_high, b_mid], axis=0)
        change = lax.dot_general(
            deep_a, deep_b, (((0,), (0,)), ((), ())), preferred_element_type=F32
        )
        cm[...] -= change[:, :RANK]
        mm[...] -= change[:, RANK:]
        return carry

    lax.fori_loop(0, RANK // PANEL, panel, 0)
    return mm[...]


def body(
    scale,
    ids_ref, grads, acts, om,
    out,
    pick, pick_x, g_in, gs, xs,
    xr, gl, gr, wl, wr,
    nls, nrs, pxl, pxr, pxl2, pxr2,
    spa, spb, ra1, rb1, mid_a, mid_b, ra2, rb2, bta, btb,
    ws, wgl, wgr,
    pwl, pwr, rl1, rr1, turn_l, turn_r, rl2, rr2, own_rl, own_rr, rbl, rbr,
    gm, gb, cm, mm,
    ssem, rsem, gsem, selfsem, in_sem, slot_sem, left_sem, right_sem,
    line_send, line_recv, share_recv, piece_recv, half_send, half_recv, om_recv,
):
    tok = lax.axis_index("tok")
    ex = lax.axis_index("exp")
    y, z = lax.div(tok, N), lax.rem(tok, N)
    x, k = lax.div(ex, 2), lax.rem(ex, 2)
    half = gl.shape[1]
    width = xr.shape[1]
    wc = width // TOK
    hc = half // TOK

    def dev(a, b, c, core):
        return (b * N + c, a * 2 + core)

    def add(a, b, n):
        return lax.rem(a + b, n)

    def remote(src, dst, s, r, where):
        return pltpu.make_async_remote_copy(
            src_ref=src, dst_ref=dst, send_sem=s, recv_sem=r, device_id=where, device_id_type=MESH
        )

    def loop(lo, hi, fn):
        lax.fori_loop(lo, hi, lambda i, c: (fn(i), c)[1], 0)

    pending = []

    def later(ref, sem, when=None):
        if when is None:
            pending.append(lambda: bytes_wait(ref, sem))
        else:
            pending.append(lambda: pl.when(when)(lambda: bytes_wait(ref, sem)))

    chunk = gs.shape[3]
    chunks = half // chunk
    pairs = pick.shape[1]

    def load(side, i):
        cols = pl.ds(pl.multiple_of(side * half + i * chunk, chunk), chunk)
        slot = lax.rem(i, 2)
        return pltpu.make_async_copy(
            grads.at[:, :, cols], g_in.at[side, slot], in_sem.at[side, slot]
        )

    x_block = pwl.shape[2]
    x_blocks = width // x_block

    def load_x(i):
        cols = pl.ds(i * x_block, x_block)
        return pltpu.make_async_copy(acts.at[:, cols], pwl.at[i], in_sem.at[2, i])

    for i in range(2):
        load(0, i).start()
        load(1, i).start()
    for i in range(x_blocks):
        load_x(i).start()

    barrier = pltpu.get_barrier_semaphore()

    def greet(where):
        pl.semaphore_signal(barrier, inc=1, device_id=where, device_id_type=MESH)

    def same_experts(d):
        greet((add(tok, d, TOK), ex))

    loop(1, TOK, same_experts)

    def same_core(d):
        greet(dev(add(x, d, N), y, z, k))
        greet(dev(add(x, y, N), add(y, d, N), z, k))
        greet(dev(add(x, N - z, N), y, add(z, d, N), k))
        greet(dev(add(x + N - y, d, N), add(y, N - d, N), z, k))
        greet(dev(add(x + z, d, N), y, add(z, d, N), k))

    loop(1, N, same_core)

    def other_core(d):
        greet(dev(add(x, d, N), y, z, 1 - k))

    loop(0, N, other_core)

    def other_core_y(d):
        greet(dev(x, add(y, d, N), z, 1 - k))
        greet(dev(x, y, add(z, d, N), 1 - k))

    loop(1, N, other_core_y)
    picks(ids_ref, pick, pick_x)
    part = pl.ds(0, ROWS - CAP)

    def sort_side(i, side, first):
        slot = lax.rem(i, 2)
        load(side, i).wait()
        if not first:
            bytes_wait(gs.at[side, slot, part, :], slot_sem.at[side, slot])
        block = g_in[side, slot].reshape(pairs, chunk)
        gs[side, slot] = dot(pick[...], block).astype(BF16)

        @pl.when(i + 2 < chunks)
        def _():
            load(side, i + 2).start()

    sort_side(0, 0, True)
    sort_side(0, 1, True)
    pl.semaphore_wait(barrier, TOK - 1 + 5 * (N - 1) + N + 2 * (N - 1))

    shift_r = lax.rem(N - z, N)
    swap_l = y == 0
    swap_r = z == 0
    xl = add(x, y, N)
    xd = add(x, shift_r, N)
    own_el, own_er = xl * 2 + k, xd * 2 + k

    def left_y(at_x, to_x):
        return lax.rem(to_x - at_x + N, N)

    def right_z(at_x, to_x):
        return lax.rem(at_x - to_x + N, N)

    quarter = half // N

    def om_rows(i):
        return pl.ds(pl.multiple_of(i * quarter, quarter), quarter)

    def om_right_rows(i):
        return pl.ds(pl.multiple_of(half + i * quarter, quarter), quarter)

    def om_left():
        return remote(
            om.at[om_rows(z), :], wl.at[om_rows(z), :], ssem.at[0], rsem.at[0],
            dev(add(x, N - y, N), y, z, k),
        )

    def om_right():
        return remote(
            om.at[om_right_rows(y), :], wr.at[om_rows(y), :], ssem.at[1], rsem.at[1],
            dev(add(x, z, N), y, z, k),
        )

    @pl.when(swap_l)
    def _():
        pltpu.make_async_copy(om.at[om_rows(z), :], wl.at[om_rows(z), :], rsem.at[0]).start()

    @pl.when(jnp.logical_not(swap_l))
    def _():
        om_left().start()

    @pl.when(swap_r)
    def _():
        pltpu.make_async_copy(om.at[om_right_rows(y), :], wr.at[om_rows(y), :], rsem.at[1]).start()

    @pl.when(jnp.logical_not(swap_r))
    def _():
        om_right().start()

    later(wl.at[om_rows(0), :], ssem.at[0], jnp.logical_not(swap_l))
    later(wr.at[om_rows(0), :], ssem.at[1], jnp.logical_not(swap_r))

    el, er = y * 2 + k, z * 2 + k

    def rows_of(e):
        return pl.ds(pl.multiple_of(e * CAP, CAP), CAP)

    def send_side(i, side):
        slot = lax.rem(i, 2)
        cols = pl.ds(pl.multiple_of(i * chunk, chunk), chunk)
        dst, own, here, sems = (
            (gl, own_el, el, left_sem) if side == 0 else (gr, own_er, er, right_sem)
        )

        def send_g(d):
            e = add(own, d, EXP)
            to, core = lax.div(e, 2), lax.rem(e, 2)
            if side == 0:
                where = dev(x, left_y(x, to), z, core)
            else:
                where = dev(x, y, right_z(x, to), core)
            remote(
                gs.at[side, slot, rows_of(e), :], dst.at[rows_of(here), cols],
                slot_sem.at[side, slot], sems.at[i], where,
            ).start()

        loop(1, EXP, send_g)
        dst[rows_of(here), cols] = gs[side, slot, rows_of(own), :]

    def send_chunk(i, first):
        for side in range(2):
            sort_side(i, side, first)
            send_side(i, side)

    send_side(0, 0)
    send_side(0, 1)

    for i in range(x_blocks):
        load_x(i).wait()
        xs[:, pl.ds(i * x_block, x_block)] = dot(pick_x[...], pwl[i]).astype(BF16)

    def send_x(d):
        e = add(ex, d, EXP)
        remote(
            xs.at[rows_of(e), :], xr.at[rows_of(ex), :], ssem.at[4], rsem.at[4], (tok, e)
        ).start()

    loop(1, EXP, send_x)
    later(xr.at[part, :], ssem.at[4])
    pltpu.make_async_copy(xs.at[rows_of(ex), :], xr.at[rows_of(ex), :], rsem.at[4]).start()

    send_chunk(1, True)
    loop(2, 3, lambda i: send_chunk(i, False))
    bytes_wait(wl.at[om_rows(z), :], rsem.at[0])
    bytes_wait(wr.at[om_rows(y), :], rsem.at[1])

    def line(side, d):
        return dev(x, y, add(z, d, N), k) if side == 0 else dev(x, add(y, d, N), z, k)

    sides = ((0, wl, z), (1, wr, y))
    for side, buf, me in sides:
        mine = buf.at[om_rows(me), :]
        remote(mine, mine, ssem.at[18 + side], om_recv.at[side, 0], line(side, 1)).start()
        remote(mine, mine, ssem.at[18 + side], om_recv.at[side, 1], line(side, N - 1)).start()
        later(buf.at[pl.ds(0, 2 * quarter), :], ssem.at[18 + side])

    loop(3, chunks - 1, lambda i: send_chunk(i, False))
    short = quarter // 2
    for side, buf, me in sides:
        below, above = add(me, N - 1, N), add(me, 1, N)
        bytes_wait(buf.at[om_rows(below), :], om_recv.at[side, 0])
        low = buf.at[pl.ds(pl.multiple_of(below * quarter, quarter), short), :]
        remote(low, low, ssem.at[24 + side], om_recv.at[side, 2], line(side, 1)).start()
        bytes_wait(buf.at[om_rows(above), :], om_recv.at[side, 1])
        high = buf.at[pl.ds(pl.multiple_of(above * quarter + short, short), short), :]
        remote(high, high, ssem.at[24 + side], om_recv.at[side, 2], line(side, N - 1)).start()
        later(buf.at[pl.ds(0, quarter), :], ssem.at[24 + side])

    send_chunk(chunks - 1, False)
    for slot in range(2):
        later(gs.at[0, slot, part, :], slot_sem.at[0, slot])
        later(gs.at[1, slot, part, :], slot_sem.at[1, slot])

    def piece(i):
        return pl.ds(pl.multiple_of(i * PIECE, PIECE), PIECE)

    def to_x(left, right, dl, dr, phase):
        nls[phase] = left.astype(BF16)
        nrs[phase] = right.astype(BF16)
        sl, sr = ssem.at[5 + 2 * phase], ssem.at[6 + 2 * phase]
        rl_, rr_ = rsem.at[5 + 2 * phase], rsem.at[6 + 2 * phase]

        def go_l(d):
            b = add(y, d, N)
            remote(nls.at[phase, piece(b), :], dl.at[piece(x), :], sl, rl_, dev(xl, b, z, k)).start()

        def go_r(d):
            c = add(z, d, N)
            remote(nrs.at[phase, piece(c), :], dr.at[piece(x), :], sr, rr_, dev(xd, y, c, k)).start()

        loop(1, N, go_l)
        loop(1, N, go_r)
        own_l = selfsem.at[12 + 2 * phase]
        own_r = selfsem.at[13 + 2 * phase]

        @pl.when(swap_l)
        def _():
            pltpu.make_async_copy(nls.at[phase, piece(y), :], dl.at[piece(x), :], rl_).start()

        @pl.when(jnp.logical_not(swap_l))
        def _():
            remote(
                nls.at[phase, piece(y), :], dl.at[piece(x), :], own_l, rl_, dev(xl, y, z, k)
            ).start()

        @pl.when(swap_r)
        def _():
            pltpu.make_async_copy(nrs.at[phase, piece(z), :], dr.at[piece(x), :], rr_).start()

        @pl.when(jnp.logical_not(swap_r))
        def _():
            remote(
                nrs.at[phase, piece(z), :], dr.at[piece(x), :], own_r, rr_, dev(xd, y, z, k)
            ).start()

        bytes_wait(dl, rl_)
        bytes_wait(dr, rr_)
        total = dl[...].astype(F32) + dr[...].astype(F32)
        three = nls.at[phase, pl.ds(0, 3 * PIECE), :]
        bytes_wait(three, sl)
        bytes_wait(nrs.at[phase, pl.ds(0, 3 * PIECE), :], sr)

        @pl.when(jnp.logical_not(swap_l))
        def _():
            bytes_wait(nls.at[phase, pl.ds(0, PIECE), :], own_l)

        @pl.when(jnp.logical_not(swap_r))
        def _():
            bytes_wait(nrs.at[phase, pl.ds(0, PIECE), :], own_r)

        return total

    rh = RANK // 2
    gram_lane = lax.broadcasted_iota(jnp.int32, (rh // 2, RANK), 1)

    def gram_all(s, phase):
        gram = dot_t(s, s, HIGH)
        fold = pltpu.roll(gram[rh : rh + rh // 2], rh, 1)
        low = jnp.where(gram_lane < rh, fold, gram[rh + rh // 2 :])
        gm[phase] = jnp.concatenate([gram[:rh], low], axis=0).astype(BF16)
        pltpu.make_async_copy(gm.at[phase], gb.at[phase, tok], gsem.at[2 * phase]).start()

        def go(d):
            t = add(tok, d, TOK)
            remote(
                gm.at[phase], gb.at[phase, tok], gsem.at[2 * phase + 1], gsem.at[2 * phase], (t, ex)
            ).start()

        loop(1, TOK, go)
        bytes_wait(gb.at[phase], gsem.at[2 * phase])
        c = lax.fori_loop(
            0, TOK, lambda i, c: c + gb[phase, i].astype(F32), jnp.zeros((RANK - rh // 2, RANK), F32)
        )
        bytes_wait(gb.at[phase, pl.ds(0, TOK - 1)], gsem.at[2 * phase + 1])
        low = c[rh:]
        upper = jnp.where(gram_lane < rh, 0.0, pltpu.roll(low, rh, 1))
        lower = jnp.where(gram_lane < rh, 0.0, low)
        return inverse_factor(jnp.concatenate([c[:rh], upper, lower], axis=0), cm, mm)

    part3 = pl.ds(0, N - 1)

    def sum_along(own, got, me, cols, rows=slice(None)):
        total = own[me, rows, cols].astype(F32)
        for i in range(1, N):
            total = total + got[add(me, i, N), rows, cols].astype(F32)
        return total

    def sum_last(own, got, me):
        def term(i, acc):
            return acc + got[add(me, i, N)].astype(F32)

        return lax.fori_loop(1, N, term, own[me].astype(F32))

    def span(i, n):
        return pl.ds(pl.multiple_of(i * n, 128), n)

    wg, hg = N * wc, N * hc

    def reduce_x(p, phase):
        pt = p.T.astype(BF16)
        s, r = line_send.at[phase], line_recv.at[phase]
        ra, rb = ra1.at[phase], rb1.at[phase]
        ra_last, rb_last = ra2.at[phase], rb2.at[phase]

        def group(d):
            b = add(y, d, N)
            v = dot(pt, xr[:, span(b, wg)]).astype(BF16)
            spa[b] = v[:rh]
            for c in range(N):
                spb[c, :, span(b, wc)] = v[rh:, c * wc : (c + 1) * wc]

            @pl.when(d < N)
            def _():
                remote(spa.at[b], ra.at[y], s.at[0], r.at[0], dev(x, b, z, k)).start()

        loop(1, N + 1, group)

        def send_b(d):
            c = add(z, d, N)
            remote(spb.at[c], rb.at[z], s.at[1], r.at[1], dev(x, y, c, k)).start()

        loop(1, N, send_b)
        bytes_wait(ra.at[part3], r.at[0])

        def second_a(d):
            c = add(z, d, N)
            mid_a[c] = sum_along(spa, ra, y, span(c, wc)).astype(BF16)

            @pl.when(d < N)
            def _():
                remote(mid_a.at[c], ra_last.at[z], s.at[2], r.at[2], dev(x, y, c, k)).start()

        loop(1, N + 1, second_a)
        bytes_wait(rb.at[part3], r.at[1])

        def second_b(d):
            b = add(y, d, N)
            mid_b[b] = sum_along(spb, rb, z, span(b, wc)).astype(BF16)

            @pl.when(d < N)
            def _():
                remote(mid_b.at[b], rb_last.at[y], s.at[3], r.at[3], dev(x, b, z, k)).start()

        loop(1, N + 1, second_b)
        bytes_wait(ra_last.at[part3], r.at[2])
        top = sum_last(mid_a, ra_last, z)
        bytes_wait(rb_last.at[part3], r.at[3])
        low = sum_last(mid_b, rb_last, y)
        bytes_wait(spa.at[part3], s.at[0])
        bytes_wait(spb.at[part3], s.at[1])
        bytes_wait(mid_a.at[part3], s.at[2])
        bytes_wait(mid_b.at[part3], s.at[3])
        return jnp.concatenate([top, low], axis=0)

    for side, buf, me in sides:
        bytes_wait(buf.at[om_rows(add(me, 2, N)), :], om_recv.at[side, 2])


    def proj_chunk(i, acc):
        cols = pl.ds(pl.multiple_of(i * chunk, chunk), chunk)
        a, b = acc
        bytes_wait(gl.at[part, cols], left_sem.at[i])
        a = a + dot(gl[:, cols], wl[cols, :])
        bytes_wait(gr.at[part, cols], right_sem.at[i])
        b = b + dot(gr[:, cols], wr[cols, :])
        return a, b

    zero = jnp.zeros((ROWS, RANK), F32)
    left, right = lax.fori_loop(0, chunks, proj_chunk, (zero, zero))
    proj = to_x(left, right, pxl, pxr, 0).astype(BF16).astype(F32)
    bytes_wait(xr, rsem.at[4])

    s = reduce_x(proj, 0)
    inv = gram_all(s, 0)
    basis = jnp.dot(inv, s, precision=HIGH, preferred_element_type=F32).astype(BF16)
    bta[y, :, span(z, wc)] = basis[:rh]
    btb[z, :, span(y, wc)] = basis[rh:]
    own_a, own_b = bta.at[y, :, span(z, wc)], btb.at[z, :, span(y, wc)]
    three = pl.ds(0, (N - 1) * wc)

    def first_b(d):
        c, b = add(z, d, N), add(y, d, N)
        remote(
            own_a, own_a, line_send.at[2, 0], line_recv.at[2, 0], dev(x, y, c, k)
        ).start()
        remote(
            own_b, own_b, line_send.at[2, 1], line_recv.at[2, 1], dev(x, b, z, k)
        ).start()

    loop(1, N, first_b)
    def then_a(i):
        piece_a = bta.at[y, :, span(add(z, i, N), wc)]

        def go(d):
            remote(
                piece_a, piece_a, line_send.at[2, 2], line_recv.at[2, 2], dev(x, add(y, d, N), z, k)
            ).start()

        loop(1, N, go)

    def then_b(i):
        piece_b = btb.at[z, :, span(add(y, i, N), wc)]

        def go(d):
            remote(
                piece_b, piece_b, line_send.at[2, 3], line_recv.at[2, 3], dev(x, y, add(z, d, N), k)
            ).start()

        loop(1, N, go)

    then_a(0)
    then_b(0)
    bytes_wait(bta.at[y, :, three], line_recv.at[2, 0])
    loop(1, N, then_a)
    bytes_wait(btb.at[z, :, three], line_recv.at[2, 1])
    loop(1, N, then_b)
    later(bta.at[0, :, three], line_send.at[2, 0])
    later(btb.at[0, :, three], line_send.at[2, 1])
    later(bta.at[part3], line_send.at[2, 2])
    later(btb.at[part3], line_send.at[2, 3])
    bytes_wait(bta.at[part3], line_recv.at[2, 2])
    bytes_wait(btb.at[part3], line_recv.at[2, 3])

    def w_step(b, acc):
        low = jnp.concatenate([btb[c, :, span(b, wc)] for c in range(N)], axis=1)
        both = jnp.concatenate([bta[b], low], axis=0)
        return acc + dot_t(xr[:, span(b, wg)], both)

    weights = lax.fori_loop(0, N, w_step, jnp.zeros((ROWS, RANK), F32))
    ws[...] = weights.astype(BF16)

    def go_w(d):
        a = add(x, d, N)
        remote(
            ws.at[piece(a), :], wgl.at[piece(y), :], ssem.at[11], rsem.at[11],
            dev(a, left_y(a, x), z, k),
        ).start()
        remote(
            ws.at[piece(a), :], wgr.at[piece(z), :], ssem.at[12], rsem.at[12],
            dev(a, y, right_z(a, x), k),
        ).start()

    loop(1, N, go_w)
    later(ws.at[pl.ds(0, 3 * PIECE), :], ssem.at[11])
    later(ws.at[pl.ds(0, 3 * PIECE), :], ssem.at[12])
    later(ws.at[piece(0), :], selfsem.at[16], jnp.logical_not(swap_l))
    later(ws.at[piece(0), :], selfsem.at[17], jnp.logical_not(swap_r))

    @pl.when(swap_l)
    def _():
        pltpu.make_async_copy(ws.at[piece(x), :], wgl.at[piece(y), :], rsem.at[11]).start()

    @pl.when(jnp.logical_not(swap_l))
    def _():
        remote(
            ws.at[piece(x), :], wgl.at[piece(y), :], selfsem.at[16], rsem.at[11],
            dev(x, left_y(x, x), z, k),
        ).start()

    @pl.when(swap_r)
    def _():
        pltpu.make_async_copy(ws.at[piece(x), :], wgr.at[piece(z), :], rsem.at[12]).start()

    @pl.when(jnp.logical_not(swap_r))
    def _():
        remote(
            ws.at[piece(x), :], wgr.at[piece(z), :], selfsem.at[17], rsem.at[12],
            dev(x, y, right_z(x, x), k),
        ).start()

    bytes_wait(wgl, rsem.at[11])
    bytes_wait(wgr, rsem.at[12])

    wlt = wgl[...].astype(F32).T.astype(BF16)
    wrt = wgr[...].astype(F32).T.astype(BF16)

    rank_halves = (pl.ds(0, rh), pl.ds(rh, rh))

    def first_left(g, h):
        rows = rank_halves[h]
        remote(
            pwl.at[g, rows], rl1.at[z, rows], half_send.at[0, h], half_recv.at[0, h],
            dev(x, y, g, k),
        ).start()

    def first_right(g, h):
        rows = rank_halves[h]
        remote(
            pwr.at[g, rows], rr1.at[y, rows], half_send.at[1, h], half_recv.at[1, h],
            dev(x, g, z, k),
        ).start()

    def power_group(d):
        g, g2 = add(z, d, N), add(y, d, N)
        pwl[g] = dot(wlt, gl[:, span(g, hg)]).astype(BF16)

        @pl.when(d < N)
        def _():
            first_left(g, 0)

        pwr[g2] = dot(wrt, gr[:, span(g2, hg)]).astype(BF16)

        @pl.when(d < N)
        def _():
            first_right(g2, 0)

    loop(1, N + 1, power_group)

    def other_half(d):
        first_left(add(z, d, N), 1)
        first_right(add(y, d, N), 1)

    loop(1, N, other_half)

    for h in range(2):
        rows = rank_halves[h]
        s_h = [half_send.at[i, h] for i in range(6)]
        r_h = [half_recv.at[i, h] for i in range(6)]
        later(rl1.at[part3, rows], s_h[0])
        later(rr1.at[part3, rows], s_h[1])

        def stage2_left(i):
            b = add(y, i, N)
            pwl[z, rows, span(b, hc)] = sum_along(pwl, rl1, z, span(b, hc), rows).astype(BF16)

            @pl.when(i < N)
            def _():
                remote(
                    pwl.at[z, rows, span(b, hc)], turn_l.at[y, rows], s_h[2], r_h[2],
                    dev(x, b, z, k),
                ).start()

        def stage2_right(i):
            c = add(z, i, N)
            pwr[y, rows, span(c, hc)] = sum_along(pwr, rr1, y, span(c, hc), rows).astype(BF16)

            @pl.when(i < N)
            def _():
                remote(
                    pwr.at[y, rows, span(c, hc)], turn_r.at[z, rows], s_h[3], r_h[3],
                    dev(x, y, c, k),
                ).start()

        bytes_wait(rl1.at[part3, rows], r_h[0])
        loop(1, N + 1, stage2_left)
        turn_l[y, rows] = pwl[z, rows, span(y, hc)]
        bytes_wait(rr1.at[part3, rows], r_h[1])
        loop(1, N + 1, stage2_right)
        turn_r[z, rows] = pwr[y, rows, span(z, hc)]

        def along_x_left(i):
            remote(
                turn_l.at[i, rows], rl2.at[x, rows], s_h[4], r_h[4], dev(add(x, i, N), y, z, k)
            ).start()

        def along_x_right(i):
            remote(
                turn_r.at[i, rows], rr2.at[x, rows], s_h[5], r_h[5], dev(add(x, N - i, N), y, z, k)
            ).start()

        bytes_wait(turn_l.at[part3, rows], r_h[2])
        loop(1, N, along_x_left)
        rl2[x, rows] = turn_l[0, rows]
        bytes_wait(turn_r.at[part3, rows], r_h[3])
        loop(1, N, along_x_right)
        rr2[x, rows] = turn_r[0, rows]
        later(turn_l.at[part3, rows], s_h[2])
        later(turn_r.at[part3, rows], s_h[3])
        later(rl2.at[part3, rows], s_h[4])
        later(rr2.at[part3, rows], s_h[5])

    for h in range(2):
        rows = rank_halves[h]
        bytes_wait(rl2.at[part3, rows], half_recv.at[4, h])
        bytes_wait(rr2.at[part3, rows], half_recv.at[5, h])

    zero = jnp.zeros((RANK, hc), F32)
    sl = lax.fori_loop(0, N, lambda i, c: c + rl2[i].astype(F32), zero)
    sr = lax.fori_loop(0, N, lambda i, c: c + rr2[i].astype(F32), zero)
    s2 = jnp.concatenate([sl, sr], axis=1)
    inv = gram_all(s2, 1)
    right_basis = jnp.dot(inv, s2, precision=HIGH, preferred_element_type=F32).astype(BF16)

    own_rl[...] = right_basis[:, :hc]
    own_rr[...] = right_basis[:, hc:]

    def send_half(h):
        rows = rank_halves[h]
        from_l, from_r = own_rl.at[rows], own_rr.at[rows]
        at_l, at_r = rbl.at[z, rows, span(y, hc)], rbr.at[y, rows, span(z, hc)]
        here_l, here_r = piece_recv.at[0, h, y], piece_recv.at[1, h, z]

        def send_r(d):
            a = add(x, d, N)
            remote(from_l, at_l, ssem.at[15], here_l, dev(a, left_y(a, x), z, k)).start()
            remote(from_r, at_r, ssem.at[16], here_r, dev(a, y, right_z(a, x), k)).start()

        loop(1, N, send_r)

        @pl.when(swap_l)
        def _():
            pltpu.make_async_copy(from_l, at_l, here_l).start()

        @pl.when(jnp.logical_not(swap_l))
        def _():
            remote(from_l, at_l, selfsem.at[10], here_l, dev(x, 0, z, k)).start()

        @pl.when(swap_r)
        def _():
            pltpu.make_async_copy(from_r, at_r, here_r).start()

        @pl.when(jnp.logical_not(swap_r))
        def _():
            remote(from_r, at_r, selfsem.at[11], here_r, dev(x, y, 0, k)).start()

    send_half(0)
    send_half(1)
    later(rl2.at[part3], ssem.at[15])
    later(rr2.at[part3], ssem.at[16])
    later(own_rl, selfsem.at[10], jnp.logical_not(swap_l))
    later(own_rr, selfsem.at[11], jnp.logical_not(swap_r))

    def forward_half(h):
        rows = rank_halves[h]

        def forward(i):
            b, c = add(y, i, N), add(z, i, N)
            left_piece = rbl.at[z, rows, span(b, hc)]
            right_piece = rbr.at[y, rows, span(c, hc)]
            bytes_wait(left_piece, piece_recv.at[0, h, b])

            for turn, d in enumerate((1, N - 1)):
                remote(
                    left_piece, left_piece, ssem.at[22], share_recv.at[0, turn, h], line(0, d)
                ).start()

            bytes_wait(right_piece, piece_recv.at[1, h, c])

            for turn, d in enumerate((1, N - 1)):
                remote(
                    right_piece, right_piece, ssem.at[23], share_recv.at[1, turn, h], line(1, d)
                ).start()

        loop(0, N, forward)

    forward_half(0)
    forward_half(1)
    pair2 = pl.ds(0, 2)
    later(rbl.at[pair2], ssem.at[22])
    later(rbr.at[pair2], ssem.at[23])

    groups = ((0, rbl, z), (1, rbr, y))
    for h, turn, back, d in ((0, 0, N - 1, 1), (1, 1, 1, N - 1)):
        for side, buf, me in groups:
            rows_h = buf.at[add(me, back, N), rank_halves[h]]
            bytes_wait(rows_h, share_recv.at[side, turn, h])
            remote(
                rows_h, rows_h, ssem.at[26 + side], share_recv.at[side, 2, h], line(side, d)
            ).start()

    later(rbl.at[0], ssem.at[26])
    later(rbr.at[0], ssem.at[27])

    def left_group(g, acc):
        return acc + dot_t(gl[:, span(g, hg)], rbl[g])

    def right_group(g, acc):
        return acc + dot_t(gr[:, span(g, hg)], rbr[g])

    zero = jnp.zeros((ROWS, RANK), F32)
    left = left_group(z, zero)
    right = right_group(y, zero)

    for turn, back in ((0, N - 1), (1, 1)):
        g, g2 = add(z, back, N), add(y, back, N)
        bytes_wait(rbl.at[g, rank_halves[1 - turn]], share_recv.at[0, turn, 1 - turn])
        left = left_group(g, left)
        bytes_wait(rbr.at[g2, rank_halves[1 - turn]], share_recv.at[1, turn, 1 - turn])
        right = right_group(g2, right)

    g, g2 = add(z, 2, N), add(y, 2, N)
    for h in range(2):
        bytes_wait(rbl.at[g, rank_halves[h]], share_recv.at[0, 2, h])
        bytes_wait(rbr.at[g2, rank_halves[h]], share_recv.at[1, 2, h])
    left = left_group(g, left)
    right = right_group(g2, right)
    second = to_x(left, right, pxl2, pxr2, 1).astype(BF16).astype(F32)

    s3 = reduce_x(second, 1)
    inv = gram_all(s3, 2)
    last = jnp.dot(inv, s3, precision=HIGH, preferred_element_type=F32)
    out[0] = last.T * scale

    for drain in pending:
        drain()


def owners(ids, grads, acts, om):
    toks, top, hidden = grads.shape
    width = acts.shape[1]
    half = hidden // 2
    wc, hc = width // TOK, half // TOK
    chunk = half // 8
    rh = RANK // 2

    def vm(*shape, dtype=BF16):
        return pltpu.VMEM(shape, dtype)

    any_spec = pl.BlockSpec(memory_space=pl.ANY)
    return pl.pallas_call(
        functools.partial(body, float(width) ** 0.5),
        out_shape=jax.ShapeDtypeStruct((1, wc, RANK), F32),
        in_specs=[pl.BlockSpec(memory_space=pltpu.VMEM)] + [any_spec] * 3,
        out_specs=pl.BlockSpec(memory_space=pltpu.VMEM),
        scratch_shapes=[
            vm(ROWS, toks * top), vm(ROWS, toks), vm(2, 2, toks, top, chunk),
            vm(2, 2, ROWS, chunk), vm(ROWS, width),
            vm(ROWS, width), vm(ROWS, half), vm(ROWS, half), vm(half, RANK), vm(half, RANK),
            vm(2, ROWS, RANK), vm(2, ROWS, RANK),
            vm(ROWS, RANK), vm(ROWS, RANK), vm(ROWS, RANK), vm(ROWS, RANK),
            vm(N, rh, N * wc), vm(N, rh, N * wc), vm(2, N, rh, N * wc), vm(2, N, rh, N * wc),
            vm(N, rh, wc), vm(N, rh, wc), vm(2, N, rh, wc), vm(2, N, rh, wc),
            vm(N, rh, N * wc), vm(N, rh, N * wc),
            vm(ROWS, RANK), vm(ROWS, RANK), vm(ROWS, RANK),
            vm(N, RANK, N * hc), vm(N, RANK, N * hc), vm(N, RANK, N * hc), vm(N, RANK, N * hc),
            vm(N, RANK, hc), vm(N, RANK, hc), vm(N, RANK, hc), vm(N, RANK, hc),
            vm(RANK, hc), vm(RANK, hc), vm(N, RANK, N * hc), vm(N, RANK, N * hc),
            vm(3, RANK - rh // 2, RANK), vm(3, TOK, RANK - rh // 2, RANK),
            vm(RANK, RANK, dtype=F32), vm(RANK, RANK, dtype=F32),
            pltpu.SemaphoreType.DMA((28,)),
            pltpu.SemaphoreType.DMA((26,)),
            pltpu.SemaphoreType.DMA((6,)),
            pltpu.SemaphoreType.DMA((18,)),
            pltpu.SemaphoreType.DMA((3, N)),
            pltpu.SemaphoreType.DMA((2, 2)),
            pltpu.SemaphoreType.DMA((8,)),
            pltpu.SemaphoreType.DMA((8,)),
            pltpu.SemaphoreType.DMA((3, 4)),
            pltpu.SemaphoreType.DMA((3, 4)),
            pltpu.SemaphoreType.DMA((2, 3, 2)),
            pltpu.SemaphoreType.DMA((2, 2, N)),
            pltpu.SemaphoreType.DMA((6, 2)),
            pltpu.SemaphoreType.DMA((6, 2)),
            pltpu.SemaphoreType.DMA((2, 3)),
        ],
        compiler_params=pltpu.CompilerParams(
            collective_id=0, has_side_effects=True, vmem_limit_bytes=60 * 1024 * 1024
        ),
        name="owners",
    )(ids, grads, acts, om)


def shards(activations, expert_ids, out_grads, sketch_matrix):
    om = sketch_matrix.reshape(sketch_matrix.shape[1:])
    return owners(expert_ids.T, out_grads, activations, om)


def solution(mesh):
    return jax.shard_map(
        shards,
        mesh=mesh,
        in_specs=(
            P(("tok", "exp"), None),
            P(("tok", "exp"), None),
            P(("tok", "exp"), None, None),
            P("exp", None, None),
        ),
        out_specs=P("exp", "tok", None),
        check_vma=False,
    )
```
